32 devices in a mesh: blk: 8 (over z, y), head: 4 (over x, core).
Axes of the slice: x: 2, y: 2, z: 4, core: 2. Of those that a mesh axis runs over, the one named last changes fastest.
Arguments:
- tokens: bfloat16 [8192, 768], P('blk'), may hold values from -6 to 6
- seg_ids: int32 [8192], replicated, may hold values from 0 to 6, as said below
- gain_attn: float32 [768], replicated, may hold values from 0.25 to 1.75
- w_query: bfloat16 [768, 768], P('blk', 'head'), may hold values from -0.21875 to 0.21875
- w_key: bfloat16 [768, 768], P('blk', 'head'), may hold values from -0.21875 to 0.21875
- w_value: bfloat16 [768, 768], P('blk', 'head'), may hold values from -0.21875 to 0.21875
- conv_kernels: float32 [3, 3, 768], P(None, None, 'head'), may hold values from -4 to 4
- w_out: bfloat16 [768, 768], P('head', 'blk'), may hold values from -0.875 to 0.875
- gain_ffn: float32 [768], replicated, may hold values from 0.25 to 1.75
- w_up: bfloat16 [768, 3072], P('blk', 'head'), may hold values from -0.21875 to 0.21875
- w_down: bfloat16 [3072, 768], P('head', 'blk'), may hold values from -0.109375 to 0.109375
- cotangent: bfloat16 [8192, 768], P('blk'), may hold values from -6 to 6
Outputs:
- output: bfloat16 [8192, 768], P('blk')
- grad_tokens: float32 [8192, 768], P('blk')
- grad_gain_attn: float32 [768], replicated
- grad_w_query: float32 [768, 768], P('blk', 'head')
- grad_w_key: float32 [768, 768], P('blk', 'head')
- grad_w_value: float32 [768, 768], P('blk', 'head')
- grad_conv_kernels: float32 [3, 3, 768], P(None, None, 'head')
- grad_w_out: float32 [768, 768], P('head', 'blk')
- grad_gain_ffn: float32 [768], replicated
- grad_w_up: float32 [768, 3072], P('blk', 'head')
- grad_w_down: float32 [3072, 768], P('head', 'blk')
The draws below stay inside these ranges and needn't reach their ends.
Inputs may be any that keep to these rules, and one draw needn't show every extreme that they name: `seg_ids`: document numbers of the packed stream: 0 at the first token, rising by one at each new document and never falling. The first document has 1 to 1023 tokens, the last is cut short, every other has 1024 or 2048 tokens, and at least one document of 2048 tokens lies whole in the stream.
All inputs are finite; a program needn't handle non-finite values.
Results may differ from the reference program's by a relative error of at most 0.019.
The reference program's roundings to bfloat16 on the way count: a program that leaves them out, or rounds other values in their place, can miss the bound.
Values may be sent and summed in bfloat16 or wider, within the bound.
No kernel may reach another device: no remote copies, remote signals or barrier semaphores. Data moves between devices by JAX's collectives and lax.ppermute only.
A program may use at most 192 MiB of HBM per device.

```python
import jax
import jax.numpy as jnp
from jax import lax

D = 768
H = 12
DH = 64
FF = 3072
TOK_DEV = 1024
SHORT = 1024
LONG = 2048
REACH = 2
TOKENS = 8192


def draw_seg_ids(key, part):
    key = jax.random.fold_in(key, 7)
    lead_key, kind_key = jax.random.split(key)
    units = TOKENS // SHORT
    long_count = units // 3
    whole_count = units - 1 - long_count
    lead_rows = jax.random.randint(lead_key, (), 1, TOK_DEV)
    order = jax.random.permutation(kind_key, whole_count)
    doc_kinds = (order < long_count).astype(jnp.int32)
    lengths = SHORT + doc_kinds * (LONG - SHORT)
    ends = lead_rows + jnp.cumsum(lengths)
    starts = jnp.concatenate([jnp.reshape(lead_rows, (1,)), ends]).astype(jnp.int32)
    places = jnp.arange(TOKENS, dtype=jnp.int32)
    return jnp.sum((places[:, None] >= starts[None, :]).astype(jnp.int32), axis=1).astype(jnp.int32)


def raised(result, rng, source, target, blocks, factor):
    owner, partner = [(jnp.arange(result.shape[dim]) // (result.shape[dim] // blocks)).reshape([-1 if axis == dim else 1 for axis in range(result.ndim)]) for dim in (source, target)]
    chosen = jax.random.permutation(rng, blocks)[partner]
    strong = (owner == chosen) | (owner == (partner + blocks // 2) % blocks)
    return jnp.where(strong, factor * result, result)


def block_scale(own_key, shape, pieces, least, high):
    gain = 1.0
    for position, blocks in pieces:
        heights = jax.random.uniform(jax.random.fold_in(jax.random.fold_in(own_key, 6), position), (blocks,), jnp.float32, least / len(pieces), high / len(pieces))
        gain = gain * jnp.repeat(jnp.exp(heights), shape[position] // blocks).reshape((-1,) + (1,) * (len(shape) - 1 - position))
    return gain


def noise(stream_key, dims, spread, limit, shards=(), kind=jnp.bfloat16):
    entries = jax.random.normal(stream_key, dims, jnp.float32) * spread
    if len(shards) > 0:
        entries = block_scale(stream_key, dims, shards, -0.22, 0.18) * entries
    return jnp.clip(entries, min=-limit, max=limit).astype(kind)


def gaussian_with(stream_key, dims, scale, bound, shards, heavy, kind=jnp.bfloat16):
    entries = scale * jax.random.normal(stream_key, dims, jnp.float32)
    if shards:
        entries = entries * block_scale(stream_key, dims, shards, -0.22, 0.18)
    return jnp.clip(raised(entries, jax.random.fold_in(stream_key, 3), *heavy), -bound, bound).astype(kind)


def setup_inputs(seed: int = 0) -> dict:
    key_of = jax.random.split(jax.random.key(seed), 13)
    tokens = gaussian_with(key_of[0], (TOKENS, D), 1.0, 6.0, ((0, 8),), (0, 1, 8, 2.0))
    seg_ids = draw_seg_ids(jax.random.fold_in(key_of[12], 71), 0)
    gain_attn = jnp.clip(1.0 + 0.15 * jax.random.normal(key_of[2], (D,), jnp.float32), 0.25, 1.75)
    w_query = noise(key_of[3], (D, D), D ** -0.5, 0.21875, ((0, 8), (1, 4)))
    w_key = noise(key_of[4], (D, D), D ** -0.5, 0.21875, ((0, 8), (1, 4)))
    w_value = noise(key_of[5], (D, D), D ** -0.5, 0.21875, ((0, 8), (1, 4)))
    conv_kernels = noise(key_of[6], (3, 3, D), 0.8, 4.0, ((2, 4),), jnp.float32)
    w_out = noise(key_of[7], (D, D), (D // 16) ** -0.5, 0.875, ((0, 4), (1, 8)))
    gain_ffn = jnp.clip(1.0 + 0.15 * jax.random.normal(key_of[8], (D,), jnp.float32), 0.25, 1.75)
    w_up = noise(key_of[9], (D, FF), D ** -0.5, 0.21875, ((0, 8), (1, 4)))
    w_down = noise(key_of[10], (FF, D), FF ** -0.5, 0.109375, ((0, 4), (1, 8)))
    cotangent = gaussian_with(key_of[11], (TOKENS, D), 1.0, 6.0, ((0, 8),), (0, 1, 8, 2.0))
    return dict(tokens=tokens, seg_ids=seg_ids, gain_attn=gain_attn, w_query=w_query, w_key=w_key, w_value=w_value, conv_kernels=conv_kernels, w_out=w_out, gain_ffn=gain_ffn, w_up=w_up, w_down=w_down, cotangent=cotangent)


EPS = 1e-06
MASKED = -1e+30

@jax.custom_vjp
def low(v):
    return lax.optimization_barrier(v.astype(jnp.bfloat16)).astype(jnp.float32)

@jax.custom_vjp
def low_back(v):
    return v

def low_keep(v):
    return (low(v), None)

def low_pass(kept, grad):
    return (grad,)

def back_keep(v):
    return (v, None)

def back_low(kept, grad):
    return (low(grad),)
low.defvjp(low_keep, low_pass)
low_back.defvjp(back_keep, back_low)

def matmul_hi(first_mat, second_mat):
    return jnp.dot(first_mat, second_mat, precision=lax.Precision.HIGHEST, preferred_element_type=jnp.float32)

def rms_norm(values, gain_vec):
    factor = lax.rsqrt(lax.optimization_barrier(jnp.mean(values * values, axis=-1, keepdims=True)) + EPS)
    return values * factor * gain_vec

def depthwise(raw_rows, kernel, doc_ids):
    mixed = kernel[0] * raw_rows
    for tap_shift in (1, 2):
        moved_rows = jnp.pad(raw_rows, ((tap_shift, 0), (0, 0)))[:raw_rows.shape[0]]
        moved_ids = jnp.pad(doc_ids, (tap_shift, 0), constant_values=-1)[:doc_ids.shape[0]]
        same_doc = (moved_ids == doc_ids)[:, None]
        mixed = mixed + kernel[tap_shift] * jnp.where(same_doc, moved_rows, 0.0)
    return mixed

def attend(queries, keys_all, values_all, doc_ids):
    total_rows = queries.shape[0]
    span = (REACH + 1) * TOK_DEV
    lead = REACH * TOK_DEV
    keys_pad = jnp.pad(keys_all, ((lead, 0), (0, 0)))
    values_pad = jnp.pad(values_all, ((lead, 0), (0, 0)))
    ids_pad = jnp.pad(doc_ids, (lead, 0), constant_values=-1)
    local_pos = jnp.arange(TOK_DEV, dtype=jnp.int32)
    key_pos = jnp.arange(span, dtype=jnp.int32) - lead

    def one_block(row_start):
        query_blk = lax.dynamic_slice_in_dim(queries, row_start, TOK_DEV, 0).reshape(TOK_DEV, H, DH)
        key_blk = lax.dynamic_slice_in_dim(keys_pad, row_start, span, 0).reshape(span, H, DH)
        value_blk = lax.dynamic_slice_in_dim(values_pad, row_start, span, 0).reshape(span, H, DH)
        query_ids = lax.dynamic_slice_in_dim(doc_ids, row_start, TOK_DEV, 0)
        key_ids = lax.dynamic_slice_in_dim(ids_pad, row_start, span, 0)
        scores = jnp.einsum('qhd,khd->hqk', query_blk, key_blk, precision=lax.Precision.HIGHEST) * DH ** (-0.5)
        scores = low_back(scores)
        allowed = (query_ids[:, None] == key_ids[None, :]) & (key_pos[None, :] <= local_pos[:, None])
        scores = jnp.where(allowed[None], scores, MASKED)
        top_score = lax.optimization_barrier(jnp.max(scores, axis=-1, keepdims=True))
        weights = jnp.exp(scores - top_score)
        weights = low(weights / lax.optimization_barrier(jnp.sum(weights, axis=-1, keepdims=True)))
        mixed = jnp.einsum('hqk,khd->qhd', weights, value_blk, precision=lax.Precision.HIGHEST)
        return mixed.reshape(TOK_DEV, H * DH)
    starts = jnp.arange(total_rows // TOK_DEV, dtype=jnp.int32) * TOK_DEV
    blocks = lax.map(jax.checkpoint(one_block), starts)
    return blocks.reshape(total_rows, H * DH)

def block_forward(tokens, gain_attn, w_query, w_key, w_value, conv_kernels, w_out, gain_ffn, w_up, w_down, doc_ids):
    normed = low(rms_norm(tokens, gain_attn))
    mixed_list = []
    for slot_index, weight_mat in enumerate((w_query, w_key, w_value)):
        raw_rows = low(low_back(matmul_hi(normed, weight_mat)))
        mixed_list.append(low(depthwise(raw_rows, conv_kernels[slot_index], doc_ids)))
    attended = low(low_back(attend(mixed_list[0], mixed_list[1], mixed_list[2], doc_ids)))
    hidden = tokens + low_back(matmul_hi(attended, w_out))
    normed_ffn = low(rms_norm(hidden, gain_ffn))
    up_rows = low_back(matmul_hi(normed_ffn, w_up))
    act_rows = low(jnp.square(jnp.maximum(up_rows, 0.0)))
    return hidden + matmul_hi(act_rows, w_down)

def reference(tokens, seg_ids, gain_attn, w_query, w_key, w_value, conv_kernels, w_out, gain_ffn, w_up, w_down, cotangent):
    params = tuple((argument.astype(jnp.float32) for argument in (tokens, gain_attn, w_query, w_key, w_value, conv_kernels, w_out, gain_ffn, w_up, w_down)))

    def forward(*inputs):
        return block_forward(*inputs, seg_ids)
    output, pull_back = jax.vjp(forward, *params)
    grads = pull_back(cotangent.astype(jnp.float32))
    return (output.astype(jnp.bfloat16), grads[0], grads[1], grads[2], grads[3], grads[4], grads[5], grads[6], grads[7], grads[8], grads[9])
```

```python
import functools

import jax
import jax.numpy as jnp
from jax import lax
from jax.experimental import pallas as pl
from jax.experimental.pallas import tpu as pltpu
from jax.sharding import PartitionSpec as P

DH = 64
REACH = 2
EPS = 1e-06
MASKED = -1e30
TILE = 256
HALO = 16
F32 = jnp.float32
BF16 = jnp.bfloat16
VMEM_LIMIT = 56 * 1024 * 1024
COST = pl.CostEstimate(flops=1, bytes_accessed=1, transcendentals=0)


def params(**kw):
    return pltpu.CompilerParams(vmem_limit_bytes=VMEM_LIMIT, **kw)


def whole():
    return pl.BlockSpec(memory_space=pltpu.VMEM)


def mm(a, b, ca=1, cb=0):
    return lax.dot_general(a, b, (((ca,), (cb,)), ((), ())), preferred_element_type=F32)


def swap(x, axis, mask):
    return lax.ppermute(x, axis, [(i, i ^ mask) for i in range(lax.axis_size(axis))])


def moved(x, axis, distance):
    size = lax.axis_size(axis)
    return lax.ppermute(x, axis, [(i, i + distance) for i in range(size) if 0 <= i + distance < size])


def bit_groups(axis):
    bits = list(range(lax.axis_size(axis).bit_length() - 2, -1, -1))
    upper, groups = bits[:-1], []
    while upper:
        groups.append(tuple(upper[:2]))
        upper = upper[2:]
    return groups + [(0,)]


def bit_of(axis, bit):
    return ((lax.axis_index(axis) >> bit) & 1) == 1


def in_order(pieces, axis, group):
    both = jnp.stack(pieces)
    if len(group) == 1:
        return jnp.where(bit_of(axis, group[0]), both[::-1], both)
    both = both.reshape(2, 2, *both.shape[1:])
    both = jnp.where(bit_of(axis, group[0]), both[::-1], both)
    both = jnp.where(bit_of(axis, group[1]), both[:, ::-1], both)
    return both.reshape(4, *both.shape[2:])


def masks_of(group):
    if len(group) == 1:
        return [0, 1 << group[0]]
    hi, lo = 1 << group[0], 1 << group[1]
    return [0, lo, hi, hi | lo]


def gather_all(shard, axis, after=None):
    lead = 1
    out = shard[None]
    for group in bit_groups(axis):
        pieces = [out] + [swap(out, axis, m) for m in masks_of(group)[1:]]
        if after is not None:
            *pieces, after = lax.optimization_barrier((*pieces, after))
        out = in_order(pieces, axis, group)
        out = jnp.moveaxis(out, 0, 1)
        lead *= out.shape[1]
        out = out.reshape(lead, *shard.shape)
    return out


def chosen(full, axis, group):
    r = 1 << len(group)
    out = full.reshape(-1, r, *full.shape[1:])
    mine = (lax.axis_index(axis) >> group[-1]) & (r - 1)
    return [lax.dynamic_index_in_dim(out, mine ^ (m >> group[-1]), 1, keepdims=False) for m in masks_of(group)]


def sum_scatter(full, axis, groups):
    out = full
    for group in reversed(groups):
        keep, *send = chosen(out, axis, group)
        total = keep.astype(F32)
        for m, part in zip(masks_of(group)[1:], send):
            total = total + swap(part, axis, m).astype(F32)
        out = total.astype(BF16)
    return total.reshape(full.shape[1:])


def sum_everywhere(x, axis):
    mask = 1
    while mask < lax.axis_size(axis):
        x = x + swap(x, axis, mask)
        mask *= 2
    return x


def quarters(own):
    far = swap(own, "head", 2)
    return own, far, swap(own, "head", 1), swap(far, "head", 1)


PAIR = 2 * DH
KV = 3 * PAIR
KEY_LANES = ((0, PAIR), (0, PAIR), (2 * PAIR, KV))
VALUE_LANES = ((PAIR, 2 * PAIR), (PAIR, 2 * PAIR), (2 * PAIR, KV))
KEY_ROWS = (0, DH, 2 * PAIR)
VALUE_ROWS = (PAIR, PAIR + DH, 2 * PAIR + DH)


def arranged(q, k, v):
    return jnp.concatenate([k[..., :PAIR], v[..., :PAIR], k[..., PAIR:], v[..., PAIR:], q], axis=-1)


def separated(x):
    k = jnp.concatenate([x[..., :PAIR], x[..., 2 * PAIR : 2 * PAIR + DH]], axis=-1)
    v = jnp.concatenate([x[..., PAIR : 2 * PAIR], x[..., 2 * PAIR + DH : KV]], axis=-1)
    return x[..., KV:], k, v


def unit_times_gain(x, gain):
    return x * lax.rsqrt(jnp.mean(x * x, axis=-1, keepdims=True) + EPS) * gain


def mix_rows(buf_ref, mix_ref, taps, starts, base, rows):
    mix_ref[...] = (
        taps[0:1] * buf_ref[8 : 8 + rows, :]
        + taps[1:2] * buf_ref[7 : 7 + rows, :]
        + taps[2:3] * buf_ref[6 : 6 + rows, :]
    )
    for start in starts:
        r = start - base

        @pl.when((r >= 0) & (r < rows))
        def _(r=r):
            mix_ref[pl.ds(r, 1), :] = taps[0:1] * buf_ref[pl.ds(8 + r, 1), :]

        @pl.when((r + 1 >= 0) & (r + 1 < rows))
        def _(r=r):
            mix_ref[pl.ds(r + 1, 1), :] = (
                taps[0:1] * buf_ref[pl.ds(9 + r, 1), :] + taps[1:2] * buf_ref[pl.ds(8 + r, 1), :]
            )


def project_own_kernel(
    meta_ref, x_ref, halo_ref, gain_ref, w_ref, taps_ref,
    raw_halo_ref, raw_ref, normed_ref, q_ref, kv_ref, kvt_ref, buf_ref, mix_ref, *, base,
):
    i = pl.program_id(0)
    rows = x_ref.shape[0]
    gain = gain_ref[...]
    w = w_ref[...]

    @pl.when(i == 0)
    def _():
        halo = jnp.where(meta_ref[HAS_ONE] == 1, halo_ref[...].astype(F32), 0.0)
        normed = unit_times_gain(halo, gain).astype(BF16)
        raw_low = mm(normed, w).astype(BF16)
        raw_halo_ref[...] = raw_low[:, KV:]
        buf_ref[0:8, :] = raw_low.astype(F32)[HALO - 8 :, :]

    normed = unit_times_gain(x_ref[...].astype(F32), gain).astype(BF16)
    raw_low = mm(normed, w).astype(BF16)
    normed_ref[...] = normed
    raw_ref[...] = raw_low
    raw = raw_low.astype(F32)
    buf_ref[8 : 8 + rows, :] = raw
    mix_rows(buf_ref, mix_ref, taps_ref[...], [meta_ref[STARTS + n] for n in range(8)], base + i * rows, rows)
    buf_ref[0:8, :] = raw[rows - 8 :, :]
    q_ref[...] = mix_ref[:, KV:].astype(BF16)
    kv = mix_ref[:, :KV]
    kv_ref[...] = kv.astype(BF16)
    kvt_ref[...] = kv.T.astype(BF16)


def project_own(meta, tokens, halo, gain, w, taps):
    rows, dim = tokens.shape
    width = w.shape[1]
    step = 2 * TILE
    tile = lambda n: pl.BlockSpec((step, n), lambda i, *_: (i, 0))
    return pl.pallas_call(
        functools.partial(project_own_kernel, base=REACH * rows),
        out_shape=(
            jax.ShapeDtypeStruct((HALO, width - KV), BF16),
            jax.ShapeDtypeStruct((rows, width), BF16),
            jax.ShapeDtypeStruct((rows, dim), BF16),
            jax.ShapeDtypeStruct((rows, width - KV), BF16),
            jax.ShapeDtypeStruct((rows, KV), BF16),
            jax.ShapeDtypeStruct((KV, rows), BF16),
        ),
        grid_spec=pltpu.PrefetchScalarGridSpec(
            num_scalar_prefetch=1,
            grid=(rows // step,),
            in_specs=[tile(dim), whole(), whole(), whole(), whole()],
            out_specs=(
                whole(),
                tile(width),
                tile(dim),
                tile(width - KV),
                tile(KV),
                pl.BlockSpec((KV, step), lambda i, *_: (0, i)),
            ),
            scratch_shapes=[pltpu.VMEM((8 + step, width), F32), pltpu.VMEM((step, width), F32)],
        ),
        compiler_params=params(),
        cost_estimate=COST,
        name="project_own",
    )(meta, tokens, halo, gain, w, taps)


def project_earlier_kernel(meta_ref, *refs):
    pieces = refs[:8]
    gain_ref, w_ref, taps_ref, raw_ref, normed_ref, kv_ref, kvt_ref, x_ref, buf_ref, mix_ref = refs[8:]
    i = pl.program_id(0)
    rows = x_ref.shape[0]
    quarter = pieces[0].shape[0]

    @pl.when(i == 0)
    def _():
        buf_ref[0:8, :] = jnp.zeros((8, KV), F32)

    for hop in range(REACH):
        for slot, d in enumerate((0, 2, 1, 3)):
            place = 4 * hop + (meta_ref[0] ^ d)

            @pl.when(i == place >> 1)
            def _(piece=pieces[4 * hop + slot], place=place):
                x_ref[pl.ds(pl.multiple_of((place & 1) * quarter, quarter), quarter), :] = piece[...]

    exists = jnp.where(i < pl.num_programs(0) // REACH, meta_ref[HAS_TWO], meta_ref[HAS_ONE])
    x = jnp.where(exists == 1, x_ref[...].astype(F32), 0.0)
    normed = unit_times_gain(x, gain_ref[...]).astype(BF16)
    normed_ref[...] = normed
    raw_low = mm(normed, w_ref[:, :KV]).astype(BF16)
    raw_ref[...] = raw_low
    raw = raw_low.astype(F32)
    buf_ref[8 : 8 + rows, :] = raw
    mix_rows(buf_ref, mix_ref, taps_ref[:, :KV], [meta_ref[STARTS + n] for n in range(8)], i * rows, rows)
    buf_ref[0:8, :] = raw[rows - 8 :, :]
    kv = mix_ref[...]
    kv_ref[...] = kv.astype(BF16)
    kvt_ref[...] = kv.T.astype(BF16)


def project_earlier(meta, pieces, gain, w, taps):
    quarter, dim = pieces[0].shape
    step = 2 * quarter
    span = len(pieces) * quarter
    tile = lambda n: pl.BlockSpec((step, n), lambda i, *_: (i, 0))
    return pl.pallas_call(
        project_earlier_kernel,
        out_shape=(
            jax.ShapeDtypeStruct((span, KV), BF16),
            jax.ShapeDtypeStruct((span, dim), BF16),
            jax.ShapeDtypeStruct((span, KV), BF16),
            jax.ShapeDtypeStruct((KV, span), BF16),
        ),
        grid_spec=pltpu.PrefetchScalarGridSpec(
            num_scalar_prefetch=1,
            grid=(span // step,),
            in_specs=[whole()] * 11,
            out_specs=(tile(KV), tile(dim), tile(KV), pl.BlockSpec((KV, step), lambda i, *_: (0, i))),
            scratch_shapes=[
                pltpu.VMEM((step, dim), BF16),
                pltpu.VMEM((8 + step, KV), F32),
                pltpu.VMEM((step, KV), F32),
            ],
        ),
        compiler_params=params(),
        cost_estimate=COST,
        name="project_earlier",
    )(meta, *pieces, gain, w, taps)


LOW, FULL, STARTS = 1, 5, 9
HAS_ONE, HAS_TWO, NEXT_ONE, NEXT_TWO = 17, 18, 19, 20


def key_loops(meta_ref, qt, begin, end, step):
    low = jnp.maximum(meta_ref[LOW + qt], begin)
    middle = jnp.clip(meta_ref[FULL + qt], low, jnp.maximum(end, low))

    def run(masked):
        def one(kt, carry):
            step(kt, masked)
            return carry

        return one

    lax.fori_loop(low, middle, run(True), 0)
    lax.fori_loop(middle, end, run(False), 0)


def masked_scores(scores, kt, first_ref, diagonal, ahead=0):
    keys = lax.broadcasted_iota(jnp.int32, scores.shape, 0)
    allowed = keys >= first_ref[...] - kt * TILE
    if diagonal:
        allowed = allowed & (keys <= lax.broadcasted_iota(jnp.int32, scores.shape, 1) + ahead)
    return jnp.where(allowed, scores, MASKED)


def query_operands(across):
    zero = jnp.zeros((DH, across.shape[1]), across.dtype)
    return (
        jnp.concatenate([across[:DH], zero], axis=0),
        jnp.concatenate([zero, across[DH:PAIR]], axis=0),
        jnp.concatenate([across[PAIR:], zero], axis=0),
    )


def value_operands(across):
    zero = jnp.zeros((DH, across.shape[1]), across.dtype)
    return (
        jnp.concatenate([across[:DH], zero], axis=0),
        jnp.concatenate([zero, across[DH:PAIR]], axis=0),
        jnp.concatenate([zero, across[PAIR:]], axis=0),
    )


def eights(x, how):
    return how(x.reshape(x.shape[0] // 8, 8, x.shape[1]), axis=0)


def attend_tiles(meta_ref, q_ref, kv_ref, kvt_ref, first_ref, acc_ref, top_ref, sum_ref, *, begin, diagonal):
    qt = pl.program_id(0)
    queries = query_operands((q_ref[...].astype(F32) * (DH**-0.5)).T.astype(BF16))
    end = begin + kv_ref.shape[0] // TILE
    own = begin + qt
    acc_ref[...] = jnp.zeros_like(acc_ref)
    top_ref[...] = jnp.full(top_ref.shape, MASKED, F32)
    sum_ref[...] = jnp.zeros_like(sum_ref)

    def scores_of(kt, h, masked, diag):
        at = pl.ds(pl.multiple_of((kt - begin) * TILE, TILE), TILE)
        scores = mm(kv_ref[at, KEY_LANES[h][0] : KEY_LANES[h][1]], queries[h])
        return masked_scores(scores, kt, first_ref, diag) if masked else scores

    def top(kt, masked, diag=False):
        for h in range(3):
            rows = slice(8 * h, 8 * h + 8)
            top_ref[rows, :] = jnp.maximum(top_ref[rows, :], eights(scores_of(kt, h, masked, diag), jnp.max))

    def add(kt, masked, diag=False):
        at = pl.ds(pl.multiple_of((kt - begin) * TILE, TILE), TILE)
        for h in range(3):
            weights = jnp.exp(scores_of(kt, h, masked, diag) - top_ref[8 * h : 8 * h + 1, :])
            rows = slice(8 * h, 8 * h + 8)
            sum_ref[rows, :] += eights(weights, jnp.sum)
            values = kvt_ref[VALUE_ROWS[h] : VALUE_ROWS[h] + DH, at]
            acc_ref[h * DH : (h + 1) * DH, :] += mm(values, weights.astype(BF16))

    for step in (top, add):
        if diagonal:
            key_loops(meta_ref, qt, begin, own, step)
            step(own, True, True)
        else:
            key_loops(meta_ref, qt, begin, end, step)
        if step is top:
            for h in range(3):
                rows = slice(8 * h, 8 * h + 8)
                top_ref[rows, :] = jnp.broadcast_to(jnp.max(top_ref[rows, :], axis=0, keepdims=True), (8, TILE))
    for h in range(3):
        rows = slice(8 * h, 8 * h + 8)
        sum_ref[rows, :] = jnp.broadcast_to(jnp.sum(sum_ref[rows, :], axis=0, keepdims=True), (8, TILE))


def attend_own_kernel(meta_ref, q_ref, kv_ref, kvt_ref, first_ref, acc_ref, stat_ref, top_ref, sum_ref, *, begin):
    attend_tiles(
        meta_ref, q_ref, kv_ref, kvt_ref, first_ref, acc_ref, top_ref, sum_ref, begin=begin, diagonal=True
    )
    stat_ref[0, 0:24, :] = top_ref[...]
    stat_ref[0, 24:48, :] = sum_ref[...]


def attend_earlier_kernel(
    meta_ref, q_ref, kv_ref, kvt_ref, first_ref, acc_own_ref, stat_own_ref,
    att_ref, ot_ref, lse_ref, acc_ref, top_ref, sum_ref,
):
    attend_tiles(meta_ref, q_ref, kv_ref, kvt_ref, first_ref, acc_ref, top_ref, sum_ref, begin=0, diagonal=False)
    for h in range(3):
        rows = slice(h * DH, (h + 1) * DH)
        top_here, top_own = top_ref[8 * h : 8 * h + 1, :], stat_own_ref[0, 8 * h : 8 * h + 1, :]
        top = jnp.maximum(top_here, top_own)
        here, own = jnp.exp(top_here - top), jnp.exp(top_own - top)
        total = here * sum_ref[8 * h : 8 * h + 1, :] + own * stat_own_ref[0, 24 + 8 * h : 25 + 8 * h, :]
        out = (acc_ref[rows, :] * here + acc_own_ref[rows, :] * own) / total
        ot_ref[rows, :] = out
        att_ref[0, rows, :] = out.astype(BF16)
        lse_ref[0, h : h + 1, :] = top + jnp.log(total)


def slot_of(i, meta):
    d = i ^ meta[0]
    return (d >> 1) | ((d & 1) << 1)


def attend_own(meta, q, kv, kvt, first_row):
    rows, part = q.shape
    tiles = rows // TILE
    across = pl.BlockSpec((part, TILE), lambda i, *_: (0, i))
    return pl.pallas_call(
        functools.partial(attend_own_kernel, begin=REACH * tiles),
        out_shape=(
            jax.ShapeDtypeStruct((part, rows), F32),
            jax.ShapeDtypeStruct((tiles, 48, TILE), F32),
        ),
        grid_spec=pltpu.PrefetchScalarGridSpec(
            num_scalar_prefetch=1,
            grid=(tiles,),
            in_specs=[
                pl.BlockSpec((TILE, part), lambda i, *_: (i, 0)),
                whole(),
                whole(),
                pl.BlockSpec((1, TILE), lambda i, *_: (0, i)),
            ],
            out_specs=(across, pl.BlockSpec((1, 48, TILE), lambda i, *_: (i, 0, 0))),
            scratch_shapes=[pltpu.VMEM((24, TILE), F32), pltpu.VMEM((24, TILE), F32)],
        ),
        compiler_params=params(),
        cost_estimate=COST,
        name="attend_own",
    )(meta, q, kv, kvt, first_row)


def attend_earlier(meta, q, kv, kvt, first_row, acc_own, stat_own):
    rows, part = q.shape
    tiles = rows // TILE
    across = pl.BlockSpec((part, TILE), lambda i, *_: (0, i))
    return pl.pallas_call(
        attend_earlier_kernel,
        out_shape=(
            jax.ShapeDtypeStruct((tiles, part, TILE), BF16),
            jax.ShapeDtypeStruct((part, rows), F32),
            jax.ShapeDtypeStruct((tiles, 8, TILE), F32),
        ),
        grid_spec=pltpu.PrefetchScalarGridSpec(
            num_scalar_prefetch=1,
            grid=(tiles,),
            in_specs=[
                pl.BlockSpec((TILE, part), lambda i, *_: (i, 0)),
                whole(),
                whole(),
                pl.BlockSpec((1, TILE), lambda i, *_: (0, i)),
                across,
                pl.BlockSpec((1, 48, TILE), lambda i, *_: (i, 0, 0)),
            ],
            out_specs=(
                pl.BlockSpec((1, part, TILE), lambda i, meta: (slot_of(i, meta), 0, 0)),
                across,
                pl.BlockSpec((1, 8, TILE), lambda i, *_: (i, 0, 0)),
            ),
            scratch_shapes=[
                pltpu.VMEM((part, TILE), F32),
                pltpu.VMEM((24, TILE), F32),
                pltpu.VMEM((24, TILE), F32),
            ],
        ),
        compiler_params=params(),
        cost_estimate=COST,
        name="attend_earlier",
    )(meta, q, kv, kvt, first_row, acc_own, stat_own)


def back_operands(q_ref, dt_ref, ot_ref, lse_ref):
    scaled = q_ref[...].astype(F32) * (DH**-0.5)
    d_out_t = dt_ref[0]
    d_wide = d_out_t.astype(F32)
    delta = [
        jnp.sum(d_wide[h * DH : (h + 1) * DH] * ot_ref[h * DH : (h + 1) * DH, :], axis=0, keepdims=True)
        for h in range(3)
    ]
    queries, d_out = scaled.astype(BF16), d_wide.T.astype(BF16)
    zero = jnp.zeros((TILE, DH), BF16)
    lane = lax.broadcasted_iota(jnp.int32, (TILE, PAIR), 1)

    def two(x):
        pair = x[:, :PAIR]
        none = jnp.zeros_like(pair)
        return jnp.concatenate([jnp.where(lane < DH, pair, none), jnp.where(lane < DH, none, pair)], axis=0)

    single = jnp.concatenate(
        [
            jnp.concatenate([queries[:, PAIR:], zero], axis=1),
            jnp.concatenate([zero, d_out[:, PAIR:]], axis=1),
        ],
        axis=0,
    )
    return (
        query_operands(scaled.T.astype(BF16)),
        value_operands(d_out_t),
        (two(queries), two(d_out), single),
        [lse_ref[0, h : h + 1, :] for h in range(3)],
        delta,
    )


def back_step(kt, masked, diag, operands, refs, begin, lead, ahead=0):
    queries_t, d_out_t, stacked, lse, delta = operands
    kv_ref, kvt_ref, first_ref, grad_ref, dq_ref = refs
    at = pl.ds(pl.multiple_of((kt - begin) * TILE, TILE), TILE)
    weights, grads = [], []
    for h in range(3):
        scores = mm(kv_ref[at, KEY_LANES[h][0] : KEY_LANES[h][1]], queries_t[h])
        if masked:
            scores = masked_scores(scores, kt, first_ref, diag, ahead)
        probs = jnp.exp(scores - lse[h])
        d_probs = mm(kv_ref[at, VALUE_LANES[h][0] : VALUE_LANES[h][1]], d_out_t[h])
        d_scores = (probs * (d_probs - delta[h])).astype(BF16)
        weights.append(probs.astype(BF16))
        grads.append(d_scores)
        dq_ref[h * DH : (h + 1) * DH, :] += mm(kvt_ref[KEY_ROWS[h] : KEY_ROWS[h] + DH, at], d_scores)
    to = pl.ds(pl.multiple_of(lead + (kt - begin) * TILE, 8), TILE)
    grad_ref[to, :PAIR] += mm(jnp.concatenate(grads[:2], axis=1), stacked[0])
    grad_ref[to, PAIR : 2 * PAIR] += mm(jnp.concatenate(weights[:2], axis=1), stacked[1])
    grad_ref[to, 2 * PAIR : KV] += mm(jnp.concatenate([grads[2], weights[2]], axis=1), stacked[2])


def unmix_rows(grad_ref, raw_ref, fix_ref, taps, starts, rows, sums_ref):
    width = grad_ref.shape[1]

    def raw_row(r):
        group = raw_ref[pl.ds(pl.multiple_of((r // HALO) * HALO, HALO), HALO), :].astype(F32)
        row = lax.broadcasted_iota(jnp.int32, group.shape, 0)
        return jnp.sum(jnp.where(row == r % HALO, group, 0.0), axis=0, keepdims=True)

    sums_ref[...] = jnp.zeros_like(sums_ref)
    inside = [(s >= 1) & (s <= rows + 1) for s in starts]
    for n, s in enumerate(starts):

        @pl.when(inside[n])
        def _(n=n, s=s):
            one_before = grad_ref[pl.ds(7 + s, 1), :]
            fix_ref[2 * n : 2 * n + 1, :] = taps[0:1] * one_before
            fix_ref[2 * n + 1 : 2 * n + 2, :] = taps[0:1] * grad_ref[pl.ds(6 + s, 1), :] + taps[1:2] * one_before
            here = grad_ref[pl.ds(8 + s, 1), :]

            @pl.when(s >= 2)
            def _():
                sums_ref[2:3, :] -= raw_row(jnp.maximum(s - 2, 0)) * here

            @pl.when(s <= rows)
            def _():
                raw_one = raw_row(s - 1)
                sums_ref[1:2, :] -= raw_one * here
                following = starts[n + 1] if n + 1 < len(starts) else s + 2

                @pl.when(following != s + 1)
                def _():
                    sums_ref[2:3, :] -= raw_one * grad_ref[pl.ds(9 + s, 1), :]

    sizes = [HALO] * (1 if rows % TILE else 0) + [TILE] * (rows // TILE)
    lo = 0
    totals = [jnp.zeros((8, width), F32) for _ in range(3)]
    for size in sizes:
        now = grad_ref[8 + lo : 8 + lo + size, :]
        one = grad_ref[9 + lo : 9 + lo + size, :]
        two = grad_ref[10 + lo : 10 + lo + size, :]
        raw = raw_ref[lo : lo + size, :].astype(F32)
        for j, shifted in enumerate((now, one, two)):
            totals[j] = totals[j] + eights(raw * shifted, jnp.sum)
        grad_ref[8 + lo : 8 + lo + size, :] = taps[0:1] * now + taps[1:2] * one + taps[2:3] * two
        lo += size
    for j in range(3):
        sums_ref[j : j + 1, :] += jnp.sum(totals[j], axis=0, keepdims=True)
    for n in reversed(range(len(starts))):

        @pl.when(inside[n])
        def _(n=n, s=starts[n]):
            grad_ref[pl.ds(7 + s, 1), :] = fix_ref[2 * n : 2 * n + 1, :]
            grad_ref[pl.ds(6 + s, 1), :] = fix_ref[2 * n + 1 : 2 * n + 2, :]


def earlier_back_kernel(
    meta_ref, q_ref, dt_ref, ot_ref, lse_ref, first_ref, kv_ref, kvt_ref, kv_own_ref, kvt_own_ref, raw_ref,
    raw_halo_ref, taps_ref, dq_ref, two_ref, one_ref, next_ref, sums_ref, sums_q_ref,
    grad_ref, grad_q_ref, fix_ref, fix_q_ref,
):
    qt = pl.program_id(0)
    before = kv_ref.shape[0]
    tiles = before // TILE

    @pl.when(qt == 0)
    def _():
        grad_ref[...] = jnp.zeros_like(grad_ref)
        grad_q_ref[...] = jnp.zeros_like(grad_q_ref)

    dq_ref[...] = jnp.zeros_like(dq_ref)

    @pl.when(meta_ref[LOW + qt] <= tiles)
    def _():
        operands = back_operands(q_ref, dt_ref, ot_ref, lse_ref)
        refs = (kv_ref, kvt_ref, first_ref, grad_ref, dq_ref)
        own = (kv_own_ref, kvt_own_ref, first_ref, grad_ref, dq_ref)
        key_loops(meta_ref, qt, 0, tiles, lambda kt, masked: back_step(kt, masked, False, operands, refs, 0, 8))
        back_step(tiles, True, True, operands, own, tiles, 8 + before, qt * TILE)

    @pl.when(qt == 0)
    def _():
        grad_q_ref[8 + HALO : 16 + HALO, :] = dq_ref[:, :PAIR].T[:8] * (DH**-0.5)

    @pl.when(qt == pl.num_programs(0) - 1)
    def _():
        starts = [meta_ref[STARTS + n] for n in range(8)]
        next_ref[...] = grad_ref[8 + before : 8 + before + TILE, :]
        unmix_rows(grad_ref, raw_ref, fix_ref, taps_ref[:, :KV], starts, before, sums_ref)
        starts = [s - (before - HALO) for s in starts]
        unmix_rows(grad_q_ref, raw_halo_ref, fix_q_ref, taps_ref[:, KV:], starts, HALO, sums_q_ref)
        half = before // 2
        two_ref[...] = grad_ref[8 : 8 + half, :].astype(BF16)
        one_ref[0:half, :] = grad_ref[8 + half : 8 + before, :].astype(BF16)
        queries = grad_q_ref[8 : 8 + HALO, :]
        one_ref[half : half + HALO, :] = jnp.concatenate([queries, jnp.zeros_like(queries)], axis=1).astype(BF16)


def tile_specs(part):
    return [
        pl.BlockSpec((TILE, part), lambda i, *_: (i, 0)),
        pl.BlockSpec((1, part, TILE), lambda i, meta: (slot_of(i, meta), 0, 0)),
        pl.BlockSpec((part, TILE), lambda i, *_: (0, i)),
        pl.BlockSpec((1, 8, TILE), lambda i, *_: (i, 0, 0)),
        pl.BlockSpec((1, TILE), lambda i, *_: (0, i)),
    ]


def earlier_back(meta, q, d_out_t, out_t, lse, first_row, kv, kvt, kv_own, kvt_own, raw, raw_halo, taps):
    rows, part = q.shape
    before = kv.shape[0]
    return pl.pallas_call(
        earlier_back_kernel,
        out_shape=(
            jax.ShapeDtypeStruct((part, rows), F32),
            jax.ShapeDtypeStruct((rows, KV), BF16),
            jax.ShapeDtypeStruct((rows + HALO, KV), BF16),
            jax.ShapeDtypeStruct((TILE, KV), F32),
            jax.ShapeDtypeStruct((8, KV), F32),
            jax.ShapeDtypeStruct((8, part), F32),
        ),
        grid_spec=pltpu.PrefetchScalarGridSpec(
            num_scalar_prefetch=1,
            grid=(rows // TILE,),
            in_specs=tile_specs(part)
            + [
                whole(),
                whole(),
                pl.BlockSpec((TILE, KV), lambda i, *_: (0, 0)),
                pl.BlockSpec((KV, TILE), lambda i, *_: (0, 0)),
                whole(),
                whole(),
                whole(),
            ],
            out_specs=(pl.BlockSpec((part, TILE), lambda i, *_: (0, i)), *[whole()] * 5),
            scratch_shapes=[
                pltpu.VMEM((8 + before + TILE + 8, KV), F32),
                pltpu.VMEM((8 + HALO + 8, part), F32),
                pltpu.VMEM((16, KV), F32),
                pltpu.VMEM((16, part), F32),
            ],
        ),
        compiler_params=params(),
        cost_estimate=COST,
        name="earlier_back",
    )(meta, q, d_out_t, out_t, lse, first_row, kv, kvt, kv_own, kvt_own, raw, raw_halo, taps)


def own_back_kernel(
    meta_ref, q_ref, dt_ref, ot_ref, lse_ref, first_ref, dq_in_ref, kv_ref, kvt_ref, raw_ref, taps_ref, next_ref,
    d_raw_ref, sums_ref, dq_ref, grad_ref, fix_ref, *, begin,
):
    qt = pl.program_id(0)
    rows = kv_ref.shape[0]

    @pl.when(qt == 0)
    def _():
        grad_ref[...] = jnp.zeros_like(grad_ref)
        grad_ref[8 : 8 + TILE, :KV] = next_ref[...]

    dq_ref[...] = dq_in_ref[...]

    @pl.when(qt > 0)
    def _():
        operands = back_operands(q_ref, dt_ref, ot_ref, lse_ref)
        refs = (kv_ref, kvt_ref, first_ref, grad_ref, dq_ref)
        step = lambda kt, masked: back_step(kt, masked, False, operands, refs, begin, 8)
        key_loops(meta_ref, qt, begin + 1, begin + qt, step)
        back_step(begin + qt, True, True, operands, refs, begin, 8)

    to = pl.ds(pl.multiple_of(8 + qt * TILE, 8), TILE)
    grad_ref[to, KV:] = dq_ref[...].T * (DH**-0.5)

    @pl.when(qt == pl.num_programs(0) - 1)
    def _():
        starts = [meta_ref[STARTS + n] - begin * TILE for n in range(8)]
        unmix_rows(grad_ref, raw_ref, fix_ref, taps_ref[...], starts, rows, sums_ref)
        d_raw_ref[...] = grad_ref[8 : 8 + rows, :].astype(BF16)


def own_back(meta, q, d_out_t, out_t, lse, first_row, dq_t, kv, kvt, raw, taps, grad_next):
    rows, part = q.shape
    width = raw.shape[1]
    return pl.pallas_call(
        functools.partial(own_back_kernel, begin=REACH * rows // TILE),
        out_shape=(
            jax.ShapeDtypeStruct((rows, width), BF16),
            jax.ShapeDtypeStruct((8, width), F32),
        ),
        grid_spec=pltpu.PrefetchScalarGridSpec(
            num_scalar_prefetch=1,
            grid=(rows // TILE,),
            in_specs=tile_specs(part) + [pl.BlockSpec((part, TILE), lambda i, *_: (0, i))] + [whole()] * 5,
            out_specs=(whole(), whole()),
            scratch_shapes=[
                pltpu.VMEM((part, TILE), F32),
                pltpu.VMEM((8 + rows + 8, width), F32),
                pltpu.VMEM((16, width), F32),
            ],
        ),
        compiler_params=params(),
        cost_estimate=COST,
        name="own_back",
    )(meta, q, d_out_t, out_t, lse, first_row, dq_t, kv, kvt, raw, taps, grad_next)


def after_attend_kernel(a0, a1, a2, a3, w0, w1, w2, w3, x_ref, gain_ref, hidden_ref, normed_ref):
    branch = mm(a0[...], w0[...], 0, 0)
    for a, w in ((a1, w1), (a2, w2), (a3, w3)):
        branch = branch + mm(a[...], w[...], 0, 0)
    hidden = x_ref[...].astype(F32) + branch
    hidden_ref[...] = hidden
    factor = lax.rsqrt(jnp.mean(hidden * hidden, axis=-1, keepdims=True) + EPS)
    normed_ref[...] = (hidden * factor * gain_ref[...]).astype(BF16)


def after_attend(attended, w_out, x, gain):
    rows, dim = x.shape
    return pl.pallas_call(
        after_attend_kernel,
        out_shape=(jax.ShapeDtypeStruct((rows, dim), F32), jax.ShapeDtypeStruct((rows, dim), BF16)),
        in_specs=[whole()] * 10,
        out_specs=(whole(), whole()),
        compiler_params=params(),
        cost_estimate=COST,
        name="after_attend",
    )(*attended, *w_out, x, gain)


def feed_kernel(x_ref, cot_ref, up_ref, down_ref, act_ref, d_up_ref, keep_ref, send_ref):
    up = mm(x_ref[...], up_ref[...])
    pos = jnp.maximum(up, 0.0)
    act_ref[...] = (pos * pos).astype(BF16)
    d_act = mm(cot_ref[...], down_ref[...])
    d_up = (d_act * 2.0 * pos).astype(BF16)
    d_up_ref[...] = d_up
    back = mm(d_up, up_ref[...], 1, 1).astype(BF16)

    @pl.when(pl.program_id(0) == 0)
    def _():
        keep_ref[...] = back

    @pl.when(pl.program_id(0) == 1)
    def _():
        send_ref[...] = back


def feed(x, cot, w_up, w_down_t):
    rows, dim = x.shape
    units = w_up.shape[1]
    step = rows // 2
    tile = lambda n: pl.BlockSpec((step, n), lambda i: (i, 0))
    return pl.pallas_call(
        feed_kernel,
        out_shape=(
            jax.ShapeDtypeStruct((rows, units), BF16),
            jax.ShapeDtypeStruct((rows, units), BF16),
            jax.ShapeDtypeStruct((step, dim), BF16),
            jax.ShapeDtypeStruct((step, dim), BF16),
        ),
        grid=(2,),
        in_specs=[tile(dim), tile(dim), whole(), whole()],
        out_specs=(tile(units), tile(units), whole(), whole()),
        compiler_params=params(),
        cost_estimate=COST,
        name="feed",
    )(x, cot, w_up, w_down_t)


def feed_out_kernel(act_ref, down_ref, keep_ref, send_ref):
    out = mm(act_ref[...], down_ref[...], 1, 1).astype(BF16)

    @pl.when(pl.program_id(0) == 0)
    def _():
        keep_ref[...] = out

    @pl.when(pl.program_id(0) == 1)
    def _():
        send_ref[...] = out


def feed_out(act, w_down_t):
    rows, units = act.shape
    dim = w_down_t.shape[0]
    half = jax.ShapeDtypeStruct((rows // 2, dim), BF16)
    return pl.pallas_call(
        feed_out_kernel,
        out_shape=(half, half),
        grid=(2,),
        in_specs=[pl.BlockSpec((rows // 2, units), lambda i: (i, 0)), whole()],
        out_specs=(whole(), whole()),
        compiler_params=params(),
        cost_estimate=COST,
        name="feed_out",
    )(act, w_down_t)


def feed_grads_kernel(x_ref, d_up_ref, cot_ref, act_ref, up_ref, down_ref):
    up_ref[...] = mm(x_ref[...], d_up_ref[...], 0, 0).astype(BF16)
    down_ref[...] = mm(cot_ref[...], act_ref[...], 0, 0).astype(BF16)


def feed_grads(x, d_up, cot, act):
    rows, dim = x.shape
    units = act.shape[1]
    block = pl.BlockSpec((rows, TILE), lambda i: (0, i))
    out = pl.BlockSpec((TILE, units), lambda i: (i, 0))
    shape = jax.ShapeDtypeStruct((dim, units), BF16)
    return pl.pallas_call(
        feed_grads_kernel,
        out_shape=(shape, shape),
        grid=(dim // TILE,),
        in_specs=[block, whole(), block, whole()],
        out_specs=(out, out),
        compiler_params=params(),
        cost_estimate=COST,
        name="feed_grads",
    )(x, d_up, cot, act)


def mix_grads_kernel(e_ref, two_ref, one_ref, o_ref, d_raw_ref, out_t_ref, grad_ref):
    rows = two_ref.shape[0]
    part = out_t_ref.shape[1]
    grad = mm(o_ref[...], d_raw_ref[...], 0, 0)
    kv = mm(e_ref[:rows, :], two_ref[...], 0, 0) + mm(e_ref[rows:, :], one_ref[:rows, :], 0, 0)
    q = mm(e_ref[2 * rows - HALO :, :], one_ref[rows:, :], 0, 0)[:, :part]
    grad_ref[:, :KV] = (grad[:, :KV] + kv).astype(BF16)
    grad_ref[:, KV:] = jnp.concatenate([grad[:, KV:] + q, out_t_ref[...].astype(F32)], axis=1).astype(BF16)


def mix_grads(normed_e, d_two, d_one, normed, d_raw, out_t):
    dim = normed.shape[1]
    width = d_raw.shape[1] + out_t.shape[1]
    block = lambda x: pl.BlockSpec((x.shape[0], TILE), lambda i: (0, i))
    out = lambda n: pl.BlockSpec((TILE, n), lambda i: (i, 0))
    return pl.pallas_call(
        mix_grads_kernel,
        out_shape=jax.ShapeDtypeStruct((dim, width), BF16),
        grid=(dim // TILE,),
        in_specs=[block(normed_e), whole(), whole(), block(normed), whole(), out(out_t.shape[1])],
        out_specs=out(width),
        compiler_params=params(),
        cost_estimate=COST,
        name="mix_grads",
    )(normed_e, d_two, d_one, normed, d_raw, out_t)


def before_back_kernel(
    s_ref, r_ref, hidden_ref, gain_ref, cot_ref, w0, w1, w2, w3, a0, a1, a2, a3,
    d_hidden_ref, d0, d1, d2, d3, keep_ref, send_ref, sum_ref,
):
    d_normed = s_ref[...].astype(F32) + r_ref[...].astype(F32)
    hidden = hidden_ref[...]
    factor = lax.rsqrt(jnp.mean(hidden * hidden, axis=-1, keepdims=True) + EPS)
    unit = hidden * factor
    sum_ref[...] = jnp.sum(d_normed * unit, axis=0, keepdims=True)
    scaled = d_normed * gain_ref[...]
    inner = jnp.mean(scaled * unit, axis=-1, keepdims=True)
    d_hidden = cot_ref[...].astype(F32) + factor * (scaled - unit * inner)
    d_hidden_ref[...] = d_hidden
    d_branch = d_hidden.astype(BF16)
    for w, d in ((w0, d0), (w1, d1), (w2, d2), (w3, d3)):
        d[...] = mm(w[...], d_branch, 1, 1).astype(BF16)
    for a, to in ((a0, keep_ref.at[0]), (a1, keep_ref.at[1]), (a2, send_ref.at[0]), (a3, send_ref.at[1])):
        to[...] = mm(a[...], d_branch).astype(BF16)


def before_back(chip_sum, far_sum, hidden, gain, cot, w_out, attended):
    rows, dim = hidden.shape
    part = w_out[0].shape[0]
    return pl.pallas_call(
        before_back_kernel,
        out_shape=(
            jax.ShapeDtypeStruct((rows, dim), F32),
            *[jax.ShapeDtypeStruct((part, rows), BF16)] * 4,
            *[jax.ShapeDtypeStruct((2, part, dim), BF16)] * 2,
            jax.ShapeDtypeStruct((1, dim), F32),
        ),
        in_specs=[whole()] * 13,
        out_specs=tuple([whole()] * 8),
        compiler_params=params(),
        cost_estimate=COST,
        name="before_back",
    )(chip_sum, far_sum, hidden, gain, cot, *w_out, *attended)


def d_normed_kernel(meta_ref, own_ref, one_ref, halo_ref, two_ref, x_ref, w_ref, keep_ref, send_ref, sum_ref):
    i = pl.program_id(0)
    step = own_ref.shape[0]
    later = jnp.where(meta_ref[NEXT_ONE] == 1, one_ref[...].astype(F32), 0.0)
    later = later + jnp.where(meta_ref[NEXT_TWO] == 1, two_ref[...].astype(F32), 0.0)
    own = own_ref[...].astype(F32)
    queries = own[:, KV:]
    part = queries.shape[1]
    last = (i == pl.num_programs(0) - 1) & (meta_ref[NEXT_ONE] == 1)
    halo = jnp.where(last, halo_ref[...].astype(F32)[:, :part], 0.0)
    queries = queries + jnp.concatenate([jnp.zeros((step - HALO, part), F32), halo], axis=0)
    d_raw = jnp.concatenate([own[:, :KV] + later, queries], axis=1).astype(BF16)
    d_normed = mm(d_raw, w_ref[...], 1, 1)
    for n in range(step // TILE):
        slot = slot_of(i * (step // TILE) + n, meta_ref)
        rows = d_normed[n * TILE : (n + 1) * TILE].astype(BF16)
        to = pl.ds(pl.multiple_of((slot & 1) * TILE, TILE), TILE)

        @pl.when(slot < 2)
        def _(rows=rows, to=to):
            keep_ref[to, :] = rows

        @pl.when(slot >= 2)
        def _(rows=rows, to=to):
            send_ref[to, :] = rows

    x = x_ref[...].astype(F32)
    unit = x * lax.rsqrt(jnp.mean(x * x, axis=-1, keepdims=True) + EPS)

    @pl.when(i == 0)
    def _():
        sum_ref[...] = jnp.zeros_like(sum_ref)

    sum_ref[...] += jnp.sum(d_normed * unit, axis=0, keepdims=True)


def d_normed_parts(meta, own, one, two, x, w):
    rows, dim = x.shape
    width = w.shape[1]
    step = 2 * TILE
    tile = lambda n: pl.BlockSpec((step, n), lambda i, *_: (i, 0))
    return pl.pallas_call(
        d_normed_kernel,
        out_shape=(
            jax.ShapeDtypeStruct((rows // 2, dim), BF16),
            jax.ShapeDtypeStruct((rows // 2, dim), BF16),
            jax.ShapeDtypeStruct((1, dim), F32),
        ),
        grid_spec=pltpu.PrefetchScalarGridSpec(
            num_scalar_prefetch=1,
            grid=(rows // step,),
            in_specs=[
                tile(width),
                tile(KV),
                pl.BlockSpec((HALO, KV), lambda i, *_: (rows // HALO, 0)),
                tile(KV),
                tile(dim),
                whole(),
            ],
            out_specs=(whole(), whole(), pl.BlockSpec((1, dim), lambda i, *_: (0, 0))),
        ),
        compiler_params=params(),
        cost_estimate=COST,
        name="d_normed_parts",
    )(meta, own, one, one, two, x, w)


def grad_tokens_kernel(s_ref, r_ref, x_ref, gain_ref, d_hidden_ref, out_ref):
    d_normed = s_ref[...].astype(F32) + r_ref[...].astype(F32)
    x = x_ref[...].astype(F32)
    factor = lax.rsqrt(jnp.mean(x * x, axis=-1, keepdims=True) + EPS)
    unit = x * factor
    scaled = d_normed * gain_ref[...]
    inner = jnp.mean(scaled * unit, axis=-1, keepdims=True)
    out_ref[...] = (d_hidden_ref[...] + factor * (scaled - unit * inner)).astype(BF16)


def grad_tokens_own(chip_sum, far_sum, x, gain, d_hidden):
    return pl.pallas_call(
        grad_tokens_kernel,
        out_shape=jax.ShapeDtypeStruct(x.shape, BF16),
        in_specs=[whole()] * 5,
        out_specs=whole(),
        compiler_params=params(),
        name="grad_tokens_own",
    )(chip_sum, far_sum, x, gain, d_hidden)


def by_place(pieces):
    hi, lo = bit_of("head", 1), bit_of("head", 0)
    both = jnp.stack([jnp.stack([pieces[0], pieces[2]]), jnp.stack([pieces[1], pieces[3]])])
    both = jnp.where(hi, both[::-1], both)
    both = jnp.where(lo, both[:, ::-1], both)
    return both.reshape(-1, both.shape[-1])


def sum_halves(keep, send):
    return (keep.astype(F32) + swap(send, "head", 1).astype(F32)).astype(BF16)


def body(
    tokens,
    seg_ids,
    gain_attn,
    w_query,
    w_key,
    w_value,
    conv_kernels,
    w_out,
    gain_ffn,
    w_up,
    w_down,
    cotangent,
):
    rows, dim = tokens.shape
    part = conv_kernels.shape[2]
    quarter = rows // lax.axis_size("head")
    blk = lax.axis_index("blk")
    head = lax.axis_index("head")
    own_quarter = lax.dynamic_slice_in_dim(tokens, head * quarter, quarter)
    two = moved(own_quarter, "blk", 2)
    halo = moved(tokens[rows - HALO :], "blk", 1)
    w_mix = gather_all(arranged(w_query, w_key, w_value), "blk").reshape(dim, 3 * part)
    one = swap(jnp.where(bit_of("blk", 0), two, own_quarter), "blk", 1)
    pieces = quarters(two) + quarters(one)
    span = (REACH + 1) * rows
    padded_ids = jnp.pad(seg_ids, (REACH * rows, 0), constant_values=-1)
    window = lax.dynamic_slice_in_dim(padded_ids, blk * rows, span)
    starts = jnp.sum((window[None, :] <= window[0] + jnp.arange(8)[:, None]).astype(jnp.int32), axis=1)
    place = jnp.arange(REACH * rows, span, dtype=jnp.int32)
    first_row = jnp.max(jnp.where(starts[:, None] <= place, starts[:, None], 0), axis=0)
    low = first_row[::TILE] // TILE
    full = (first_row[TILE - 1 :: TILE] + TILE - 1) // TILE
    last = lax.axis_size("blk") - 1
    exists = jnp.stack([blk >= 1, blk >= 2, blk + 1 <= last, blk + 2 <= last])
    meta = jnp.concatenate([head[None], low, full, starts, exists]).astype(jnp.int32)
    first_row = first_row[None]
    taps = arranged(*conv_kernels)
    gain_one, gain_two = gain_attn[None], gain_ffn[None]

    raw_halo, raw, normed, q, kv, kvt = project_own(meta, tokens, halo, gain_one, w_mix, taps)
    acc_own, stat_own = attend_own(meta, q, kv, kvt, first_row)
    raw_e, normed_e, kv_e, kvt_e = project_earlier(meta, pieces, gain_one, w_mix, taps)
    att, out_t, lse = attend_earlier(meta, q, kv_e, kvt_e, first_row, acc_own, stat_own)

    units = w_up.shape[1]
    shard = w_up.shape[0]
    packed = jnp.concatenate([w_up, w_out.T.reshape(-1, units)])
    packed, _ = lax.optimization_barrier((packed, one))
    wide = gather_all(packed, "blk")
    full_up = wide[:, :shard].reshape(dim, units)
    out_full = wide[:, shard:].reshape(dim, part).T
    packed_down, _ = lax.optimization_barrier((w_down.T, pieces[5]))
    down_t = gather_all(packed_down, "blk", raw_e).reshape(dim, units)
    out_pieces = quarters(out_full)

    near = swap(att[2:], "head", 1)
    across = swap(jnp.stack([att[1], near[1]]), "head", 2)
    attended = (att[0], across[0], near[0], across[1])
    hidden, normed_two = after_attend(attended, out_pieces, own_quarter, gain_two)
    hi, lo = bit_of("head", 1), bit_of("head", 0)
    cot = cotangent.reshape(2, 2, quarter, dim)
    cot = jnp.where(hi, cot[::-1], cot)
    cot = jnp.where(lo, cot[:, ::-1], cot)
    cot = jnp.swapaxes(cot, 0, 1).reshape(rows, dim)
    ffn_in = jnp.concatenate(quarters(normed_two))
    act, d_up, *back = feed(ffn_in, cot, full_up, down_t)
    chip_back = sum_halves(*back)
    grad_up, grad_down_t = feed_grads(ffn_in, d_up, cot, act)
    both = jnp.stack([grad_up.reshape(-1, shard, units), grad_down_t.reshape(-1, shard, units)], axis=1)
    group = bit_groups("blk")[-1]
    both, both_send = chosen(both, "blk", group)
    both_near = swap(both_send, "blk", 1)
    far_back = swap(chip_back[quarter:], "head", 2)
    d_hidden, *d_outs, keep_out, send_out, gain_two_part = before_back(
        chip_back[:quarter], far_back, hidden, gain_two, cot[:quarter], out_pieces, attended
    )
    across = swap(jnp.stack([d_outs[1], d_outs[3]]), "head", 2)
    near = swap(jnp.stack([d_outs[2], across[1]]), "head", 1)
    d_out_t = jnp.stack([d_outs[0], across[0], near[0], near[1]])
    d_out_t, both_near = lax.optimization_barrier((d_out_t, both_near))

    dq_t, d_two, d_one, grad_next, sums_before, sums_halo = earlier_back(
        meta, q, d_out_t, out_t, lse, first_row, kv_e, kvt_e, kv, kvt, raw_e, raw_halo, taps
    )
    from_two = moved(d_two, "blk", -2)
    from_one = moved(d_one, "blk", -1)
    d_raw, sums_own = own_back(meta, q, d_out_t, out_t, lse, first_row, dq_t, kv, kvt, raw, taps, grad_next)

    both = (both.astype(F32) + both_near.astype(F32)).astype(BF16)
    both = sum_scatter(both, "blk", bit_groups("blk")[:-1])
    grad_up_shard, grad_down_shard = both[0], both[1].T
    act_late, _ = lax.optimization_barrier((act, dq_t))
    chip_ffn = sum_halves(*feed_out(act_late, down_t))
    far_ffn = swap(chip_ffn[quarter:], "head", 2)
    output = (hidden + (chip_ffn[:quarter].astype(F32) + far_ffn.astype(F32))).astype(BF16)
    output = by_place(quarters(output))
    chip_out = keep_out.astype(F32) + swap(send_out, "head", 1).astype(F32)
    far = swap(chip_out[1].astype(BF16), "head", 2)
    grad_out = (chip_out[0] + far.astype(F32)).astype(BF16).T

    grad_mix = mix_grads(normed_e, d_two, d_one, normed, d_raw, grad_out)
    mix_shard = sum_scatter(grad_mix.reshape(-1, shard, 4 * part), "blk", bit_groups("blk"))
    grad_query_shard, grad_key_shard, grad_value_shard = separated(mix_shard[:, : 3 * part])
    grad_out_shard = mix_shard[:, 3 * part :].T

    *back, gain_one_part = d_normed_parts(meta, d_raw, from_one, from_two, tokens, w_mix)
    chip_back = sum_halves(*back)
    far_back = swap(chip_back[quarter:], "head", 2)
    grad_tokens = grad_tokens_own(chip_back[:quarter], far_back, own_quarter, gain_one, d_hidden)
    grad_tokens = by_place(quarters(grad_tokens)).astype(F32)

    taps_part = jnp.concatenate([sums_own[:3, :KV] + sums_before[:3], sums_own[:3, KV:] + sums_halo[:3]], axis=1)
    taps_part = jnp.stack(separated(taps_part)).reshape(-1)
    gains = sum_everywhere(jnp.concatenate([gain_two_part, gain_one_part]), "head")
    small = sum_everywhere(jnp.concatenate([gains.reshape(-1), taps_part]), "blk")
    grad_gain_ffn, grad_gain_attn = small[:dim], small[dim : 2 * dim]
    grad_kernels = small[2 * dim :].reshape(3, 3, part)
    return (
        output,
        grad_tokens,
        grad_gain_attn,
        grad_query_shard,
        grad_key_shard,
        grad_value_shard,
        grad_kernels,
        grad_out_shard,
        grad_gain_ffn,
        grad_up_shard,
        grad_down_shard,
    )


def solution(mesh):
    return jax.shard_map(
        body,
        mesh=mesh,
        in_specs=(
            P("blk", None),
            P(),
            P(),
            P("blk", "head"),
            P("blk", "head"),
            P("blk", "head"),
            P(None, None, "head"),
            P("head", "blk"),
            P(),
            P("blk", "head"),
            P("head", "blk"),
            P("blk", None),
        ),
        out_specs=(
            P("blk", None),
            P("blk", None),
            P(),
            P("blk", "head"),
            P("blk", "head"),
            P("blk", "head"),
            P(None, None, "head"),
            P("head", "blk"),
            P(),
            P("blk", "head"),
            P("head", "blk"),
        ),
        check_vma=False,
    )
```

```python
import functools

import jax
import jax.numpy as jnp
from jax import lax
from jax.experimental import pallas as pl
from jax.experimental.pallas import tpu as pltpu
from jax.sharding import PartitionSpec as P

DH = 64
REACH = 2
EPS = 1e-06
MASKED = -1e30
TILE = 256
HALO = 16
F32 = jnp.float32
BF16 = jnp.bfloat16
MIB = 1024 * 1024
COST = pl.CostEstimate(flops=1, bytes_accessed=1, transcendentals=0)


def params(mib=20):
    return pltpu.CompilerParams(vmem_limit_bytes=mib * MIB)


def whole():
    return pl.BlockSpec(memory_space=pltpu.VMEM)


def mm(a, b, ca=1, cb=0):
    return lax.dot_general(a, b, (((ca,), (cb,)), ((), ())), preferred_element_type=F32)


def swap(x, axis, mask):
    return lax.ppermute(x, axis, [(i, i ^ mask) for i in range(lax.axis_size(axis))])


def moved(x, axis, distance):
    size = lax.axis_size(axis)
    return lax.ppermute(x, axis, [(i, i + distance) for i in range(size) if 0 <= i + distance < size])


def bit_groups(axis):
    bits = list(range(lax.axis_size(axis).bit_length() - 2, -1, -1))
    upper, groups = bits[:-1], []
    while upper:
        groups.append(tuple(upper[:2]))
        upper = upper[2:]
    return groups + [(0,)]


def bit_of(axis, bit):
    return ((lax.axis_index(axis) >> bit) & 1) == 1


def in_order(pieces, axis, group):
    both = jnp.stack(pieces)
    if len(group) == 1:
        return jnp.where(bit_of(axis, group[0]), both[::-1], both)
    both = both.reshape(2, 2, *both.shape[1:])
    both = jnp.where(bit_of(axis, group[0]), both[::-1], both)
    both = jnp.where(bit_of(axis, group[1]), both[:, ::-1], both)
    return both.reshape(4, *both.shape[2:])


def masks_of(group):
    if len(group) == 1:
        return [0, 1 << group[0]]
    hi, lo = 1 << group[0], 1 << group[1]
    return [0, lo, hi, hi | lo]


def gathered(out, axis, groups, size, after=None):
    for group in groups:
        pieces = [out] + [swap(out, axis, m) for m in masks_of(group)[1:]]
        if after is not None:
            *pieces, after = lax.optimization_barrier((*pieces, after))
        out = jnp.moveaxis(in_order(pieces, axis, group), 0, 1)
        out = out.reshape(-1, *size)
    return out


def chosen(full, axis, group):
    r = 1 << len(group)
    out = full.reshape(full.shape[0], -1, r, *full.shape[2:])
    mine = (lax.axis_index(axis) >> group[-1]) & (r - 1)
    return [lax.dynamic_index_in_dim(out, mine ^ (m >> group[-1]), 2, keepdims=False) for m in masks_of(group)]


def received(parts, axis, group):
    keep, *send = parts
    return [keep] + [swap(part, axis, m) for m, part in zip(masks_of(group)[1:], send)]


def total_of(parts):
    total = parts[0].astype(F32)
    for part in parts[1:]:
        total = total + part.astype(F32)
    return total


def sum_scatter(full, axis, groups):
    *rest, last = reversed(groups)
    out = full
    for group in rest:
        out = total_of(received(chosen(out, axis, group), axis, group)).astype(BF16)
    return received(chosen(out, axis, last), axis, last)


def sum_everywhere(x, axis, groups):
    for group in groups:
        x = total_of([x] + [swap(x, axis, m) for m in masks_of(group)[1:]])
    return x


def quarters(own):
    far = swap(own, "head", 2)
    return own, far, swap(own, "head", 1), swap(far, "head", 1)


PAIR = 2 * DH
KV = 3 * PAIR
KEY_LANES = ((0, PAIR), (0, PAIR), (2 * PAIR, KV))
VALUE_LANES = ((PAIR, 2 * PAIR), (PAIR, 2 * PAIR), (2 * PAIR, KV))
KEY_ROWS = (0, DH, 2 * PAIR)
VALUE_ROWS = (PAIR, PAIR + DH, 2 * PAIR + DH)


def arranged(q, k, v):
    return jnp.concatenate([k[..., :PAIR], v[..., :PAIR], k[..., PAIR:], v[..., PAIR:], q], axis=-1)


def separated(x):
    k = jnp.concatenate([x[..., :PAIR], x[..., 2 * PAIR : 2 * PAIR + DH]], axis=-1)
    v = jnp.concatenate([x[..., PAIR : 2 * PAIR], x[..., 2 * PAIR + DH : KV]], axis=-1)
    return x[..., KV:], k, v


def pack_kernel(up_ref, out_ref, down_ref, packed_ref, down_t_ref):
    shard, units = up_ref.shape
    out_t = out_ref[...].astype(F32).T
    few = packed_ref.shape[0] - shard
    packed_ref[0:shard, :] = up_ref[...]
    out_t = jnp.concatenate([out_t[n : n + few] for n in range(0, shard, few)], axis=1)
    packed_ref[shard:, :] = out_t.astype(BF16)
    down_t_ref[...] = down_ref[...].astype(F32).T.astype(BF16)


def pack(w_up, w_out, w_down):
    shard, units = w_up.shape
    part = w_out.shape[0]
    return pl.pallas_call(
        pack_kernel,
        out_shape=(
            jax.ShapeDtypeStruct((shard + shard * part // units, units), BF16),
            jax.ShapeDtypeStruct((shard, units), BF16),
        ),
        in_specs=[whole()] * 3,
        out_specs=(whole(), whole()),
        compiler_params=params(),
        cost_estimate=COST,
        name="pack",
    )(w_up, w_out, w_down)


def unit_times_gain(x, gain):
    return x * lax.rsqrt(jnp.mean(x * x, axis=-1, keepdims=True) + EPS) * gain


def mix_rows(buf_ref, mix_ref, taps, starts, base, rows):
    mix_ref[...] = (
        taps[0:1] * buf_ref[8 : 8 + rows, :]
        + taps[1:2] * buf_ref[7 : 7 + rows, :]
        + taps[2:3] * buf_ref[6 : 6 + rows, :]
    )
    for start in starts:
        r = start - base

        @pl.when((r >= 0) & (r < rows))
        def _(r=r):
            mix_ref[pl.ds(r, 1), :] = taps[0:1] * buf_ref[pl.ds(8 + r, 1), :]

        @pl.when((r + 1 >= 0) & (r + 1 < rows))
        def _(r=r):
            mix_ref[pl.ds(r + 1, 1), :] = (
                taps[0:1] * buf_ref[pl.ds(9 + r, 1), :] + taps[1:2] * buf_ref[pl.ds(8 + r, 1), :]
            )


def project_own_kernel(
    meta_ref, x_ref, halo_ref, gain_ref, w_in_ref, taps_ref,
    w_ref, raw_halo_ref, raw_ref, normed_ref, q_ref, kv_ref, kvt_ref, buf_ref, mix_ref, *, base,
):
    i = pl.program_id(0)
    rows = x_ref.shape[0]
    gain = gain_ref[...]

    @pl.when(i == 0)
    def _():
        w_in = w_in_ref[...]
        part = w_in.shape[1] // 3
        w_ref[...] = arranged(w_in[:, :part], w_in[:, part : 2 * part], w_in[:, 2 * part : 3 * part])

    w = w_ref[...]

    @pl.when(i == 0)
    def _():
        halo = jnp.where(meta_ref[HAS_ONE] == 1, halo_ref[...].astype(F32), 0.0)
        normed = unit_times_gain(halo, gain).astype(BF16)
        raw_low = mm(normed, w).astype(BF16)
        raw_halo_ref[...] = raw_low[:, KV:]
        buf_ref[0:8, :] = raw_low.astype(F32)[HALO - 8 :, :]

    normed = unit_times_gain(x_ref[...].astype(F32), gain).astype(BF16)
    raw_low = mm(normed, w).astype(BF16)
    normed_ref[...] = normed
    raw_ref[...] = raw_low
    raw = raw_low.astype(F32)
    buf_ref[8 : 8 + rows, :] = raw
    mix_rows(buf_ref, mix_ref, taps_ref[...], [meta_ref[STARTS + n] for n in range(8)], base + i * rows, rows)
    buf_ref[0:8, :] = raw[rows - 8 :, :]
    q_ref[...] = mix_ref[:, KV:].astype(BF16)
    kv = mix_ref[:, :KV]
    kv_ref[...] = kv.astype(BF16)
    kvt_ref[...] = kv.T.astype(BF16)


def project_own(meta, tokens, halo, gain, w, taps):
    rows, dim = tokens.shape
    width = w.shape[1]
    step = 2 * TILE
    tile = lambda n: pl.BlockSpec((step, n), lambda i, *_: (i, 0))
    return pl.pallas_call(
        functools.partial(project_own_kernel, base=REACH * rows),
        out_shape=(
            jax.ShapeDtypeStruct((dim, width), BF16),
            jax.ShapeDtypeStruct((HALO, width - KV), BF16),
            jax.ShapeDtypeStruct((rows, width), BF16),
            jax.ShapeDtypeStruct((rows, dim), BF16),
            jax.ShapeDtypeStruct((rows, width - KV), BF16),
            jax.ShapeDtypeStruct((rows, KV), BF16),
            jax.ShapeDtypeStruct((KV, rows), BF16),
        ),
        grid_spec=pltpu.PrefetchScalarGridSpec(
            num_scalar_prefetch=1,
            grid=(rows // step,),
            in_specs=[tile(dim), whole(), whole(), whole(), whole()],
            out_specs=(
                whole(),
                whole(),
                tile(width),
                tile(dim),
                tile(width - KV),
                tile(KV),
                pl.BlockSpec((KV, step), lambda i, *_: (0, i)),
            ),
            scratch_shapes=[pltpu.VMEM((8 + step, width), F32), pltpu.VMEM((step, width), F32)],
        ),
        compiler_params=params(),
        cost_estimate=COST,
        name="project_own",
    )(meta, tokens, halo, gain, w, taps)


def project_earlier_kernel(meta_ref, *refs):
    pieces = refs[:8]
    gain_ref, w_ref, taps_ref, raw_ref, normed_ref, kv_ref, kvt_ref, x_ref, buf_ref, mix_ref = refs[8:]
    i = pl.program_id(0)
    rows = x_ref.shape[0]
    quarter = pieces[0].shape[0]

    @pl.when(i == 0)
    def _():
        buf_ref[0:8, :] = jnp.zeros((8, KV), F32)

    for hop in range(REACH):
        for slot, d in enumerate((0, 2, 1, 3)):
            place = 4 * hop + (meta_ref[0] ^ d)

            @pl.when(i == place >> 1)
            def _(piece=pieces[4 * hop + slot], place=place):
                x_ref[pl.ds(pl.multiple_of((place & 1) * quarter, quarter), quarter), :] = piece[...]

    exists = jnp.where(i < pl.num_programs(0) // REACH, meta_ref[HAS_TWO], meta_ref[HAS_ONE])
    x = jnp.where(exists == 1, x_ref[...].astype(F32), 0.0)
    normed = unit_times_gain(x, gain_ref[...]).astype(BF16)
    normed_ref[...] = normed
    raw_low = mm(normed, w_ref[:, :KV]).astype(BF16)
    raw_ref[...] = raw_low
    raw = raw_low.astype(F32)
    buf_ref[8 : 8 + rows, :] = raw
    mix_rows(buf_ref, mix_ref, taps_ref[:, :KV], [meta_ref[STARTS + n] for n in range(8)], i * rows, rows)
    buf_ref[0:8, :] = raw[rows - 8 :, :]
    kv = mix_ref[...]
    kv_ref[...] = kv.astype(BF16)
    kvt_ref[...] = kv.T.astype(BF16)


def project_earlier(meta, pieces, gain, w, taps):
    quarter, dim = pieces[0].shape
    step = 2 * quarter
    span = len(pieces) * quarter
    tile = lambda n: pl.BlockSpec((step, n), lambda i, *_: (i, 0))
    return pl.pallas_call(
        project_earlier_kernel,
        out_shape=(
            jax.ShapeDtypeStruct((span, KV), BF16),
            jax.ShapeDtypeStruct((span, dim), BF16),
            jax.ShapeDtypeStruct((span, KV), BF16),
            jax.ShapeDtypeStruct((KV, span), BF16),
        ),
        grid_spec=pltpu.PrefetchScalarGridSpec(
            num_scalar_prefetch=1,
            grid=(span // step,),
            in_specs=[whole()] * 11,
            out_specs=(tile(KV), tile(dim), tile(KV), pl.BlockSpec((KV, step), lambda i, *_: (0, i))),
            scratch_shapes=[
                pltpu.VMEM((step, dim), BF16),
                pltpu.VMEM((8 + step, KV), F32),
                pltpu.VMEM((step, KV), F32),
            ],
        ),
        compiler_params=params(),
        cost_estimate=COST,
        name="project_earlier",
    )(meta, *pieces, gain, w, taps)


LOW, FULL, STARTS = 1, 5, 9
HAS_ONE, HAS_TWO, NEXT_ONE, NEXT_TWO = 17, 18, 19, 20


STEP = 2 * TILE


def masked_scores(scores, key_base, query_base, first, diagonal):
    keys = lax.broadcasted_iota(jnp.int32, scores.shape, 0)
    allowed = keys >= first - key_base
    if diagonal is not None:
        allowed = allowed & (keys <= lax.broadcasted_iota(jnp.int32, scores.shape, 1) + (query_base - diagonal))
    return jnp.where(allowed, scores, MASKED)


def place_heads(to_ref, lanes, across, halves):
    zero = jnp.zeros((DH, across.shape[1]), to_ref.dtype)
    for h, half in enumerate(halves):
        to_ref[h, half * DH : (half + 1) * DH, lanes] = across[h * DH : (h + 1) * DH].astype(to_ref.dtype)
        to_ref[h, (1 - half) * DH : (2 - half) * DH, lanes] = zero


KEY_HALVES, VALUE_HALVES = (0, 1, 0), (0, 1, 1)


def eights(x, how):
    return how(x.reshape(x.shape[0] // 8, 8, x.shape[1]), axis=0)


def query_tiles(rows):
    return [slice(n, n + TILE) for n in range(0, rows, TILE)]


def staged(items, first, second, depth=2):
    waiting = []
    for item in items:
        waiting.append((item, first(item)))
        if len(waiting) > depth:
            second(*waiting.pop(0))
    for pair in waiting:
        second(*pair)


def attend_tiles(steps, q_ref, kv_ref, kvt_ref, first_ref, acc_ref, q_across_ref, top_ref, sum_ref):
    for lanes in query_tiles(q_ref.shape[0]):
        place_heads(q_across_ref, lanes, (q_ref[lanes, :].astype(F32) * (DH**-0.5)).T, KEY_HALVES)
    acc_ref[...] = jnp.zeros_like(acc_ref)
    top_ref[...] = jnp.full(top_ref.shape, MASKED, F32)
    sum_ref[...] = jnp.zeros_like(sum_ref)

    def run(row, keys, window_row, begin, masked, diagonal):
        at = pl.ds(row, keys)
        items = [(h, lanes) for h in range(3) for lanes in query_tiles(q_ref.shape[0])[begin // TILE :]]
        key_rows = [kv_ref[at, KEY_LANES[h][0] : KEY_LANES[h][1]] for h in range(3)]
        values = [kvt_ref[VALUE_ROWS[h] : VALUE_ROWS[h] + DH, at] for h in range(3)]
        queries = [q_across_ref[h, :, lanes] for h, lanes in items]
        tops = [top_ref[h : h + 1, lanes] for h, lanes in items]
        firsts = {lanes.start: first_ref[:, lanes] for _, lanes in items}
        results = []

        def first(n):
            h, lanes = items[n]
            scores = mm(key_rows[h], queries[n])
            if masked:
                scores = masked_scores(scores, window_row, lanes.start, firsts[lanes.start], diagonal)
            return scores

        def second(n, scores):
            h, lanes = items[n]
            top = jnp.maximum(tops[n], jnp.max(eights(scores, jnp.max), axis=0, keepdims=True))
            weights = jnp.exp(scores - top)
            total = jnp.sum(eights(weights, jnp.sum), axis=0, keepdims=True)
            results.append((top, total, mm(values[h], weights.astype(BF16))))

        staged(range(len(items)), first, second)
        for n, (h, lanes) in enumerate(items):
            top, total, out = results[n]
            fade = jnp.exp(tops[n] - top)
            top_ref[h : h + 1, lanes] = top
            sum_ref[h : h + 1, lanes] = sum_ref[h : h + 1, lanes] * fade + total
            rows = slice(h * DH, (h + 1) * DH)
            acc_ref[rows, lanes] = acc_ref[rows, lanes] * fade + out

    steps(run)


def earlier_steps(meta_ref, before, rows):
    last = rows // TILE - 1
    end = before // STEP
    low = meta_ref[LOW] // (STEP // TILE)
    full = (meta_ref[FULL + last] + STEP // TILE - 1) // (STEP // TILE)
    middle = jnp.clip(full, low, jnp.maximum(end, low))

    def steps(run):
        def one(masked):
            def step(n, carry):
                row = pl.multiple_of(n * STEP, STEP)
                run(row, STEP, row, 0, masked, None)
                return carry

            return step

        lax.fori_loop(low, middle, one(True), 0)
        lax.fori_loop(middle, end, one(False), 0)

    return steps


def attend_own_kernel(q_ref, kv_ref, kvt_ref, first_ref, acc_ref, stat_ref, q_across_ref, *, base):
    rows = q_ref.shape[0]

    def steps(run):
        for row in range(0, rows, STEP):
            run(row, STEP, base + row, row, True, row)

    top_ref, sum_ref = stat_ref.at[0:8], stat_ref.at[8:16]
    attend_tiles(steps, q_ref, kv_ref, kvt_ref, first_ref, acc_ref, q_across_ref, top_ref, sum_ref)


def attend_earlier_kernel(
    meta_ref, q_ref, kv_ref, kvt_ref, first_ref, acc_own_ref, stat_own_ref,
    att_ref, ot_ref, lse_ref, q_across_ref, top_ref, sum_ref,
):
    rows = q_ref.shape[0]
    steps = earlier_steps(meta_ref, kv_ref.shape[0], rows)
    attend_tiles(steps, q_ref, kv_ref, kvt_ref, first_ref, ot_ref, q_across_ref, top_ref, sum_ref)
    for h in range(3):
        to = slice(h * DH, (h + 1) * DH)
        top_here, top_own = top_ref[h : h + 1, :], stat_own_ref[h : h + 1, :]
        top = jnp.maximum(top_here, top_own)
        here, own = jnp.exp(top_here - top), jnp.exp(top_own - top)
        total = here * sum_ref[h : h + 1, :] + own * stat_own_ref[8 + h : 9 + h, :]
        out = ot_ref[to, :] * (here / total) + acc_own_ref[to, :] * (own / total)
        ot_ref[to, :] = out
        lse_ref[h : h + 1, :] = top + jnp.log(total)
        for n, lanes in enumerate(query_tiles(rows)):
            att_ref[slot_of(n, meta_ref), to, :] = out[:, lanes].astype(BF16)


def slot_of(i, meta):
    d = i ^ meta[0]
    return (d >> 1) | ((d & 1) << 1)


def attend_own(q, kv, kvt, first_row):
    rows, part = q.shape
    return pl.pallas_call(
        functools.partial(attend_own_kernel, base=REACH * rows),
        out_shape=(jax.ShapeDtypeStruct((part, rows), F32), jax.ShapeDtypeStruct((16, rows), F32)),
        in_specs=[whole()] * 4,
        out_specs=(whole(), whole()),
        scratch_shapes=[pltpu.VMEM((3, PAIR, rows), BF16)],
        compiler_params=params(),
        cost_estimate=COST,
        name="attend_own",
    )(q, kv, kvt, first_row)


def attend_earlier(meta, q, kv, kvt, first_row, acc_own, stat_own):
    rows, part = q.shape
    return pl.pallas_call(
        attend_earlier_kernel,
        out_shape=(
            jax.ShapeDtypeStruct((rows // TILE, part, TILE), BF16),
            jax.ShapeDtypeStruct((part, rows), F32),
            jax.ShapeDtypeStruct((8, rows), F32),
        ),
        in_specs=[pl.BlockSpec(memory_space=pltpu.SMEM)] + [whole()] * 6,
        out_specs=(whole(), whole(), whole()),
        scratch_shapes=[
            pltpu.VMEM((3, PAIR, rows), BF16),
            pltpu.VMEM((8, rows), F32),
            pltpu.VMEM((8, rows), F32),
        ],
        compiler_params=params(),
        cost_estimate=COST,
        name="attend_earlier",
    )(meta, q, kv, kvt, first_row, acc_own, stat_own)


def back_scratch(rows):
    return [
        pltpu.VMEM((3, PAIR, rows), BF16),
        pltpu.VMEM((3, PAIR, rows), BF16),
        pltpu.VMEM((3, rows, PAIR), BF16),
        pltpu.VMEM((3, rows, PAIR), BF16),
        pltpu.VMEM((8, rows), F32),
        pltpu.VMEM((3, STEP, rows), BF16),
        pltpu.VMEM((3, STEP, rows), BF16),
    ]


def back_prepare(meta_ref, q_ref, dt_ref, ot_ref, scratch):
    q_across_ref, d_across_ref, q_alone_ref, d_alone_ref, delta_ref = scratch[:5]
    lane = lax.broadcasted_iota(jnp.int32, (TILE, PAIR), 1)
    none = jnp.zeros((TILE, PAIR), BF16)

    def alone(to_ref, rows, x, halves):
        last = jnp.concatenate([x[:, PAIR:]] * 2, axis=1)
        for h, half in enumerate(halves):
            to_ref[h, rows, :] = jnp.where((lane < DH) == (half == 0), x[:, :PAIR] if h < 2 else last, none)

    for n, rows in enumerate(query_tiles(q_ref.shape[0])):
        scaled = q_ref[rows, :].astype(F32) * (DH**-0.5)
        place_heads(q_across_ref, rows, scaled.T, KEY_HALVES)
        alone(q_alone_ref, rows, scaled.astype(BF16), KEY_HALVES)
        d_wide = dt_ref[slot_of(n, meta_ref)].astype(F32)
        place_heads(d_across_ref, rows, d_wide, VALUE_HALVES)
        alone(d_alone_ref, rows, d_wide.T.astype(BF16), VALUE_HALVES)
        terms = d_wide * ot_ref[:, rows]
        for h in range(3):
            delta_ref[h : h + 1, rows] = jnp.sum(terms[h * DH : (h + 1) * DH], axis=0, keepdims=True)


def back_step(row, keys, window_row, begin, masked, diagonal, kv_ref, kvt_ref, lse_ref, first_ref, grad_ref, lead, dq_ref, scratch):
    q_across_ref, d_across_ref, q_alone_ref, d_alone_ref, delta_ref, p_ref, ds_ref = scratch
    rows = dq_ref.shape[1]
    at = pl.ds(row, keys)
    items = [(h, lanes) for h in range(3) for lanes in query_tiles(rows)[begin // TILE :]]
    key_rows = [kv_ref[at, KEY_LANES[h][0] : KEY_LANES[h][1]] for h in range(3)]
    value_rows = [kv_ref[at, VALUE_LANES[h][0] : VALUE_LANES[h][1]] for h in range(3)]
    keys_t = [kvt_ref[KEY_ROWS[h] : KEY_ROWS[h] + DH, at] for h in range(3)]
    queries = [q_across_ref[h, :, lanes] for h, lanes in items]
    d_outs = [d_across_ref[h, :, lanes] for h, lanes in items]
    lses = [lse_ref[h : h + 1, lanes] for h, lanes in items]
    deltas = [delta_ref[h : h + 1, lanes] for h, lanes in items]
    firsts = {lanes.start: first_ref[:, lanes] for _, lanes in items}
    results = []

    def first(n):
        h, lanes = items[n]
        scores = mm(key_rows[h], queries[n])
        if masked:
            scores = masked_scores(scores, window_row, lanes.start, firsts[lanes.start], diagonal)
        return scores, mm(value_rows[h], d_outs[n])

    def second(n, both):
        h, lanes = items[n]
        scores, d_probs = both
        probs = jnp.exp(scores - lses[n])
        d_scores = (probs * (d_probs - deltas[n])).astype(BF16)
        p_ref[h, :keys, lanes] = probs.astype(BF16)
        ds_ref[h, :keys, lanes] = d_scores
        results.append(mm(keys_t[h], d_scores))

    staged(range(len(items)), first, second, 1)
    for n, (h, lanes) in enumerate(items):
        dq_ref[h * DH : (h + 1) * DH, lanes] += results[n]
    seen = slice(begin, rows)
    to = pl.ds(pl.multiple_of(lead + row, 8), keys)
    terms = (
        ((ds_ref, q_alone_ref, 0), (ds_ref, q_alone_ref, 1)),
        ((p_ref, d_alone_ref, 0), (p_ref, d_alone_ref, 1)),
        ((ds_ref, q_alone_ref, 2), (p_ref, d_alone_ref, 2)),
    )
    for n, ((left_a, right_a, a), (left_b, right_b, b)) in enumerate(terms):
        lanes = slice(n * PAIR, (n + 1) * PAIR)
        grad_ref[to, lanes] += mm(left_a[a, :keys, seen], right_a[a, seen, :]) + mm(
            left_b[b, :keys, seen], right_b[b, seen, :]
        )


def unmix_rows(grad_ref, raw_ref, fix_ref, taps, starts, rows, sums_ref):
    width = grad_ref.shape[1]

    def raw_row(r):
        group = raw_ref[pl.ds(pl.multiple_of((r // HALO) * HALO, HALO), HALO), :].astype(F32)
        row = lax.broadcasted_iota(jnp.int32, group.shape, 0)
        return jnp.sum(jnp.where(row == r % HALO, group, 0.0), axis=0, keepdims=True)

    sums_ref[...] = jnp.zeros_like(sums_ref)
    inside = [(s >= 1) & (s <= rows + 1) for s in starts]
    for n, s in enumerate(starts):

        @pl.when(inside[n])
        def _(n=n, s=s):
            one_before = grad_ref[pl.ds(7 + s, 1), :]
            fix_ref[2 * n : 2 * n + 1, :] = taps[0:1] * one_before
            fix_ref[2 * n + 1 : 2 * n + 2, :] = taps[0:1] * grad_ref[pl.ds(6 + s, 1), :] + taps[1:2] * one_before
            here = grad_ref[pl.ds(8 + s, 1), :]

            @pl.when(s >= 2)
            def _():
                sums_ref[2:3, :] -= raw_row(jnp.maximum(s - 2, 0)) * here

            @pl.when(s <= rows)
            def _():
                raw_one = raw_row(s - 1)
                sums_ref[1:2, :] -= raw_one * here
                following = starts[n + 1] if n + 1 < len(starts) else s + 2

                @pl.when(following != s + 1)
                def _():
                    sums_ref[2:3, :] -= raw_one * grad_ref[pl.ds(9 + s, 1), :]

    sizes = [HALO] * (1 if rows % TILE else 0) + [TILE] * (rows // TILE)
    lo = 0
    totals = [jnp.zeros((8, width), F32) for _ in range(3)]
    for size in sizes:
        now = grad_ref[8 + lo : 8 + lo + size, :]
        one = grad_ref[9 + lo : 9 + lo + size, :]
        two = grad_ref[10 + lo : 10 + lo + size, :]
        raw = raw_ref[lo : lo + size, :].astype(F32)
        for j, shifted in enumerate((now, one, two)):
            totals[j] = totals[j] + eights(raw * shifted, jnp.sum)
        grad_ref[8 + lo : 8 + lo + size, :] = taps[0:1] * now + taps[1:2] * one + taps[2:3] * two
        lo += size
    for j in range(3):
        sums_ref[j : j + 1, :] += jnp.sum(totals[j], axis=0, keepdims=True)
    for n in reversed(range(len(starts))):

        @pl.when(inside[n])
        def _(n=n, s=starts[n]):
            grad_ref[pl.ds(7 + s, 1), :] = fix_ref[2 * n : 2 * n + 1, :]
            grad_ref[pl.ds(6 + s, 1), :] = fix_ref[2 * n + 1 : 2 * n + 2, :]


def earlier_back_kernel(
    meta_ref, q_ref, dt_ref, ot_ref, lse_ref, first_ref, kv_ref, kvt_ref, kv_own_ref, kvt_own_ref, raw_ref,
    raw_halo_ref, taps_ref, dq_ref, two_ref, one_ref, next_ref, sums_ref, sums_q_ref,
    grad_ref, grad_q_ref, fix_ref, fix_q_ref, *scratch,
):
    before = kv_ref.shape[0]
    rows = q_ref.shape[0]
    grad_ref[...] = jnp.zeros_like(grad_ref)
    grad_q_ref[...] = jnp.zeros_like(grad_q_ref)
    dq_ref[...] = jnp.zeros_like(dq_ref)
    back_prepare(meta_ref, q_ref, dt_ref, ot_ref, scratch)
    run = lambda *step: back_step(*step, kv_ref, kvt_ref, lse_ref, first_ref, grad_ref, 8, dq_ref, scratch)
    earlier_steps(meta_ref, before, rows)(run)
    back_step(
        0, TILE, before, 0, True, 0, kv_own_ref, kvt_own_ref, lse_ref, first_ref, grad_ref, 8 + before, dq_ref, scratch
    )
    grad_q_ref[8 + HALO : 16 + HALO, :] = dq_ref[:, :PAIR].T[:8] * (DH**-0.5)
    starts = [meta_ref[STARTS + n] for n in range(8)]
    next_ref[...] = grad_ref[8 + before : 8 + before + TILE, :]
    unmix_rows(grad_ref, raw_ref, fix_ref, taps_ref[:, :KV], starts, before, sums_ref)
    starts = [s - (before - HALO) for s in starts]
    unmix_rows(grad_q_ref, raw_halo_ref, fix_q_ref, taps_ref[:, KV:], starts, HALO, sums_q_ref)
    half = before // 2
    two_ref[...] = grad_ref[8 : 8 + half, :].astype(BF16)
    one_ref[0:half, :] = grad_ref[8 + half : 8 + before, :].astype(BF16)
    queries = grad_q_ref[8 : 8 + HALO, :]
    one_ref[half : half + HALO, :] = jnp.concatenate([queries, jnp.zeros_like(queries)], axis=1).astype(BF16)


def earlier_back(meta, q, d_out_t, out_t, lse, first_row, kv, kvt, kv_own, kvt_own, raw, raw_halo, taps):
    rows, part = q.shape
    before = kv.shape[0]
    return pl.pallas_call(
        earlier_back_kernel,
        out_shape=(
            jax.ShapeDtypeStruct((part, rows), F32),
            jax.ShapeDtypeStruct((rows, KV), BF16),
            jax.ShapeDtypeStruct((rows + HALO, KV), BF16),
            jax.ShapeDtypeStruct((TILE, KV), F32),
            jax.ShapeDtypeStruct((8, KV), F32),
            jax.ShapeDtypeStruct((8, part), F32),
        ),
        grid=(1,),
        in_specs=[pl.BlockSpec(memory_space=pltpu.SMEM)]
        + [whole()] * 7
        + [
            pl.BlockSpec((TILE, KV), lambda i: (0, 0)),
            pl.BlockSpec((KV, TILE), lambda i: (0, 0)),
            whole(),
            whole(),
            whole(),
        ],
        out_specs=tuple([whole()] * 6),
        scratch_shapes=[
            pltpu.VMEM((8 + before + TILE + 8, KV), F32),
            pltpu.VMEM((8 + HALO + 8, part), F32),
            pltpu.VMEM((16, KV), F32),
            pltpu.VMEM((16, part), F32),
            *back_scratch(rows),
        ],
        compiler_params=params(34),
        cost_estimate=COST,
        name="earlier_back",
    )(meta, q, d_out_t, out_t, lse, first_row, kv, kvt, kv_own, kvt_own, raw, raw_halo, taps)


def own_back_kernel(
    meta_ref, q_ref, dt_ref, ot_ref, lse_ref, first_ref, dq_in_ref, kv_ref, kvt_ref, raw_ref, taps_ref, next_ref,
    normed_e_ref, two_ref, one_ref, normed_ref, out_keep_ref, out_near_ref, out_far_ref,
    d_raw_ref, sums_ref, mix_ref, dq_ref, grad_ref, fix_ref, *scratch,
):
    rows = kv_ref.shape[0]
    base = REACH * rows
    grad_ref[...] = jnp.zeros_like(grad_ref)
    grad_ref[8 : 8 + TILE, :KV] = next_ref[...]
    dq_ref[...] = dq_in_ref[...]
    back_prepare(meta_ref, q_ref, dt_ref, ot_ref, scratch)
    row = TILE
    while row < rows:
        keys = TILE if row % STEP else STEP
        back_step(
            row, keys, base + row, row, True, row, kv_ref, kvt_ref, lse_ref, first_ref, grad_ref, 8, dq_ref, scratch
        )
        row += keys
    for lanes in query_tiles(rows):
        grad_ref[8 + lanes.start : 8 + lanes.stop, KV:] = dq_ref[:, lanes].T * (DH**-0.5)
    starts = [meta_ref[STARTS + n] - base for n in range(8)]
    unmix_rows(grad_ref, raw_ref, fix_ref, taps_ref[...], starts, rows, sums_ref)
    d_raw_ref[...] = grad_ref[8 : 8 + rows, :].astype(BF16)
    part = out_keep_ref.shape[0]
    out_grad = out_keep_ref[...].astype(F32) + out_near_ref[0].astype(F32) + out_far_ref[...].astype(F32)
    for n in range(normed_ref.shape[1] // TILE):
        lanes = slice(n * TILE, (n + 1) * TILE)
        grad = mm(normed_ref[:, lanes], d_raw_ref[...], 0, 0)
        earlier = mm(normed_e_ref[:rows, lanes], two_ref[...], 0, 0)
        earlier = earlier + mm(normed_e_ref[rows:, lanes], one_ref[:rows, :], 0, 0)
        halo = mm(normed_e_ref[2 * rows - HALO :, lanes], one_ref[rows:, :], 0, 0)[:, :part]
        mix_ref[lanes, :KV] = (grad[:, :KV] + earlier).astype(BF16)
        rest = jnp.concatenate([grad[:, KV:] + halo, out_grad[:, lanes].T], axis=1)
        mix_ref[lanes, KV:] = rest.astype(BF16)


def own_back(
    meta, q, d_out_t, out_t, lse, first_row, dq_t, kv, kvt, raw, taps, grad_next, normed_e, two, one, normed, *grad_out
):
    rows, part = q.shape
    width = raw.shape[1]
    return pl.pallas_call(
        own_back_kernel,
        out_shape=(
            jax.ShapeDtypeStruct((rows, width), BF16),
            jax.ShapeDtypeStruct((8, width), F32),
            jax.ShapeDtypeStruct((normed.shape[1], width + part), BF16),
        ),
        in_specs=[pl.BlockSpec(memory_space=pltpu.SMEM)] + [whole()] * 18,
        out_specs=(whole(), whole(), whole()),
        scratch_shapes=[
            pltpu.VMEM((part, rows), F32),
            pltpu.VMEM((8 + rows + 8, width), F32),
            pltpu.VMEM((16, width), F32),
            *back_scratch(rows),
        ],
        compiler_params=params(34),
        cost_estimate=COST,
        name="own_back",
    )(
        meta, q, d_out_t, out_t, lse, first_row, dq_t, kv, kvt, raw, taps, grad_next,
        normed_e, two, one, normed, *grad_out,
    )


def after_attend_kernel(a0, a1, a2, a3, w0, w1, w2, w3, x_ref, gain_ref, hidden_ref, normed_ref):
    branch = mm(a0[...], w0[...], 0, 0)
    for a, w in ((a1, w1), (a2, w2), (a3, w3)):
        branch = branch + mm(a[...], w[...], 0, 0)
    hidden = x_ref[...].astype(F32) + branch
    hidden_ref[...] = hidden
    factor = lax.rsqrt(jnp.mean(hidden * hidden, axis=-1, keepdims=True) + EPS)
    normed_ref[...] = (hidden * factor * gain_ref[...]).astype(BF16)


def after_attend(attended, w_out, x, gain):
    rows, dim = x.shape
    return pl.pallas_call(
        after_attend_kernel,
        out_shape=(jax.ShapeDtypeStruct((rows, dim), F32), jax.ShapeDtypeStruct((rows, dim), BF16)),
        in_specs=[whole()] * 10,
        out_specs=(whole(), whole()),
        compiler_params=params(),
        cost_estimate=COST,
        name="after_attend",
    )(*attended, *w_out, x, gain)


def feed_kernel(x0, x2, x1, x3, cot_ref, up_ref, down_ref, x_ref, act_ref, d_up_ref, keep_ref, send_ref):
    def half(first, second, back_ref):
        x = jnp.concatenate([first[...], second[...]], axis=0)
        x_ref[...] = x
        up = mm(x, up_ref[...])
        pos = jnp.maximum(up, 0.0)
        act_ref[...] = (pos * pos).astype(BF16)
        d_act = mm(cot_ref[...], down_ref[...])
        d_up = (d_act * 2.0 * pos).astype(BF16)
        d_up_ref[...] = d_up
        back_ref[...] = mm(d_up, up_ref[...], 1, 1).astype(BF16)

    @pl.when(pl.program_id(0) == 0)
    def _():
        half(x0, x2, keep_ref)

    @pl.when(pl.program_id(0) == 1)
    def _():
        half(x1, x3, send_ref)


def feed(x, cot, w_up, w_down_t):
    rows, dim = cot.shape
    units = w_up.shape[1]
    step = rows // 2
    tile = lambda n: pl.BlockSpec((step, n), lambda i: (i, 0))
    return pl.pallas_call(
        feed_kernel,
        out_shape=(
            jax.ShapeDtypeStruct((rows, dim), BF16),
            jax.ShapeDtypeStruct((rows, units), BF16),
            jax.ShapeDtypeStruct((rows, units), BF16),
            jax.ShapeDtypeStruct((step, dim), BF16),
            jax.ShapeDtypeStruct((step, dim), BF16),
        ),
        grid=(2,),
        in_specs=[whole()] * 4 + [tile(dim), whole(), whole()],
        out_specs=(tile(dim), tile(units), tile(units), whole(), whole()),
        compiler_params=params(),
        cost_estimate=COST,
        name="feed",
    )(*x, cot, w_up, w_down_t)


def feed_rest_kernel(x_ref, d_up_ref, cot_ref, act_ref, down_ref, grads_ref, keep_ref, send_ref):
    grads_ref[0] = mm(x_ref[...], d_up_ref[...], 0, 0).astype(BF16)
    grads_ref[1] = mm(cot_ref[...], act_ref[...], 0, 0).astype(BF16)
    out = mm(act_ref[...], down_ref[...], 1, 1).astype(BF16)
    half = out.shape[0] // 2
    keep_ref[...] = out[:half]
    send_ref[...] = out[half:]


def feed_rest(x, d_up, cot, act, w_down_t):
    rows, dim = x.shape
    units = act.shape[1]
    block = pl.BlockSpec((rows, TILE), lambda i: (0, i))
    half = pl.BlockSpec((rows // 2, TILE), lambda i: (0, i))
    return pl.pallas_call(
        feed_rest_kernel,
        out_shape=(
            jax.ShapeDtypeStruct((2, dim, units), BF16),
            jax.ShapeDtypeStruct((rows // 2, dim), BF16),
            jax.ShapeDtypeStruct((rows // 2, dim), BF16),
        ),
        grid=(dim // TILE,),
        in_specs=[block, whole(), block, whole(), pl.BlockSpec((TILE, units), lambda i: (i, 0))],
        out_specs=(pl.BlockSpec((2, TILE, units), lambda i: (0, i, 0)), half, half),
        compiler_params=params(),
        cost_estimate=COST,
        name="feed_rest",
    )(x, d_up, cot, act, w_down_t)


def before_back_kernel(
    s_ref, r_ref, hidden_ref, gain_ref, cot_ref, w0, w1, w2, w3, a0, a1, a2, a3,
    d_hidden_ref, d0, d1, d2, d3, keep_ref, keep_far_ref, send_ref, sum_ref,
):
    d_normed = s_ref[...].astype(F32) + r_ref[...].astype(F32)
    hidden = hidden_ref[...]
    factor = lax.rsqrt(jnp.mean(hidden * hidden, axis=-1, keepdims=True) + EPS)
    unit = hidden * factor
    sum_ref[...] = jnp.sum(d_normed * unit, axis=0, keepdims=True)
    scaled = d_normed * gain_ref[...]
    inner = jnp.mean(scaled * unit, axis=-1, keepdims=True)
    d_hidden = cot_ref[...].astype(F32) + factor * (scaled - unit * inner)
    d_hidden_ref[...] = d_hidden
    d_branch = d_hidden.astype(BF16)
    for w, d in ((w0, d0), (w1, d1), (w2, d2), (w3, d3)):
        d[...] = mm(w[...], d_branch, 1, 1).astype(BF16)
    for a, to in ((a0, keep_ref), (a1, keep_far_ref), (a2, send_ref.at[0]), (a3, send_ref.at[1])):
        to[...] = mm(a[...], d_branch).astype(BF16)


def before_back(chip_sum, far_sum, hidden, gain, cot, w_out, attended):
    rows, dim = hidden.shape
    part = w_out[0].shape[0]
    return pl.pallas_call(
        before_back_kernel,
        out_shape=(
            jax.ShapeDtypeStruct((rows, dim), F32),
            *[jax.ShapeDtypeStruct((part, rows), BF16)] * 4,
            *[jax.ShapeDtypeStruct((part, dim), BF16)] * 2,
            jax.ShapeDtypeStruct((2, part, dim), BF16),
            jax.ShapeDtypeStruct((1, dim), F32),
        ),
        in_specs=[whole()] * 13,
        out_specs=tuple([whole()] * 9),
        compiler_params=params(),
        cost_estimate=COST,
        name="before_back",
    )(chip_sum, far_sum, hidden, gain, cot, *w_out, *attended)


def d_normed_kernel(meta_ref, own_ref, one_ref, halo_ref, two_ref, x_ref, w_ref, keep_ref, send_ref, sum_ref):
    i = pl.program_id(0)
    step = own_ref.shape[0]
    later = jnp.where(meta_ref[NEXT_ONE] == 1, one_ref[...].astype(F32), 0.0)
    later = later + jnp.where(meta_ref[NEXT_TWO] == 1, two_ref[...].astype(F32), 0.0)
    own = own_ref[...].astype(F32)
    queries = own[:, KV:]
    part = queries.shape[1]
    last = (i == pl.num_programs(0) - 1) & (meta_ref[NEXT_ONE] == 1)
    halo = jnp.where(last, halo_ref[...].astype(F32)[:, :part], 0.0)
    queries = queries + jnp.concatenate([jnp.zeros((step - HALO, part), F32), halo], axis=0)
    d_raw = jnp.concatenate([own[:, :KV] + later, queries], axis=1).astype(BF16)
    d_normed = mm(d_raw, w_ref[...], 1, 1)
    for n in range(step // TILE):
        slot = slot_of(i * (step // TILE) + n, meta_ref)
        rows = d_normed[n * TILE : (n + 1) * TILE].astype(BF16)
        to = pl.ds(pl.multiple_of((slot & 1) * TILE, TILE), TILE)

        @pl.when(slot < 2)
        def _(rows=rows, to=to):
            keep_ref[to, :] = rows

        @pl.when(slot >= 2)
        def _(rows=rows, to=to):
            send_ref[to, :] = rows

    x = x_ref[...].astype(F32)
    unit = x * lax.rsqrt(jnp.mean(x * x, axis=-1, keepdims=True) + EPS)

    @pl.when(i == 0)
    def _():
        sum_ref[...] = jnp.zeros_like(sum_ref)

    sum_ref[...] += jnp.sum(d_normed * unit, axis=0, keepdims=True)


def d_normed_parts(meta, own, one, two, x, w):
    rows, dim = x.shape
    width = w.shape[1]
    step = 2 * TILE
    tile = lambda n: pl.BlockSpec((step, n), lambda i, *_: (i, 0))
    return pl.pallas_call(
        d_normed_kernel,
        out_shape=(
            jax.ShapeDtypeStruct((rows // 2, dim), BF16),
            jax.ShapeDtypeStruct((rows // 2, dim), BF16),
            jax.ShapeDtypeStruct((1, dim), F32),
        ),
        grid_spec=pltpu.PrefetchScalarGridSpec(
            num_scalar_prefetch=1,
            grid=(rows // step,),
            in_specs=[
                tile(width),
                tile(KV),
                pl.BlockSpec((HALO, KV), lambda i, *_: (rows // HALO, 0)),
                tile(KV),
                tile(dim),
                whole(),
            ],
            out_specs=(whole(), whole(), pl.BlockSpec((1, dim), lambda i, *_: (0, 0))),
        ),
        compiler_params=params(),
        cost_estimate=COST,
        name="d_normed_parts",
    )(meta, own, one, one, two, x, w)


def grad_tokens_kernel(s_ref, r_ref, x_ref, gain_ref, d_hidden_ref, out_ref):
    d_normed = s_ref[...].astype(F32) + r_ref[...].astype(F32)
    x = x_ref[...].astype(F32)
    factor = lax.rsqrt(jnp.mean(x * x, axis=-1, keepdims=True) + EPS)
    unit = x * factor
    scaled = d_normed * gain_ref[...]
    inner = jnp.mean(scaled * unit, axis=-1, keepdims=True)
    out_ref[...] = (d_hidden_ref[...] + factor * (scaled - unit * inner)).astype(BF16)


def grad_tokens_own(chip_sum, far_sum, x, gain, d_hidden):
    return pl.pallas_call(
        grad_tokens_kernel,
        out_shape=jax.ShapeDtypeStruct(x.shape, BF16),
        in_specs=[whole()] * 5,
        out_specs=whole(),
        compiler_params=params(),
        name="grad_tokens_own",
    )(chip_sum, far_sum, x, gain, d_hidden)


def assemble_kernel(meta_ref, *refs):
    *pieces, out_ref = refs
    for piece, d in zip(pieces, (0, 2, 1, 3)):

        @pl.when(pl.program_id(0) == (meta_ref[0] ^ d))
        def _(piece=piece):
            out_ref[...] = piece[...].astype(out_ref.dtype)


def by_place(meta, pieces, dtype):
    rows, dim = pieces[0].shape
    return pl.pallas_call(
        assemble_kernel,
        out_shape=jax.ShapeDtypeStruct((4 * rows, dim), dtype),
        grid_spec=pltpu.PrefetchScalarGridSpec(
            num_scalar_prefetch=1,
            grid=(4,),
            in_specs=[whole()] * 4,
            out_specs=pl.BlockSpec((rows, dim), lambda i, *_: (i, 0)),
        ),
        compiler_params=params(),
        cost_estimate=COST,
        name="assemble",
    )(meta, *pieces)


def sum_halves(keep, send):
    return (keep.astype(F32) + swap(send, "head", 1).astype(F32)).astype(BF16)


def body(
    tokens,
    seg_ids,
    gain_attn,
    w_query,
    w_key,
    w_value,
    conv_kernels,
    w_out,
    gain_ffn,
    w_up,
    w_down,
    cotangent,
):
    rows, dim = tokens.shape
    part = conv_kernels.shape[2]
    quarter = rows // lax.axis_size("head")
    blk = lax.axis_index("blk")
    head = lax.axis_index("head")
    groups = bit_groups("blk")
    together = lax.optimization_barrier
    own_quarter = lax.dynamic_slice_in_dim(tokens, head * quarter, quarter)
    two = moved(own_quarter, "blk", 2)
    shard, units = w_up.shape
    w_mix = jnp.concatenate([w_query, w_key, w_value], axis=1)
    packed, down_some = pack(w_up, w_out, w_down)
    w_some = gathered(w_mix[None], "blk", groups[:-1], w_mix.shape)
    one = swap(jnp.where(bit_of("blk", 0), two, own_quarter), "blk", 1)
    pieces = [*quarters(two), *quarters(one)]
    halo = moved(tokens[rows - HALO :], "blk", 1)
    w_mix = gathered(w_some, "blk", groups[-1:], w_mix.shape).reshape(dim, 3 * part)
    packed, _, _ = together((packed, w_some, two))
    span = (REACH + 1) * rows
    padded_ids = jnp.pad(seg_ids, (REACH * rows, 0), constant_values=-1)
    window = lax.dynamic_slice_in_dim(padded_ids, blk * rows, span)
    starts = jnp.sum((window[None, :] <= window[0] + jnp.arange(8)[:, None]).astype(jnp.int32), axis=1)
    place = jnp.arange(REACH * rows, span, dtype=jnp.int32)
    first_row = jnp.max(jnp.where(starts[:, None] <= place, starts[:, None], 0), axis=0)
    low = first_row[::TILE] // TILE
    full = (first_row[TILE - 1 :: TILE] + TILE - 1) // TILE
    last = lax.axis_size("blk") - 1
    exists = jnp.stack([blk >= 1, blk >= 2, blk + 1 <= last, blk + 2 <= last])
    meta = jnp.concatenate([head[None], low, full, starts, exists]).astype(jnp.int32)
    first_row = first_row[None]
    taps = arranged(*conv_kernels)
    gain_one, gain_two = gain_attn[None], gain_ffn[None]

    w_mix, *pieces[:2], pieces[4] = together((w_mix, *pieces[:2], pieces[4]))
    w_mix, raw_halo, raw, normed, q, kv, kvt = project_own(meta, tokens, halo, gain_one, w_mix, taps)
    packed_some = gathered(packed[None], "blk", groups[:-1], packed.shape, raw)
    down_some, _ = together((down_some, raw))
    q, pieces[5] = together((q, pieces[5]))
    acc_own, stat_own = attend_own(q, kv, kvt, first_row)
    wide = gathered(packed_some, "blk", groups[-1:], packed.shape, acc_own)
    down_some = gathered(down_some[None], "blk", groups[:-1], (shard, dim), acc_own)
    full_up = wide[:, :shard].reshape(dim, units)
    out_full = wide[:, shard:].reshape(-1, packed.shape[0] - shard, units // part, part)
    out_full = jnp.swapaxes(out_full, 1, 2).reshape(dim, part).T
    out_far = swap(out_full, "head", 2)
    down_t = gathered(down_some, "blk", groups[-1:], (shard, dim)).reshape(dim, units)
    raw_e, normed_e, kv_e, kvt_e = project_earlier(meta, pieces, gain_one, w_mix, taps)
    out_far, out_full, _ = together((out_far, out_full, raw_e))
    out_pieces = [out_full, out_far, swap(out_full, "head", 1), swap(out_far, "head", 1)]
    hi, lo = bit_of("head", 1), bit_of("head", 0)
    cot = cotangent.reshape(2, 2, quarter, dim)
    cot = jnp.where(hi, cot[::-1], cot)
    cot = jnp.where(lo, cot[:, ::-1], cot)
    cot = jnp.swapaxes(cot, 0, 1).reshape(rows, dim)
    kv_late, cot, full_up, *out_pieces = together((kv_e, cot, full_up, *out_pieces))
    att, out_t, lse = attend_earlier(meta, q, kv_late, kvt_e, first_row, acc_own, stat_own)

    near = swap(att[2:], "head", 1)
    across = swap(jnp.stack([att[1], near[1]]), "head", 2)
    attended = (att[0], across[0], near[0], across[1])
    quarter_late, down_t = together((own_quarter, down_t))
    hidden, normed_two = after_attend(attended, out_pieces, quarter_late, gain_two)
    ffn_in, act, d_up, *back = feed(quarters(normed_two), cot, full_up, down_t)
    chip_back = sum_halves(*back)
    far_back = swap(chip_back[quarter:], "head", 2)
    feed_grads, *ffn = feed_rest(ffn_in, d_up, cot, act, down_t)
    near_parts = chosen(feed_grads.reshape(2, -1, shard, units), "blk", groups[-1])
    far_back, *near_parts = together((far_back, *near_parts))
    near_parts = received(near_parts, "blk", groups[-1])
    d_hidden, *d_outs, keep_out, keep_far, send_out, gain_two_part = before_back(
        chip_back[:quarter], far_back, hidden, gain_two, cot[:quarter], out_pieces, attended
    )
    across = swap(jnp.stack([d_outs[1], d_outs[3]]), "head", 2)
    near = swap(jnp.stack([d_outs[2], across[1]]), "head", 1)
    d_out_t = jnp.stack([d_outs[0], across[0], near[0], near[1]])
    chip_ffn = sum_halves(*ffn)
    near_out = swap(send_out, "head", 1)
    far_out = swap(total_of([keep_far, near_out[1]]).astype(BF16), "head", 2)
    d_out_t, chip_ffn = together((d_out_t, chip_ffn))
    far_ffn = swap(chip_ffn[quarter:], "head", 2)

    dq_t, d_two, d_one, grad_next, sums_before, sums_halo = earlier_back(
        meta, q, d_out_t, out_t, lse, first_row, kv_e, kvt_e, kv, kvt, raw_e, raw_halo, taps
    )
    from_two = moved(d_two, "blk", -2)
    from_one = moved(d_one, "blk", -1)
    dq_t, far_ffn, far_out = together((dq_t, far_ffn, far_out))
    d_raw, sums_own, grad_mix = own_back(
        meta, q, d_out_t, out_t, lse, first_row, dq_t, kv, kvt, raw, taps, grad_next,
        normed_e, d_two, d_one, normed, keep_out, near_out, far_out,
    )
    chip_ffn, far_ffn, _ = together((chip_ffn, far_ffn, d_raw))
    output = list(quarters((hidden + total_of([chip_ffn[:quarter], far_ffn])).astype(BF16)))
    gain_two_part, _ = together((gain_two_part, d_raw))
    gain_two_part = sum_everywhere(gain_two_part, "head", [(0,), (1,)])
    d_raw, gain_two_part, *more = together((d_raw, gain_two_part, *output, *near_parts))
    output, near_parts = more[:4], more[4:]
    mix_parts = chosen(grad_mix.reshape(1, -1, shard, 4 * part), "blk", groups[-1])
    mix_parts = received(mix_parts, "blk", groups[-1])
    *back, gain_one_part = d_normed_parts(meta, d_raw, from_one, from_two, tokens, w_mix)
    chip_back = sum_halves(*back)
    far_back = swap(chip_back[quarter:], "head", 2)
    _, *near_parts = together((back[0], *near_parts))
    feed_grads = sum_scatter(total_of(near_parts).astype(BF16), "blk", groups[:-1])
    _, gain_one_part = together((chip_back, gain_one_part))
    gain_one_part = sum_everywhere(gain_one_part, "head", [(0,), (1,)])
    grad_tokens = grad_tokens_own(chip_back[:quarter], far_back, own_quarter, gain_one, d_hidden)
    grad_tokens = list(quarters(grad_tokens))
    grad_tokens[2], gain_one_part, output[0], *mix_parts = together(
        (grad_tokens[2], gain_one_part, output[0], *mix_parts)
    )
    grad_tokens = by_place(meta, grad_tokens, F32)
    mix_parts = sum_scatter(total_of(mix_parts).astype(BF16), "blk", groups[:-1])

    output = by_place(meta, output, BF16)
    feed_grads = total_of(feed_grads).reshape(2, shard, units)
    grad_up_shard, grad_down_shard = feed_grads[0], feed_grads[1].T
    mix_shard = total_of(mix_parts).reshape(shard, 4 * part)
    grad_query_shard, grad_key_shard, grad_value_shard = separated(mix_shard[:, : 3 * part])
    grad_out_shard = mix_shard[:, 3 * part :].T

    taps_part = jnp.concatenate([sums_own[:3, :KV] + sums_before[:3], sums_own[:3, KV:] + sums_halo[:3]], axis=1)
    taps_part = jnp.stack(separated(taps_part)).reshape(-1)
    small = jnp.concatenate([gain_two_part[0], gain_one_part[0], taps_part])
    small = sum_everywhere(small, "blk", groups)
    grad_gain_ffn, grad_gain_attn = small[:dim], small[dim : 2 * dim]
    grad_kernels = small[2 * dim :].reshape(3, 3, part)
    return (
        output,
        grad_tokens,
        grad_gain_attn,
        grad_query_shard,
        grad_key_shard,
        grad_value_shard,
        grad_kernels,
        grad_out_shard,
        grad_gain_ffn,
        grad_up_shard,
        grad_down_shard,
    )


def solution(mesh):
    return jax.shard_map(
        body,
        mesh=mesh,
        in_specs=(
            P("blk", None),
            P(),
            P(),
            P("blk", "head"),
            P("blk", "head"),
            P("blk", "head"),
            P(None, None, "head"),
            P("head", "blk"),
            P(),
            P("blk", "head"),
            P("head", "blk"),
            P("blk", None),
        ),
        out_specs=(
            P("blk", None),
            P("blk", None),
            P(),
            P("blk", "head"),
            P("blk", "head"),
            P("blk", "head"),
            P(None, None, "head"),
            P("head", "blk"),
            P(),
            P("blk", "head"),
            P("head", "blk"),
        ),
        check_vma=False,
    )
```

```python
import functools

import jax
import jax.numpy as jnp
from jax import lax
from jax.experimental import pallas as pl
from jax.experimental.pallas import tpu as pltpu
from jax.sharding import PartitionSpec as P

DH = 64
REACH = 2
EPS = 1e-06
MASKED = -1e30
TILE = 256
HALO = 16
F32 = jnp.float32
BF16 = jnp.bfloat16
MIB = 1024 * 1024
COST = pl.CostEstimate(flops=1, bytes_accessed=1, transcendentals=0)


def params(mib=20):
    return pltpu.CompilerParams(vmem_limit_bytes=mib * MIB)


def whole():
    return pl.BlockSpec(memory_space=pltpu.VMEM)


def mm(a, b, ca=1, cb=0):
    return lax.dot_general(a, b, (((ca,), (cb,)), ((), ())), preferred_element_type=F32)


def swap(x, axis, mask):
    return lax.ppermute(x, axis, [(i, i ^ mask) for i in range(lax.axis_size(axis))])


def moved(x, axis, distance):
    size = lax.axis_size(axis)
    return lax.ppermute(x, axis, [(i, i + distance) for i in range(size) if 0 <= i + distance < size])


def bit_groups(axis):
    bits = list(range(lax.axis_size(axis).bit_length() - 2, -1, -1))
    upper, groups = bits[:-1], []
    while upper:
        groups.append(tuple(upper[:2]))
        upper = upper[2:]
    return groups + [(0,)]


def bit_of(axis, bit):
    return ((lax.axis_index(axis) >> bit) & 1) == 1


def masks_of(group):
    if len(group) == 1:
        return [0, 1 << group[0]]
    hi, lo = 1 << group[0], 1 << group[1]
    return [0, lo, hi, hi | lo]


def sent_round(shard, axis):
    pieces = [shard[None]]
    for group in bit_groups(axis)[:-1]:
        out = jnp.concatenate(pieces)
        pieces = [out] + [swap(out, axis, m) for m in masks_of(group)[1:]]
    return pieces


def gathered_masks(axis):
    masks = [0]
    *groups, last = bit_groups(axis)
    for group in groups:
        masks = [m ^ old for m in masks_of(group) for old in masks]
    return masks, [m ^ masks_of(last)[1] for m in masks]


def joined_kernel(*refs):
    *pieces, out_ref = refs
    at = 0
    for piece in pieces:
        for n in range(piece.shape[0]):
            out_ref[at] = piece[n]
            at += 1


def joined(pieces):
    count = sum(piece.shape[0] for piece in pieces)
    return pl.pallas_call(
        joined_kernel,
        out_shape=jax.ShapeDtypeStruct((count, *pieces[0].shape[1:]), pieces[0].dtype),
        in_specs=[whole()] * len(pieces),
        out_specs=whole(),
        compiler_params=params(),
        cost_estimate=COST,
        name="joined",
    )(*pieces)


def pieces_of(own, axis, shard):
    other = swap(own, axis, 1)
    if shard % 16 == 0:
        return own, other
    size = lax.axis_size(axis)
    masks = sum(gathered_masks(axis), [])
    both = jnp.concatenate([own, other])
    place = lax.axis_index(axis) ^ jnp.array(masks)
    return (jnp.zeros_like(both).at[place].set(both),)


def put_rows(to_ref, refs, blk, axis_masks, shard):
    if len(refs) == 1:
        for n in range(refs[0].shape[0]):
            to_ref[n * shard : (n + 1) * shard, :] = refs[0][n, :shard, :].astype(to_ref.dtype)
        return
    for ref, masks in zip(refs, axis_masks):
        for n, mask in enumerate(masks):
            to = pl.ds(pl.multiple_of((blk ^ mask) * shard, 16), shard)
            to_ref[to, :] = ref[n, :shard, :].astype(to_ref.dtype)


def chosen(full, axis, group):
    r = 1 << len(group)
    out = full.reshape(full.shape[0], -1, r, *full.shape[2:])
    mine = (lax.axis_index(axis) >> group[-1]) & (r - 1)
    return [lax.dynamic_index_in_dim(out, mine ^ (m >> group[-1]), 2, keepdims=False) for m in masks_of(group)]


def received(parts, axis, group):
    keep, *send = parts
    return [keep] + [swap(part, axis, m) for m, part in zip(masks_of(group)[1:], send)]


def total_of(parts):
    total = parts[0].astype(F32)
    for part in parts[1:]:
        total = total + part.astype(F32)
    return total


def sum_scatter(full, axis, groups):
    *rest, last = reversed(groups)
    out = full
    for group in rest:
        out = total_of(received(chosen(out, axis, group), axis, group)).astype(BF16)
    return received(chosen(out, axis, last), axis, last)


def sum_everywhere(x, axis, groups):
    for group in groups:
        x = total_of([x] + [swap(x, axis, m) for m in masks_of(group)[1:]])
    return x


def quarters(own):
    far = swap(own, "head", 2)
    return own, far, swap(own, "head", 1), swap(far, "head", 1)


PAIR = 2 * DH
KV = 3 * PAIR
KEY_LANES = ((0, PAIR), (0, PAIR), (2 * PAIR, KV))
VALUE_LANES = ((PAIR, 2 * PAIR), (PAIR, 2 * PAIR), (2 * PAIR, KV))
KEY_ROWS = (0, DH, 2 * PAIR)
VALUE_ROWS = (PAIR, PAIR + DH, 2 * PAIR + DH)


def arranged(q, k, v):
    return jnp.concatenate([k[..., :PAIR], v[..., :PAIR], k[..., PAIR:], v[..., PAIR:], q], axis=-1)


def separated(x):
    k = jnp.concatenate([x[..., :PAIR], x[..., 2 * PAIR : 2 * PAIR + DH]], axis=-1)
    v = jnp.concatenate([x[..., PAIR : 2 * PAIR], x[..., 2 * PAIR + DH : KV]], axis=-1)
    return x[..., KV:], k, v


def pack_kernel(up_ref, out_ref, down_ref, packed_ref, down_t_ref):
    shard, units = up_ref.shape
    out_t = out_ref[...].astype(F32).T
    few = packed_ref.shape[0] - shard
    packed_ref[0:shard, :] = up_ref[...]
    out_t = jnp.concatenate([out_t[n : n + few] for n in range(0, shard, few)], axis=1)
    packed_ref[shard:, :] = out_t.astype(BF16)
    down_t_ref[...] = down_ref[...].astype(F32).T.astype(BF16)


def pack(w_up, w_out, w_down):
    shard, units = w_up.shape
    part = w_out.shape[0]
    return pl.pallas_call(
        pack_kernel,
        out_shape=(
            jax.ShapeDtypeStruct((shard + shard * part // units, units), BF16),
            jax.ShapeDtypeStruct((shard, units), BF16),
        ),
        in_specs=[whole()] * 3,
        out_specs=(whole(), whole()),
        compiler_params=params(),
        cost_estimate=COST,
        name="pack",
    )(w_up, w_out, w_down)


def unpack_out_kernel(meta_ref, *refs, masks, shard):
    *packed_refs, out_ref, out_t_ref = refs
    few = packed_refs[0].shape[1] - shard
    part = out_t_ref.shape[1]

    def put(ref, n, place):
        rows = ref[n].astype(F32)[shard:]
        for k in range(shard // few):
            to = pl.ds(place * shard + k * few, few)
            out_t_ref[to, :] = rows[:, k * part : (k + 1) * part]

    if len(packed_refs) == 1:
        for n in range(packed_refs[0].shape[0]):
            put(packed_refs[0], n, n)
    else:
        for ref, distances in zip(packed_refs, masks):
            for n, mask in enumerate(distances):
                put(ref, n, meta_ref[BLK] ^ mask)
    out_ref[...] = out_t_ref[...].T.astype(BF16)


def unpack_out(meta, packed, masks, shard, part):
    dim = shard * sum(x.shape[0] for x in packed)
    return pl.pallas_call(
        functools.partial(unpack_out_kernel, masks=masks, shard=shard),
        out_shape=jax.ShapeDtypeStruct((part, dim), BF16),
        in_specs=[pl.BlockSpec(memory_space=pltpu.SMEM), *[whole()] * len(packed)],
        out_specs=whole(),
        scratch_shapes=[pltpu.VMEM((dim, part), F32)],
        compiler_params=params(),
        cost_estimate=COST,
        name="unpack_out",
    )(meta, *packed)


def unit_times_gain(x, gain):
    return x * lax.rsqrt(jnp.mean(x * x, axis=-1, keepdims=True) + EPS) * gain


def mix_rows(buf_ref, mix_ref, taps, starts, base, rows):
    mix_ref[...] = (
        taps[0:1] * buf_ref[8 : 8 + rows, :]
        + taps[1:2] * buf_ref[7 : 7 + rows, :]
        + taps[2:3] * buf_ref[6 : 6 + rows, :]
    )
    for start in starts:
        r = start - base

        @pl.when((r >= 0) & (r < rows))
        def _(r=r):
            mix_ref[pl.ds(r, 1), :] = taps[0:1] * buf_ref[pl.ds(8 + r, 1), :]

        @pl.when((r + 1 >= 0) & (r + 1 < rows))
        def _(r=r):
            mix_ref[pl.ds(r + 1, 1), :] = (
                taps[0:1] * buf_ref[pl.ds(9 + r, 1), :] + taps[1:2] * buf_ref[pl.ds(8 + r, 1), :]
            )


def project_own_kernel(
    meta_ref, x_ref, halo_ref, gain_ref, taps_ref, *refs, base, masks, shard,
):
    *w_refs, w_ref, raw_halo_ref, raw_ref, normed_ref, q_ref, kv_ref, kvt_ref, buf_ref, mix_ref, w_in_ref = refs
    i = pl.program_id(0)
    rows = x_ref.shape[0]
    gain = gain_ref[...]

    @pl.when(i == 0)
    def _():
        put_rows(w_in_ref, w_refs, meta_ref[BLK], masks, shard)
        w_in = w_in_ref[...]
        part = w_in.shape[1] // 3
        w_ref[...] = arranged(w_in[:, :part], w_in[:, part : 2 * part], w_in[:, 2 * part : 3 * part])

    w = w_ref[...]

    @pl.when(i == 0)
    def _():
        halo = halo_ref[halo_ref.shape[0] - HALO :, :].astype(F32)
        halo = jnp.where(meta_ref[HAS_ONE] == 1, halo, 0.0)
        normed = unit_times_gain(halo, gain).astype(BF16)
        raw_low = mm(normed, w).astype(BF16)
        raw_halo_ref[...] = raw_low[:, KV:]
        buf_ref[0:8, :] = raw_low.astype(F32)[HALO - 8 :, :]

    normed = unit_times_gain(x_ref[...].astype(F32), gain).astype(BF16)
    raw_low = mm(normed, w).astype(BF16)
    normed_ref[...] = normed
    raw_ref[...] = raw_low
    raw = raw_low.astype(F32)
    buf_ref[8 : 8 + rows, :] = raw
    mix_rows(buf_ref, mix_ref, taps_ref[...], [meta_ref[STARTS + n] for n in range(8)], base + i * rows, rows)
    buf_ref[0:8, :] = raw[rows - 8 :, :]
    q_ref[...] = mix_ref[:, KV:].astype(BF16)
    kv = mix_ref[:, :KV]
    kv_ref[...] = kv.astype(BF16)
    kvt_ref[...] = kv.T.astype(BF16)


def project_own(meta, tokens, halo, gain, taps, w, masks):
    rows, dim = tokens.shape
    shard, width = w[0].shape[1:]
    step = 2 * TILE
    tile = lambda n: pl.BlockSpec((step, n), lambda i, *_: (i, 0))
    return pl.pallas_call(
        functools.partial(project_own_kernel, base=REACH * rows, masks=masks, shard=shard),
        out_shape=(
            jax.ShapeDtypeStruct((dim, width), BF16),
            jax.ShapeDtypeStruct((HALO, width - KV), BF16),
            jax.ShapeDtypeStruct((rows, width), BF16),
            jax.ShapeDtypeStruct((rows, dim), BF16),
            jax.ShapeDtypeStruct((rows, width - KV), BF16),
            jax.ShapeDtypeStruct((rows, KV), BF16),
            jax.ShapeDtypeStruct((KV, rows), BF16),
        ),
        grid_spec=pltpu.PrefetchScalarGridSpec(
            num_scalar_prefetch=1,
            grid=(rows // step,),
            in_specs=[tile(dim), whole(), whole(), whole(), *[whole()] * len(w)],
            out_specs=(
                whole(),
                whole(),
                tile(width),
                tile(dim),
                tile(width - KV),
                tile(KV),
                pl.BlockSpec((KV, step), lambda i, *_: (0, i)),
            ),
            scratch_shapes=[
                pltpu.VMEM((8 + step, width), F32),
                pltpu.VMEM((step, width), F32),
                pltpu.VMEM((dim, width), BF16),
            ],
        ),
        compiler_params=params(),
        cost_estimate=COST,
        name="project_own",
    )(meta, tokens, halo, gain, taps, *w)


def project_earlier_kernel(meta_ref, *refs):
    pieces = refs[:8]
    gain_ref, w_ref, taps_ref, raw_ref, normed_ref, kv_ref, kvt_ref, x_ref, buf_ref, mix_ref = refs[8:]
    i = pl.program_id(0)
    rows = x_ref.shape[0]
    quarter = rows // 2

    @pl.when(i == 0)
    def _():
        buf_ref[0:8, :] = jnp.zeros((8, KV), F32)

    for hop in range(REACH):
        for slot, d in enumerate((0, 2, 1, 3)):
            place = 4 * hop + (meta_ref[0] ^ d)

            @pl.when(i == place >> 1)
            def _(piece=pieces[4 * hop + slot], place=place):
                x_ref[pl.ds(pl.multiple_of((place & 1) * quarter, quarter), quarter), :] = piece[:quarter, :]

    exists = jnp.where(i < pl.num_programs(0) // REACH, meta_ref[HAS_TWO], meta_ref[HAS_ONE])
    x = jnp.where(exists == 1, x_ref[...].astype(F32), 0.0)
    normed = unit_times_gain(x, gain_ref[...]).astype(BF16)
    normed_ref[...] = normed
    raw_low = mm(normed, w_ref[:, :KV]).astype(BF16)
    raw_ref[...] = raw_low
    raw = raw_low.astype(F32)
    buf_ref[8 : 8 + rows, :] = raw
    mix_rows(buf_ref, mix_ref, taps_ref[:, :KV], [meta_ref[STARTS + n] for n in range(8)], i * rows, rows)
    buf_ref[0:8, :] = raw[rows - 8 :, :]
    kv = mix_ref[...]
    kv_ref[...] = kv.astype(BF16)
    kvt_ref[...] = kv.T.astype(BF16)


def project_earlier(meta, pieces, gain, w, taps):
    dim = pieces[0].shape[1]
    quarter = pieces[0].shape[0] - HALO
    step = 2 * quarter
    span = len(pieces) * quarter
    tile = lambda n: pl.BlockSpec((step, n), lambda i, *_: (i, 0))
    return pl.pallas_call(
        project_earlier_kernel,
        out_shape=(
            jax.ShapeDtypeStruct((span, KV), BF16),
            jax.ShapeDtypeStruct((span, dim), BF16),
            jax.ShapeDtypeStruct((span, KV), BF16),
            jax.ShapeDtypeStruct((KV, span), BF16),
        ),
        grid_spec=pltpu.PrefetchScalarGridSpec(
            num_scalar_prefetch=1,
            grid=(span // step,),
            in_specs=[whole()] * 11,
            out_specs=(tile(KV), tile(dim), tile(KV), pl.BlockSpec((KV, step), lambda i, *_: (0, i))),
            scratch_shapes=[
                pltpu.VMEM((step, dim), BF16),
                pltpu.VMEM((8 + step, KV), F32),
                pltpu.VMEM((step, KV), F32),
            ],
        ),
        compiler_params=params(),
        cost_estimate=COST,
        name="project_earlier",
    )(meta, *pieces, gain, w, taps)


LOW, FULL, STARTS = 1, 5, 9
HAS_ONE, HAS_TWO, NEXT_ONE, NEXT_TWO, BLK = 17, 18, 19, 20, 21


STEP = 2 * TILE


def masked_scores(scores, key_base, query_base, first, diagonal):
    keys = lax.broadcasted_iota(jnp.int32, scores.shape, 0)
    allowed = keys >= first - key_base
    if diagonal is not None:
        allowed = allowed & (keys <= lax.broadcasted_iota(jnp.int32, scores.shape, 1) + (query_base - diagonal))
    return jnp.where(allowed, scores, MASKED)


def place_heads(to_ref, lanes, across, halves):
    zero = jnp.zeros((DH, across.shape[1]), to_ref.dtype)
    for h, half in enumerate(halves):
        to_ref[h, half * DH : (half + 1) * DH, lanes] = across[h * DH : (h + 1) * DH].astype(to_ref.dtype)
        to_ref[h, (1 - half) * DH : (2 - half) * DH, lanes] = zero


KEY_HALVES, VALUE_HALVES = (0, 1, 0), (0, 1, 1)


def eights(x, how):
    return how(x.reshape(x.shape[0] // 8, 8, x.shape[1]), axis=0)


def query_tiles(rows):
    return [slice(n, n + TILE) for n in range(0, rows, TILE)]


def staged(items, first, second, depth=2):
    waiting = []
    for item in items:
        waiting.append((item, first(item)))
        if len(waiting) > depth:
            second(*waiting.pop(0))
    for pair in waiting:
        second(*pair)


def attend_tiles(steps, q_ref, kv_ref, kvt_ref, first_ref, acc_ref, q_across_ref, top_ref, sum_ref):
    for lanes in query_tiles(q_ref.shape[0]):
        place_heads(q_across_ref, lanes, (q_ref[lanes, :].astype(F32) * (DH**-0.5)).T, KEY_HALVES)
    acc_ref[...] = jnp.zeros_like(acc_ref)
    top_ref[...] = jnp.full(top_ref.shape, MASKED, F32)
    sum_ref[...] = jnp.zeros_like(sum_ref)

    def run(row, keys, window_row, begin, masked, diagonal):
        at = pl.ds(row, keys)
        items = [(h, lanes) for h in range(3) for lanes in query_tiles(q_ref.shape[0])[begin // TILE :]]
        key_rows = [kv_ref[at, KEY_LANES[h][0] : KEY_LANES[h][1]] for h in range(3)]
        values = [kvt_ref[VALUE_ROWS[h] : VALUE_ROWS[h] + DH, at] for h in range(3)]
        queries = [q_across_ref[h, :, lanes] for h, lanes in items]
        tops = [top_ref[h : h + 1, lanes] for h, lanes in items]
        firsts = {lanes.start: first_ref[:, lanes] for _, lanes in items}
        results = []

        def first(n):
            h, lanes = items[n]
            scores = mm(key_rows[h], queries[n])
            if masked:
                scores = masked_scores(scores, window_row, lanes.start, firsts[lanes.start], diagonal)
            return scores

        def second(n, scores):
            h, lanes = items[n]
            top = jnp.maximum(tops[n], jnp.max(eights(scores, jnp.max), axis=0, keepdims=True))
            weights = jnp.exp(scores - top)
            total = jnp.sum(eights(weights, jnp.sum), axis=0, keepdims=True)
            results.append((top, total, mm(values[h], weights.astype(BF16))))

        staged(range(len(items)), first, second)
        for n, (h, lanes) in enumerate(items):
            top, total, out = results[n]
            fade = jnp.exp(tops[n] - top)
            top_ref[h : h + 1, lanes] = top
            sum_ref[h : h + 1, lanes] = sum_ref[h : h + 1, lanes] * fade + total
            rows = slice(h * DH, (h + 1) * DH)
            acc_ref[rows, lanes] = acc_ref[rows, lanes] * fade + out

    steps(run)


def earlier_steps(meta_ref, before, rows):
    last = rows // TILE - 1
    end = before // STEP
    low = meta_ref[LOW] // (STEP // TILE)
    full = (meta_ref[FULL + last] + STEP // TILE - 1) // (STEP // TILE)
    middle = jnp.clip(full, low, jnp.maximum(end, low))

    def steps(run):
        def one(masked):
            def step(n, carry):
                row = pl.multiple_of(n * STEP, STEP)
                run(row, STEP, row, 0, masked, None)
                return carry

            return step

        lax.fori_loop(low, middle, one(True), 0)
        lax.fori_loop(middle, end, one(False), 0)

    return steps


def attend_own_kernel(q_ref, kv_ref, kvt_ref, first_ref, acc_ref, stat_ref, q_across_ref, *, base):
    rows = q_ref.shape[0]

    def steps(run):
        for row in range(0, rows, STEP):
            run(row, STEP, base + row, row, True, row)

    top_ref, sum_ref = stat_ref.at[0:8], stat_ref.at[8:16]
    attend_tiles(steps, q_ref, kv_ref, kvt_ref, first_ref, acc_ref, q_across_ref, top_ref, sum_ref)


def attend_earlier_kernel(
    meta_ref, q_ref, kv_ref, kvt_ref, first_ref, acc_own_ref, stat_own_ref,
    att_ref, ot_ref, lse_ref, q_across_ref, top_ref, sum_ref,
):
    rows = q_ref.shape[0]
    steps = earlier_steps(meta_ref, kv_ref.shape[0], rows)
    attend_tiles(steps, q_ref, kv_ref, kvt_ref, first_ref, ot_ref, q_across_ref, top_ref, sum_ref)
    for h in range(3):
        to = slice(h * DH, (h + 1) * DH)
        top_here, top_own = top_ref[h : h + 1, :], stat_own_ref[h : h + 1, :]
        top = jnp.maximum(top_here, top_own)
        here, own = jnp.exp(top_here - top), jnp.exp(top_own - top)
        total = here * sum_ref[h : h + 1, :] + own * stat_own_ref[8 + h : 9 + h, :]
        out = ot_ref[to, :] * (here / total) + acc_own_ref[to, :] * (own / total)
        ot_ref[to, :] = out
        lse_ref[h : h + 1, :] = top + jnp.log(total)
        for n, lanes in enumerate(query_tiles(rows)):
            att_ref[slot_of(n, meta_ref), to, :] = out[:, lanes].astype(BF16)


def slot_of(i, meta):
    d = i ^ meta[0]
    return (d >> 1) | ((d & 1) << 1)


def attend_own(q, kv, kvt, first_row):
    rows, part = q.shape
    return pl.pallas_call(
        functools.partial(attend_own_kernel, base=REACH * rows),
        out_shape=(jax.ShapeDtypeStruct((part, rows), F32), jax.ShapeDtypeStruct((16, rows), F32)),
        in_specs=[whole()] * 4,
        out_specs=(whole(), whole()),
        scratch_shapes=[pltpu.VMEM((3, PAIR, rows), BF16)],
        compiler_params=params(),
        cost_estimate=COST,
        name="attend_own",
    )(q, kv, kvt, first_row)


def attend_earlier(meta, q, kv, kvt, first_row, acc_own, stat_own):
    rows, part = q.shape
    return pl.pallas_call(
        attend_earlier_kernel,
        out_shape=(
            jax.ShapeDtypeStruct((rows // TILE, part, TILE), BF16),
            jax.ShapeDtypeStruct((part, rows), F32),
            jax.ShapeDtypeStruct((8, rows), F32),
        ),
        in_specs=[pl.BlockSpec(memory_space=pltpu.SMEM)] + [whole()] * 6,
        out_specs=(whole(), whole(), whole()),
        scratch_shapes=[
            pltpu.VMEM((3, PAIR, rows), BF16),
            pltpu.VMEM((8, rows), F32),
            pltpu.VMEM((8, rows), F32),
        ],
        compiler_params=params(),
        cost_estimate=COST,
        name="attend_earlier",
    )(meta, q, kv, kvt, first_row, acc_own, stat_own)


def back_scratch(rows):
    return [
        pltpu.VMEM((3, PAIR, rows), BF16),
        pltpu.VMEM((3, PAIR, rows), BF16),
        pltpu.VMEM((3, rows, PAIR), BF16),
        pltpu.VMEM((3, rows, PAIR), BF16),
        pltpu.VMEM((8, rows), F32),
        pltpu.VMEM((3, STEP, rows), BF16),
        pltpu.VMEM((3, STEP, rows), BF16),
    ]


def back_prepare(meta_ref, q_ref, dt_ref, ot_ref, scratch):
    q_across_ref, d_across_ref, q_alone_ref, d_alone_ref, delta_ref = scratch[:5]
    lane = lax.broadcasted_iota(jnp.int32, (TILE, PAIR), 1)
    none = jnp.zeros((TILE, PAIR), BF16)

    def alone(to_ref, rows, x, halves):
        last = jnp.concatenate([x[:, PAIR:]] * 2, axis=1)
        for h, half in enumerate(halves):
            to_ref[h, rows, :] = jnp.where((lane < DH) == (half == 0), x[:, :PAIR] if h < 2 else last, none)

    for n, rows in enumerate(query_tiles(q_ref.shape[0])):
        scaled = q_ref[rows, :].astype(F32) * (DH**-0.5)
        place_heads(q_across_ref, rows, scaled.T, KEY_HALVES)
        alone(q_alone_ref, rows, scaled.astype(BF16), KEY_HALVES)
        d_wide = dt_ref[slot_of(n, meta_ref)].astype(F32)
        place_heads(d_across_ref, rows, d_wide, VALUE_HALVES)
        alone(d_alone_ref, rows, d_wide.T.astype(BF16), VALUE_HALVES)
        terms = d_wide * ot_ref[:, rows]
        for h in range(3):
            delta_ref[h : h + 1, rows] = jnp.sum(terms[h * DH : (h + 1) * DH], axis=0, keepdims=True)


def back_step(row, keys, window_row, begin, masked, diagonal, kv_ref, kvt_ref, lse_ref, first_ref, grad_ref, lead, dq_ref, scratch):
    q_across_ref, d_across_ref, q_alone_ref, d_alone_ref, delta_ref, p_ref, ds_ref = scratch
    rows = dq_ref.shape[1]
    at = pl.ds(row, keys)
    items = [(h, lanes) for h in range(3) for lanes in query_tiles(rows)[begin // TILE :]]
    key_rows = [kv_ref[at, KEY_LANES[h][0] : KEY_LANES[h][1]] for h in range(3)]
    value_rows = [kv_ref[at, VALUE_LANES[h][0] : VALUE_LANES[h][1]] for h in range(3)]
    keys_t = [kvt_ref[KEY_ROWS[h] : KEY_ROWS[h] + DH, at] for h in range(3)]
    queries = [q_across_ref[h, :, lanes] for h, lanes in items]
    d_outs = [d_across_ref[h, :, lanes] for h, lanes in items]
    lses = [lse_ref[h : h + 1, lanes] for h, lanes in items]
    deltas = [delta_ref[h : h + 1, lanes] for h, lanes in items]
    firsts = {lanes.start: first_ref[:, lanes] for _, lanes in items}
    results = []

    def first(n):
        h, lanes = items[n]
        scores = mm(key_rows[h], queries[n])
        if masked:
            scores = masked_scores(scores, window_row, lanes.start, firsts[lanes.start], diagonal)
        return scores, mm(value_rows[h], d_outs[n])

    def second(n, both):
        h, lanes = items[n]
        scores, d_probs = both
        probs = jnp.exp(scores - lses[n])
        d_scores = (probs * (d_probs - deltas[n])).astype(BF16)
        p_ref[h, :keys, lanes] = probs.astype(BF16)
        ds_ref[h, :keys, lanes] = d_scores
        results.append(mm(keys_t[h], d_scores))

    staged(range(len(items)), first, second, 1)
    for n, (h, lanes) in enumerate(items):
        dq_ref[h * DH : (h + 1) * DH, lanes] += results[n]
    seen = slice(begin, rows)
    to = pl.ds(pl.multiple_of(lead + row, 8), keys)
    terms = (
        ((ds_ref, q_alone_ref, 0), (ds_ref, q_alone_ref, 1)),
        ((p_ref, d_alone_ref, 0), (p_ref, d_alone_ref, 1)),
        ((ds_ref, q_alone_ref, 2), (p_ref, d_alone_ref, 2)),
    )
    for n, ((left_a, right_a, a), (left_b, right_b, b)) in enumerate(terms):
        lanes = slice(n * PAIR, (n + 1) * PAIR)
        grad_ref[to, lanes] += mm(left_a[a, :keys, seen], right_a[a, seen, :]) + mm(
            left_b[b, :keys, seen], right_b[b, seen, :]
        )


def unmix_rows(grad_ref, raw_ref, fix_ref, taps, starts, rows, sums_ref):
    width = grad_ref.shape[1]

    def raw_row(r):
        group = raw_ref[pl.ds(pl.multiple_of((r // HALO) * HALO, HALO), HALO), :].astype(F32)
        row = lax.broadcasted_iota(jnp.int32, group.shape, 0)
        return jnp.sum(jnp.where(row == r % HALO, group, 0.0), axis=0, keepdims=True)

    sums_ref[...] = jnp.zeros_like(sums_ref)
    inside = [(s >= 1) & (s <= rows + 1) for s in starts]
    for n, s in enumerate(starts):

        @pl.when(inside[n])
        def _(n=n, s=s):
            one_before = grad_ref[pl.ds(7 + s, 1), :]
            fix_ref[2 * n : 2 * n + 1, :] = taps[0:1] * one_before
            fix_ref[2 * n + 1 : 2 * n + 2, :] = taps[0:1] * grad_ref[pl.ds(6 + s, 1), :] + taps[1:2] * one_before
            here = grad_ref[pl.ds(8 + s, 1), :]

            @pl.when(s >= 2)
            def _():
                sums_ref[2:3, :] -= raw_row(jnp.maximum(s - 2, 0)) * here

            @pl.when(s <= rows)
            def _():
                raw_one = raw_row(s - 1)
                sums_ref[1:2, :] -= raw_one * here
                following = starts[n + 1] if n + 1 < len(starts) else s + 2

                @pl.when(following != s + 1)
                def _():
                    sums_ref[2:3, :] -= raw_one * grad_ref[pl.ds(9 + s, 1), :]

    sizes = [HALO] * (1 if rows % TILE else 0) + [TILE] * (rows // TILE)
    lo = 0
    totals = [jnp.zeros((8, width), F32) for _ in range(3)]
    for size in sizes:
        now = grad_ref[8 + lo : 8 + lo + size, :]
        one = grad_ref[9 + lo : 9 + lo + size, :]
        two = grad_ref[10 + lo : 10 + lo + size, :]
        raw = raw_ref[lo : lo + size, :].astype(F32)
        for j, shifted in enumerate((now, one, two)):
            totals[j] = totals[j] + eights(raw * shifted, jnp.sum)
        grad_ref[8 + lo : 8 + lo + size, :] = taps[0:1] * now + taps[1:2] * one + taps[2:3] * two
        lo += size
    for j in range(3):
        sums_ref[j : j + 1, :] += jnp.sum(totals[j], axis=0, keepdims=True)
    for n in reversed(range(len(starts))):

        @pl.when(inside[n])
        def _(n=n, s=starts[n]):
            grad_ref[pl.ds(7 + s, 1), :] = fix_ref[2 * n : 2 * n + 1, :]
            grad_ref[pl.ds(6 + s, 1), :] = fix_ref[2 * n + 1 : 2 * n + 2, :]


def earlier_back_kernel(
    meta_ref, q_ref, dt_ref, ot_ref, lse_ref, first_ref, kv_ref, kvt_ref, kv_own_ref, kvt_own_ref, raw_ref,
    raw_halo_ref, taps_ref, dq_ref, two_ref, one_ref, next_ref, sums_ref, sums_q_ref,
    grad_ref, grad_q_ref, fix_ref, fix_q_ref, *scratch,
):
    before = kv_ref.shape[0]
    rows = q_ref.shape[0]
    grad_ref[...] = jnp.zeros_like(grad_ref)
    grad_q_ref[...] = jnp.zeros_like(grad_q_ref)
    dq_ref[...] = jnp.zeros_like(dq_ref)
    back_prepare(meta_ref, q_ref, dt_ref, ot_ref, scratch)
    run = lambda *step: back_step(*step, kv_ref, kvt_ref, lse_ref, first_ref, grad_ref, 8, dq_ref, scratch)
    earlier_steps(meta_ref, before, rows)(run)
    back_step(
        0, TILE, before, 0, True, 0, kv_own_ref, kvt_own_ref, lse_ref, first_ref, grad_ref, 8 + before, dq_ref, scratch
    )
    grad_q_ref[8 + HALO : 16 + HALO, :] = dq_ref[:, :PAIR].T[:8] * (DH**-0.5)
    starts = [meta_ref[STARTS + n] for n in range(8)]
    next_ref[...] = grad_ref[8 + before : 8 + before + TILE, :]
    unmix_rows(grad_ref, raw_ref, fix_ref, taps_ref[:, :KV], starts, before, sums_ref)
    starts = [s - (before - HALO) for s in starts]
    unmix_rows(grad_q_ref, raw_halo_ref, fix_q_ref, taps_ref[:, KV:], starts, HALO, sums_q_ref)
    half = before // 2
    two_ref[...] = grad_ref[8 : 8 + half, :].astype(BF16)
    one_ref[0:half, :] = grad_ref[8 + half : 8 + before, :].astype(BF16)
    queries = grad_q_ref[8 : 8 + HALO, :]
    one_ref[half : half + HALO, :] = jnp.concatenate([queries, jnp.zeros_like(queries)], axis=1).astype(BF16)


def earlier_back(meta, q, d_out_t, out_t, lse, first_row, kv, kvt, kv_own, kvt_own, raw, raw_halo, taps):
    rows, part = q.shape
    before = kv.shape[0]
    return pl.pallas_call(
        earlier_back_kernel,
        out_shape=(
            jax.ShapeDtypeStruct((part, rows), F32),
            jax.ShapeDtypeStruct((rows, KV), BF16),
            jax.ShapeDtypeStruct((rows + HALO, KV), BF16),
            jax.ShapeDtypeStruct((TILE, KV), F32),
            jax.ShapeDtypeStruct((8, KV), F32),
            jax.ShapeDtypeStruct((8, part), F32),
        ),
        grid=(1,),
        in_specs=[pl.BlockSpec(memory_space=pltpu.SMEM)]
        + [whole()] * 7
        + [
            pl.BlockSpec((TILE, KV), lambda i: (0, 0)),
            pl.BlockSpec((KV, TILE), lambda i: (0, 0)),
            whole(),
            whole(),
            whole(),
        ],
        out_specs=tuple([whole()] * 6),
        scratch_shapes=[
            pltpu.VMEM((8 + before + TILE + 8, KV), F32),
            pltpu.VMEM((8 + HALO + 8, part), F32),
            pltpu.VMEM((16, KV), F32),
            pltpu.VMEM((16, part), F32),
            *back_scratch(rows),
        ],
        compiler_params=params(34),
        cost_estimate=COST,
        name="earlier_back",
    )(meta, q, d_out_t, out_t, lse, first_row, kv, kvt, kv_own, kvt_own, raw, raw_halo, taps)


def own_back_kernel(
    meta_ref, q_ref, dt_ref, ot_ref, lse_ref, first_ref, dq_in_ref, kv_ref, kvt_ref, raw_ref, taps_ref, next_ref,
    normed_e_ref, two_ref, one_ref, normed_ref, out_keep_ref, out_near_ref, out_far_ref,
    d_raw_ref, sums_ref, mix_ref, dq_ref, grad_ref, fix_ref, *scratch,
):
    rows = kv_ref.shape[0]
    base = REACH * rows
    grad_ref[...] = jnp.zeros_like(grad_ref)
    grad_ref[8 : 8 + TILE, :KV] = next_ref[...]
    dq_ref[...] = dq_in_ref[...]
    back_prepare(meta_ref, q_ref, dt_ref, ot_ref, scratch)
    row = TILE
    while row < rows:
        keys = TILE if row % STEP else STEP
        back_step(
            row, keys, base + row, row, True, row, kv_ref, kvt_ref, lse_ref, first_ref, grad_ref, 8, dq_ref, scratch
        )
        row += keys
    for lanes in query_tiles(rows):
        grad_ref[8 + lanes.start : 8 + lanes.stop, KV:] = dq_ref[:, lanes].T * (DH**-0.5)
    starts = [meta_ref[STARTS + n] - base for n in range(8)]
    unmix_rows(grad_ref, raw_ref, fix_ref, taps_ref[...], starts, rows, sums_ref)
    d_raw_ref[...] = grad_ref[8 : 8 + rows, :].astype(BF16)
    part = out_keep_ref.shape[0]
    out_grad = out_keep_ref[...].astype(F32) + out_near_ref[0].astype(F32) + out_far_ref[...].astype(F32)
    for n in range(normed_ref.shape[1] // TILE):
        lanes = slice(n * TILE, (n + 1) * TILE)
        grad = mm(normed_ref[:, lanes], d_raw_ref[...], 0, 0)
        earlier = mm(normed_e_ref[:rows, lanes], two_ref[...], 0, 0)
        earlier = earlier + mm(normed_e_ref[rows:, lanes], one_ref[:rows, :], 0, 0)
        halo = mm(normed_e_ref[2 * rows - HALO :, lanes], one_ref[rows:, :], 0, 0)[:, :part]
        mix_ref[lanes, :KV] = (grad[:, :KV] + earlier).astype(BF16)
        rest = jnp.concatenate([grad[:, KV:] + halo, out_grad[:, lanes].T], axis=1)
        mix_ref[lanes, KV:] = rest.astype(BF16)


def own_back(
    meta, q, d_out_t, out_t, lse, first_row, dq_t, kv, kvt, raw, taps, grad_next, normed_e, two, one, normed, *grad_out
):
    rows, part = q.shape
    width = raw.shape[1]
    return pl.pallas_call(
        own_back_kernel,
        out_shape=(
            jax.ShapeDtypeStruct((rows, width), BF16),
            jax.ShapeDtypeStruct((8, width), F32),
            jax.ShapeDtypeStruct((normed.shape[1], width + part), BF16),
        ),
        in_specs=[pl.BlockSpec(memory_space=pltpu.SMEM)] + [whole()] * 18,
        out_specs=(whole(), whole(), whole()),
        scratch_shapes=[
            pltpu.VMEM((part, rows), F32),
            pltpu.VMEM((8 + rows + 8, width), F32),
            pltpu.VMEM((16, width), F32),
            *back_scratch(rows),
        ],
        compiler_params=params(34),
        cost_estimate=COST,
        name="own_back",
    )(
        meta, q, d_out_t, out_t, lse, first_row, dq_t, kv, kvt, raw, taps, grad_next,
        normed_e, two, one, normed, *grad_out,
    )


def after_attend_kernel(a0, a1, a2, a3, w0, w1, w2, w3, x_ref, gain_ref, hidden_ref, normed_ref):
    branch = mm(a0[...], w0[...], 0, 0)
    for a, w in ((a1, w1), (a2, w2), (a3, w3)):
        branch = branch + mm(a[...], w[...], 0, 0)
    hidden = x_ref[...].astype(F32) + branch
    hidden_ref[...] = hidden
    factor = lax.rsqrt(jnp.mean(hidden * hidden, axis=-1, keepdims=True) + EPS)
    normed_ref[...] = (hidden * factor * gain_ref[...]).astype(BF16)


def after_attend(attended, w_out, x, gain):
    rows, dim = x.shape
    return pl.pallas_call(
        after_attend_kernel,
        out_shape=(jax.ShapeDtypeStruct((rows, dim), F32), jax.ShapeDtypeStruct((rows, dim), BF16)),
        in_specs=[whole()] * 10,
        out_specs=(whole(), whole()),
        compiler_params=params(),
        cost_estimate=COST,
        name="after_attend",
    )(*attended, *w_out, x, gain)


def feed_kernel(meta_ref, x0, x2, x1, x3, cot_ref, *refs, masks, shard):
    count = (len(refs) - 7) // 2
    packed_refs, down_refs = refs[:count], refs[count : 2 * count]
    x_ref, act_ref, d_up_ref, keep_ref, send_ref, down_ref, up_ref = refs[2 * count :]

    def half(first, second, back_ref):
        x = jnp.concatenate([first[...], second[...]], axis=0)
        x_ref[...] = x
        up = mm(x, up_ref[...])
        pos = jnp.maximum(up, 0.0)
        act_ref[...] = (pos * pos).astype(BF16)
        d_act = mm(cot_ref[...], down_ref[...])
        d_up = (d_act * 2.0 * pos).astype(BF16)
        d_up_ref[...] = d_up
        back_ref[...] = mm(d_up, up_ref[...], 1, 1).astype(BF16)

    @pl.when(pl.program_id(0) == 0)
    def _():
        put_rows(up_ref, packed_refs, meta_ref[BLK], masks, shard)
        put_rows(down_ref, down_refs, meta_ref[BLK], masks, shard)
        half(x0, x2, keep_ref)

    @pl.when(pl.program_id(0) == 1)
    def _():
        half(x1, x3, send_ref)


def feed(meta, x, cot, packed, down, masks):
    rows, dim = cot.shape
    shard, units = down[0].shape[1:]
    step = rows // 2
    tile = lambda n: pl.BlockSpec((step, n), lambda i, *_: (i, 0))
    return pl.pallas_call(
        functools.partial(feed_kernel, masks=masks, shard=shard),
        out_shape=(
            jax.ShapeDtypeStruct((rows, dim), BF16),
            jax.ShapeDtypeStruct((rows, units), BF16),
            jax.ShapeDtypeStruct((rows, units), BF16),
            jax.ShapeDtypeStruct((step, dim), BF16),
            jax.ShapeDtypeStruct((step, dim), BF16),
            jax.ShapeDtypeStruct((dim, units), BF16),
        ),
        grid_spec=pltpu.PrefetchScalarGridSpec(
            num_scalar_prefetch=1,
            grid=(2,),
            in_specs=[whole()] * 4 + [tile(dim)] + [whole()] * (len(packed) + len(down)),
            out_specs=(tile(dim), tile(units), tile(units), whole(), whole(), whole()),
            scratch_shapes=[pltpu.VMEM((dim, units), BF16)],
        ),
        compiler_params=params(),
        cost_estimate=COST,
        name="feed",
    )(meta, *x, cot, *packed, *down)


def feed_rest_kernel(x_ref, d_up_ref, cot_ref, act_ref, down_ref, grads_ref, keep_ref, send_ref):
    grads_ref[0] = mm(x_ref[...], d_up_ref[...], 0, 0).astype(BF16)
    grads_ref[1] = mm(cot_ref[...], act_ref[...], 0, 0).astype(BF16)
    out = mm(act_ref[...], down_ref[...], 1, 1).astype(BF16)
    half = out.shape[0] // 2
    keep_ref[...] = out[:half]
    send_ref[...] = out[half:]


def feed_rest(x, d_up, cot, act, w_down_t):
    rows, dim = x.shape
    units = act.shape[1]
    block = pl.BlockSpec((rows, TILE), lambda i: (0, i))
    half = pl.BlockSpec((rows // 2, TILE), lambda i: (0, i))
    return pl.pallas_call(
        feed_rest_kernel,
        out_shape=(
            jax.ShapeDtypeStruct((2, dim, units), BF16),
            jax.ShapeDtypeStruct((rows // 2, dim), BF16),
            jax.ShapeDtypeStruct((rows // 2, dim), BF16),
        ),
        grid=(dim // TILE,),
        in_specs=[block, whole(), block, whole(), pl.BlockSpec((TILE, units), lambda i: (i, 0))],
        out_specs=(pl.BlockSpec((2, TILE, units), lambda i: (0, i, 0)), half, half),
        compiler_params=params(),
        cost_estimate=COST,
        name="feed_rest",
    )(x, d_up, cot, act, w_down_t)


def before_back_kernel(
    s_ref, r_ref, hidden_ref, gain_ref, cot_ref, w0, w1, w2, w3, a0, a1, a2, a3,
    d_hidden_ref, d0, d1, d2, d3, keep_ref, keep_far_ref, send_ref, sum_ref,
):
    d_normed = s_ref[...].astype(F32) + r_ref[...].astype(F32)
    hidden = hidden_ref[...]
    factor = lax.rsqrt(jnp.mean(hidden * hidden, axis=-1, keepdims=True) + EPS)
    unit = hidden * factor
    sum_ref[...] = jnp.sum(d_normed * unit, axis=0, keepdims=True)
    scaled = d_normed * gain_ref[...]
    inner = jnp.mean(scaled * unit, axis=-1, keepdims=True)
    d_hidden = cot_ref[...].astype(F32) + factor * (scaled - unit * inner)
    d_hidden_ref[...] = d_hidden
    d_branch = d_hidden.astype(BF16)
    for w, d in ((w0, d0), (w1, d1), (w2, d2), (w3, d3)):
        d[...] = mm(w[...], d_branch, 1, 1).astype(BF16)
    for a, to in ((a0, keep_ref), (a1, keep_far_ref), (a2, send_ref.at[0]), (a3, send_ref.at[1])):
        to[...] = mm(a[...], d_branch).astype(BF16)


def before_back(chip_sum, far_sum, hidden, gain, cot, w_out, attended):
    rows, dim = hidden.shape
    part = w_out[0].shape[0]
    return pl.pallas_call(
        before_back_kernel,
        out_shape=(
            jax.ShapeDtypeStruct((rows, dim), F32),
            *[jax.ShapeDtypeStruct((part, rows), BF16)] * 4,
            *[jax.ShapeDtypeStruct((part, dim), BF16)] * 2,
            jax.ShapeDtypeStruct((2, part, dim), BF16),
            jax.ShapeDtypeStruct((1, dim), F32),
        ),
        in_specs=[whole()] * 13,
        out_specs=tuple([whole()] * 9),
        compiler_params=params(),
        cost_estimate=COST,
        name="before_back",
    )(chip_sum, far_sum, hidden, gain, cot, *w_out, *attended)


def d_normed_kernel(meta_ref, own_ref, one_ref, halo_ref, two_ref, x_ref, w_ref, keep_ref, send_ref, sum_ref):
    i = pl.program_id(0)
    step = own_ref.shape[0]
    later = jnp.where(meta_ref[NEXT_ONE] == 1, one_ref[...].astype(F32), 0.0)
    later = later + jnp.where(meta_ref[NEXT_TWO] == 1, two_ref[...].astype(F32), 0.0)
    own = own_ref[...].astype(F32)
    queries = own[:, KV:]
    part = queries.shape[1]
    last = (i == pl.num_programs(0) - 1) & (meta_ref[NEXT_ONE] == 1)
    halo = jnp.where(last, halo_ref[...].astype(F32)[:, :part], 0.0)
    queries = queries + jnp.concatenate([jnp.zeros((step - HALO, part), F32), halo], axis=0)
    d_raw = jnp.concatenate([own[:, :KV] + later, queries], axis=1).astype(BF16)
    d_normed = mm(d_raw, w_ref[...], 1, 1)
    for n in range(step // TILE):
        slot = slot_of(i * (step // TILE) + n, meta_ref)
        rows = d_normed[n * TILE : (n + 1) * TILE].astype(BF16)
        to = pl.ds(pl.multiple_of((slot & 1) * TILE, TILE), TILE)

        @pl.when(slot < 2)
        def _(rows=rows, to=to):
            keep_ref[to, :] = rows

        @pl.when(slot >= 2)
        def _(rows=rows, to=to):
            send_ref[to, :] = rows

    x = x_ref[...].astype(F32)
    unit = x * lax.rsqrt(jnp.mean(x * x, axis=-1, keepdims=True) + EPS)

    @pl.when(i == 0)
    def _():
        sum_ref[...] = jnp.zeros_like(sum_ref)

    sum_ref[...] += jnp.sum(d_normed * unit, axis=0, keepdims=True)


def d_normed_parts(meta, own, one, two, x, w):
    rows, dim = x.shape
    width = w.shape[1]
    step = 2 * TILE
    tile = lambda n: pl.BlockSpec((step, n), lambda i, *_: (i, 0))
    return pl.pallas_call(
        d_normed_kernel,
        out_shape=(
            jax.ShapeDtypeStruct((rows // 2, dim), BF16),
            jax.ShapeDtypeStruct((rows // 2, dim), BF16),
            jax.ShapeDtypeStruct((1, dim), F32),
        ),
        grid_spec=pltpu.PrefetchScalarGridSpec(
            num_scalar_prefetch=1,
            grid=(rows // step,),
            in_specs=[
                tile(width),
                tile(KV),
                pl.BlockSpec((HALO, KV), lambda i, *_: (rows // HALO, 0)),
                tile(KV),
                tile(dim),
                whole(),
            ],
            out_specs=(whole(), whole(), pl.BlockSpec((1, dim), lambda i, *_: (0, 0))),
        ),
        compiler_params=params(),
        cost_estimate=COST,
        name="d_normed_parts",
    )(meta, own, one, one, two, x, w)


def grad_tokens_kernel(s_ref, r_ref, x_ref, gain_ref, d_hidden_ref, out_ref):
    d_normed = s_ref[...].astype(F32) + r_ref[...].astype(F32)
    x = x_ref[...].astype(F32)
    factor = lax.rsqrt(jnp.mean(x * x, axis=-1, keepdims=True) + EPS)
    unit = x * factor
    scaled = d_normed * gain_ref[...]
    inner = jnp.mean(scaled * unit, axis=-1, keepdims=True)
    out_ref[...] = (d_hidden_ref[...] + factor * (scaled - unit * inner)).astype(BF16)


def grad_tokens_own(chip_sum, far_sum, x, gain, d_hidden):
    return pl.pallas_call(
        grad_tokens_kernel,
        out_shape=jax.ShapeDtypeStruct(x.shape, BF16),
        in_specs=[whole()] * 5,
        out_specs=whole(),
        compiler_params=params(),
        name="grad_tokens_own",
    )(chip_sum, far_sum, x, gain, d_hidden)


def assemble_kernel(meta_ref, *refs):
    *pieces, out_ref = refs
    for piece, d in zip(pieces, (0, 2, 1, 3)):

        @pl.when(pl.program_id(0) == (meta_ref[0] ^ d))
        def _(piece=piece):
            out_ref[...] = piece[...].astype(out_ref.dtype)


def by_place(meta, pieces, dtype):
    rows, dim = pieces[0].shape
    return pl.pallas_call(
        assemble_kernel,
        out_shape=jax.ShapeDtypeStruct((4 * rows, dim), dtype),
        grid_spec=pltpu.PrefetchScalarGridSpec(
            num_scalar_prefetch=1,
            grid=(4,),
            in_specs=[whole()] * 4,
            out_specs=pl.BlockSpec((rows, dim), lambda i, *_: (i, 0)),
        ),
        compiler_params=params(),
        cost_estimate=COST,
        name="assemble",
    )(meta, *pieces)


def sum_halves(keep, send):
    return (keep.astype(F32) + swap(send, "head", 1).astype(F32)).astype(BF16)


def body(
    tokens,
    seg_ids,
    gain_attn,
    w_query,
    w_key,
    w_value,
    conv_kernels,
    w_out,
    gain_ffn,
    w_up,
    w_down,
    cotangent,
):
    rows, dim = tokens.shape
    part = conv_kernels.shape[2]
    quarter = rows // lax.axis_size("head")
    blk = lax.axis_index("blk")
    head = lax.axis_index("head")
    groups = bit_groups("blk")
    halves = [(bit,) for group in groups[:-1] for bit in group]
    together = lax.optimization_barrier
    own_quarter = lax.dynamic_slice_in_dim(tokens, head * quarter, quarter)
    sent = jnp.concatenate([own_quarter, tokens[rows - HALO :]])
    two = moved(sent, "blk", 2)
    shard, units = w_up.shape
    masks = gathered_masks("blk")
    w_mix = jnp.concatenate([w_query, w_key, w_value], axis=1)
    w_some = sent_round(w_mix, "blk")
    one = swap(jnp.where(bit_of("blk", 0), two, sent), "blk", 1)
    pieces = [*quarters(two), *quarters(one)]
    packed, down_some = pack(w_up, w_out, w_down)
    w_some, packed = together((joined(w_some), packed))
    w_mix = pieces_of(w_some, "blk", shard)
    packed_some = sent_round(packed, "blk")
    span = (REACH + 1) * rows
    padded_ids = jnp.pad(seg_ids, (REACH * rows, 0), constant_values=-1)
    window = lax.dynamic_slice_in_dim(padded_ids, blk * rows, span)
    starts = jnp.sum((window[None, :] <= window[0] + jnp.arange(8)[:, None]).astype(jnp.int32), axis=1)
    place = jnp.arange(REACH * rows, span, dtype=jnp.int32)
    first_row = jnp.max(jnp.where(starts[:, None] <= place, starts[:, None], 0), axis=0)
    low = first_row[::TILE] // TILE
    full = (first_row[TILE - 1 :: TILE] + TILE - 1) // TILE
    last = lax.axis_size("blk") - 1
    exists = jnp.stack([blk >= 1, blk >= 2, blk + 1 <= last, blk + 2 <= last])
    meta = jnp.concatenate([head[None], low, full, starts, exists, blk[None]]).astype(jnp.int32)
    first_row = first_row[None]
    taps = arranged(*conv_kernels)
    gain_one, gain_two = gain_attn[None], gain_ffn[None]

    hi, lo = bit_of("head", 1), bit_of("head", 0)
    cot = cotangent.reshape(2, 2, quarter, dim)
    cot = jnp.where(hi, cot[::-1], cot)
    cot = jnp.where(lo, cot[:, ::-1], cot)
    cot = jnp.swapaxes(cot, 0, 1).reshape(rows, dim)
    *w_mix, cot, pieces[0], pieces[1], pieces[4] = together((*w_mix, cot, pieces[0], pieces[1], pieces[4]))
    w_mix, raw_halo, raw, normed, q, kv, kvt = project_own(meta, tokens, pieces[4], gain_one, taps, w_mix, masks)
    q, pieces[5] = together((q, pieces[5]))
    acc_own, stat_own = attend_own(q, kv, kvt, first_row)
    acc_own, down_some, *packed_some = together((acc_own, down_some, *packed_some))
    packed = pieces_of(joined(packed_some), "blk", shard)
    down_some = sent_round(down_some, "blk")
    raw_e, normed_e, kv_e, kvt_e = project_earlier(meta, pieces, gain_one, w_mix, taps)
    raw_e, *more = together((raw_e, *packed, *down_some))
    packed, down_some = more[: len(packed)], more[len(packed) :]
    down = pieces_of(joined(down_some), "blk", shard)
    out_full = unpack_out(meta, packed, masks, shard, part)
    out_far = swap(out_full, "head", 2)
    out_pieces = [out_full, out_far, swap(out_full, "head", 1), swap(out_far, "head", 1)]
    kv_late, out_full = together((kv_e, out_full))
    att, out_t, lse = attend_earlier(meta, q, kv_late, kvt_e, first_row, acc_own, stat_own)

    near = swap(att[2:], "head", 1)
    across = swap(jnp.stack([att[1], near[1]]), "head", 2)
    attended = (att[0], across[0], near[0], across[1])
    quarter_late, *down = together((own_quarter, *down))
    hidden, normed_two = after_attend(attended, out_pieces, quarter_late, gain_two)
    ffn_in, act, d_up, *back, down_t = feed(meta, quarters(normed_two), cot, packed, down, masks)
    chip_back = sum_halves(*back)
    far_back = swap(chip_back[quarter:], "head", 2)
    feed_grads, *ffn = feed_rest(ffn_in, d_up, cot, act, down_t)
    near_parts = chosen(feed_grads.reshape(2, -1, shard, units), "blk", groups[-1])
    far_back, *near_parts = together((far_back, *near_parts))
    near_parts = received(near_parts, "blk", groups[-1])
    d_hidden, *d_outs, keep_out, keep_far, send_out, gain_two_part = before_back(
        chip_back[:quarter], far_back, hidden, gain_two, cot[:quarter], out_pieces, attended
    )
    across = swap(jnp.stack([d_outs[1], d_outs[3]]), "head", 2)
    near = swap(jnp.stack([d_outs[2], across[1]]), "head", 1)
    d_out_t = jnp.stack([d_outs[0], across[0], near[0], near[1]])
    chip_ffn = sum_halves(*ffn)
    near_out = swap(send_out, "head", 1)
    far_out = swap(total_of([keep_far, near_out[1]]).astype(BF16), "head", 2)
    d_out_t, chip_ffn = together((d_out_t, chip_ffn))
    far_ffn = swap(chip_ffn[quarter:], "head", 2)

    dq_t, d_two, d_one, grad_next, sums_before, sums_halo = earlier_back(
        meta, q, d_out_t, out_t, lse, first_row, kv_e, kvt_e, kv, kvt, raw_e, raw_halo, taps
    )
    from_two = moved(d_two, "blk", -2)
    from_one = moved(d_one, "blk", -1)
    output = (hidden + total_of([chip_ffn[:quarter], far_ffn])).astype(BF16)
    dq_t, output, far_out = together((dq_t, output, far_out))
    output_far = swap(output, "head", 2)
    d_raw, sums_own, grad_mix = own_back(
        meta, q, d_out_t, out_t, lse, first_row, dq_t, kv, kvt, raw, taps, grad_next,
        normed_e, d_two, d_one, normed, keep_out, near_out, far_out,
    )
    mix_parts = chosen(grad_mix.reshape(1, -1, shard, 4 * part), "blk", groups[-1])
    mix_parts = received(mix_parts, "blk", groups[-1])
    output_far, output, d_raw = together((output_far, output, d_raw))
    output = [output, output_far, swap(output, "head", 1), swap(output_far, "head", 1)]
    d_raw, *more = together((d_raw, *output, *near_parts, *mix_parts))
    output, near_parts, mix_parts = more[:4], more[4:6], more[6:]
    *back, gain_one_part = d_normed_parts(meta, d_raw, from_one, from_two, tokens, w_mix)
    near_parts = total_of(near_parts).astype(BF16)
    chip_back = sum_halves(*back)
    gains = jnp.concatenate([gain_two_part, gain_one_part])
    gains = gains + swap(gains, "head", 1)
    chip_back, gains, near_parts, *mix_parts = together((chip_back, gains, near_parts, *mix_parts))
    far_back = swap(chip_back[quarter:], "head", 2)
    up_parts = sum_scatter(near_parts[:1], "blk", halves)
    down_parts = sum_scatter(near_parts[1:], "blk", halves)
    mix_parts = sum_scatter(total_of(mix_parts).astype(BF16), "blk", halves)
    far_back, far_gains = together((far_back, swap(gains, "head", 2)))
    grad_tokens = grad_tokens_own(chip_back[:quarter], far_back, own_quarter, gain_one, d_hidden)
    grad_tokens, far_gains = together((grad_tokens, far_gains))
    gains = gains + far_gains
    grad_far = swap(grad_tokens, "head", 2)
    grad_far, output[0], *more = together((grad_far, output[0], *up_parts, *down_parts, *mix_parts))
    up_parts, down_parts, mix_parts = more[:2], more[2:4], more[4:]
    grad_tokens = [grad_tokens, grad_far, swap(grad_tokens, "head", 1), swap(grad_far, "head", 1)]
    grad_tokens = by_place(meta, grad_tokens, F32)

    output = by_place(meta, output, BF16)
    grad_up_shard = total_of(up_parts).reshape(shard, units)
    grad_down_shard = total_of(down_parts).reshape(shard, units).T
    mix_shard = total_of(mix_parts).reshape(shard, 4 * part)
    grad_query_shard, grad_key_shard, grad_value_shard = separated(mix_shard[:, : 3 * part])
    grad_out_shard = mix_shard[:, 3 * part :].T

    taps_part = jnp.concatenate([sums_own[:3, :KV] + sums_before[:3], sums_own[:3, KV:] + sums_halo[:3]], axis=1)
    taps_part = jnp.stack(separated(taps_part)).reshape(-1)
    small = jnp.concatenate([gains.reshape(-1), taps_part])
    small = sum_everywhere(small, "blk", groups)
    grad_gain_ffn, grad_gain_attn = small[:dim], small[dim : 2 * dim]
    grad_kernels = small[2 * dim :].reshape(3, 3, part)
    return (
        output,
        grad_tokens,
        grad_gain_attn,
        grad_query_shard,
        grad_key_shard,
        grad_value_shard,
        grad_kernels,
        grad_out_shard,
        grad_gain_ffn,
        grad_up_shard,
        grad_down_shard,
    )


def solution(mesh):
    return jax.shard_map(
        body,
        mesh=mesh,
        in_specs=(
            P("blk", None),
            P(),
            P(),
            P("blk", "head"),
            P("blk", "head"),
            P("blk", "head"),
            P(None, None, "head"),
            P("head", "blk"),
            P(),
            P("blk", "head"),
            P("head", "blk"),
            P("blk", None),
        ),
        out_specs=(
            P("blk", None),
            P("blk", None),
            P(),
            P("blk", "head"),
            P("blk", "head"),
            P("blk", "head"),
            P(None, None, "head"),
            P("head", "blk"),
            P(),
            P("blk", "head"),
            P("head", "blk"),
        ),
        check_vma=False,
    )
```

```python
import functools

import jax
import jax.numpy as jnp
from jax import lax
from jax.experimental import pallas as pl
from jax.experimental.pallas import tpu as pltpu
from jax.sharding import PartitionSpec as P

DH = 64
REACH = 2
EPS = 1e-06
MASKED = -1e30
TILE = 256
HALO = 16
F32 = jnp.float32
BF16 = jnp.bfloat16
MIB = 1024 * 1024
COST = pl.CostEstimate(flops=1, bytes_accessed=1, transcendentals=0)


def params(mib=20):
    return pltpu.CompilerParams(vmem_limit_bytes=mib * MIB)


def whole():
    return pl.BlockSpec(memory_space=pltpu.VMEM)


def mm(a, b, ca=1, cb=0):
    return lax.dot_general(a, b, (((ca,), (cb,)), ((), ())), preferred_element_type=F32)


def swap(x, axis, mask):
    return lax.ppermute(x, axis, [(i, i ^ mask) for i in range(lax.axis_size(axis))])


def moved(x, axis, distance):
    size = lax.axis_size(axis)
    return lax.ppermute(x, axis, [(i, i + distance) for i in range(size) if 0 <= i + distance < size])


def bit_groups(axis):
    bits = list(range(lax.axis_size(axis).bit_length() - 2, -1, -1))
    upper, groups = bits[:-1], []
    while upper:
        groups.append(tuple(upper[:2]))
        upper = upper[2:]
    return groups + [(0,)]


def bit_of(axis, bit):
    return ((lax.axis_index(axis) >> bit) & 1) == 1


def masks_of(group):
    if len(group) == 1:
        return [0, 1 << group[0]]
    hi, lo = 1 << group[0], 1 << group[1]
    return [0, lo, hi, hi | lo]


def sent_round(shard, axis):
    pieces = [shard[None]]
    for group in bit_groups(axis)[:-1]:
        out = jnp.concatenate(pieces)
        pieces = [out] + [swap(out, axis, m) for m in masks_of(group)[1:]]
    return pieces


def gathered_masks(axis):
    masks = [0]
    *groups, last = bit_groups(axis)
    for group in groups:
        masks = [m ^ old for m in masks_of(group) for old in masks]
    return masks, [m ^ masks_of(last)[1] for m in masks]


def joined_kernel(*refs):
    *pieces, out_ref = refs
    at = 0
    for piece in pieces:
        for n in range(piece.shape[0]):
            out_ref[at] = piece[n]
            at += 1


def joined(pieces):
    count = sum(piece.shape[0] for piece in pieces)
    return pl.pallas_call(
        joined_kernel,
        out_shape=jax.ShapeDtypeStruct((count, *pieces[0].shape[1:]), pieces[0].dtype),
        in_specs=[whole()] * len(pieces),
        out_specs=whole(),
        compiler_params=params(),
        cost_estimate=COST,
        name="joined",
    )(*pieces)


def pieces_of(own, axis, shard):
    other = swap(own, axis, 1)
    if shard % 16 == 0:
        return own, other
    size = lax.axis_size(axis)
    masks = sum(gathered_masks(axis), [])
    both = jnp.concatenate([own, other])
    place = lax.axis_index(axis) ^ jnp.array(masks)
    return (jnp.zeros_like(both).at[place].set(both),)


def put_rows(to_ref, refs, blk, axis_masks, shard):
    if len(refs) == 1:
        for n in range(refs[0].shape[0]):
            to_ref[n * shard : (n + 1) * shard, :] = refs[0][n, :shard, :].astype(to_ref.dtype)
        return
    for ref, masks in zip(refs, axis_masks):
        for n, mask in enumerate(masks):
            to = pl.ds(pl.multiple_of((blk ^ mask) * shard, 16), shard)
            to_ref[to, :] = ref[n, :shard, :].astype(to_ref.dtype)


def chosen(full, axis, group):
    r = 1 << len(group)
    out = full.reshape(full.shape[0], -1, r, *full.shape[2:])
    mine = (lax.axis_index(axis) >> group[-1]) & (r - 1)
    return [lax.dynamic_index_in_dim(out, mine ^ (m >> group[-1]), 2, keepdims=False) for m in masks_of(group)]


def received(parts, axis, group):
    keep, *send = parts
    return [keep] + [swap(part, axis, m) for m, part in zip(masks_of(group)[1:], send)]


def total_of(parts):
    total = parts[0].astype(F32)
    for part in parts[1:]:
        total = total + part.astype(F32)
    return total


def sum_scatter(full, axis, groups):
    *rest, last = reversed(groups)
    out = full
    for group in rest:
        out = total_of(received(chosen(out, axis, group), axis, group)).astype(BF16)
    return received(chosen(out, axis, last), axis, last)


def sum_everywhere(x, axis, groups):
    for group in groups:
        x = total_of([x] + [swap(x, axis, m) for m in masks_of(group)[1:]])
    return x


def quarters(own):
    far = swap(own, "head", 2)
    return own, far, swap(own, "head", 1), swap(far, "head", 1)


PAIR = 2 * DH
KV = 3 * PAIR
KEY_LANES = ((0, PAIR), (0, PAIR), (2 * PAIR, KV))
VALUE_LANES = ((PAIR, 2 * PAIR), (PAIR, 2 * PAIR), (2 * PAIR, KV))
KEY_ROWS = (0, DH, 2 * PAIR)
VALUE_ROWS = (PAIR, PAIR + DH, 2 * PAIR + DH)


def arranged(q, k, v):
    return jnp.concatenate([k[..., :PAIR], v[..., :PAIR], k[..., PAIR:], v[..., PAIR:], q], axis=-1)


def separated(x):
    k = jnp.concatenate([x[..., :PAIR], x[..., 2 * PAIR : 2 * PAIR + DH]], axis=-1)
    v = jnp.concatenate([x[..., PAIR : 2 * PAIR], x[..., 2 * PAIR + DH : KV]], axis=-1)
    return x[..., KV:], k, v


def pack_kernel(up_ref, out_ref, down_ref, packed_ref, down_t_ref):
    shard, units = up_ref.shape
    out_t = out_ref[...].astype(F32).T
    few = packed_ref.shape[0] - shard
    packed_ref[0:shard, :] = up_ref[...]
    out_t = jnp.concatenate([out_t[n : n + few] for n in range(0, shard, few)], axis=1)
    packed_ref[shard:, :] = out_t.astype(BF16)
    down_t_ref[...] = down_ref[...].astype(F32).T.astype(BF16)


def pack(w_up, w_out, w_down):
    shard, units = w_up.shape
    part = w_out.shape[0]
    return pl.pallas_call(
        pack_kernel,
        out_shape=(
            jax.ShapeDtypeStruct((shard + shard * part // units, units), BF16),
            jax.ShapeDtypeStruct((shard, units), BF16),
        ),
        in_specs=[whole()] * 3,
        out_specs=(whole(), whole()),
        compiler_params=params(),
        cost_estimate=COST,
        name="pack",
    )(w_up, w_out, w_down)


def unpack_out_kernel(meta_ref, *refs, masks, shard):
    *packed_refs, out_ref, out_t_ref = refs
    few = packed_refs[0].shape[1] - shard
    part = out_t_ref.shape[1]

    def put(ref, n, place):
        rows = ref[n].astype(F32)[shard:]
        for k in range(shard // few):
            to = pl.ds(place * shard + k * few, few)
            out_t_ref[to, :] = rows[:, k * part : (k + 1) * part]

    if len(packed_refs) == 1:
        for n in range(packed_refs[0].shape[0]):
            put(packed_refs[0], n, n)
    else:
        for ref, distances in zip(packed_refs, masks):
            for n, mask in enumerate(distances):
                put(ref, n, meta_ref[BLK] ^ mask)
    out_ref[...] = out_t_ref[...].T.astype(BF16)


def unpack_out(meta, packed, masks, shard, part):
    dim = shard * sum(x.shape[0] for x in packed)
    return pl.pallas_call(
        functools.partial(unpack_out_kernel, masks=masks, shard=shard),
        out_shape=jax.ShapeDtypeStruct((part, dim), BF16),
        in_specs=[pl.BlockSpec(memory_space=pltpu.SMEM), *[whole()] * len(packed)],
        out_specs=whole(),
        scratch_shapes=[pltpu.VMEM((dim, part), F32)],
        compiler_params=params(),
        cost_estimate=COST,
        name="unpack_out",
    )(meta, *packed)


def unit_times_gain(x, gain):
    return x * lax.rsqrt(jnp.mean(x * x, axis=-1, keepdims=True) + EPS) * gain


def mix_rows(buf_ref, mix_ref, taps, starts, base, rows):
    mix_ref[...] = (
        taps[0:1] * buf_ref[8 : 8 + rows, :]
        + taps[1:2] * buf_ref[7 : 7 + rows, :]
        + taps[2:3] * buf_ref[6 : 6 + rows, :]
    )
    for start in starts:
        r = start - base

        @pl.when((r >= 0) & (r < rows))
        def _(r=r):
            mix_ref[pl.ds(r, 1), :] = taps[0:1] * buf_ref[pl.ds(8 + r, 1), :]

        @pl.when((r + 1 >= 0) & (r + 1 < rows))
        def _(r=r):
            mix_ref[pl.ds(r + 1, 1), :] = (
                taps[0:1] * buf_ref[pl.ds(9 + r, 1), :] + taps[1:2] * buf_ref[pl.ds(8 + r, 1), :]
            )


def project_own_kernel(
    meta_ref, x_ref, halo_ref, gain_ref, taps_ref, *refs, base, masks, shard,
):
    *w_refs, w_ref, raw_halo_ref, raw_ref, normed_ref, q_ref, kv_ref, kvt_ref, buf_ref, mix_ref, w_in_ref = refs
    i = pl.program_id(0)
    rows = x_ref.shape[0]
    gain = gain_ref[...]

    @pl.when(i == 0)
    def _():
        put_rows(w_in_ref, w_refs, meta_ref[BLK], masks, shard)
        w_in = w_in_ref[...]
        part = w_in.shape[1] // 3
        w_ref[...] = arranged(w_in[:, :part], w_in[:, part : 2 * part], w_in[:, 2 * part : 3 * part])

    w = w_ref[...]

    @pl.when(i == 0)
    def _():
        halo = halo_ref[halo_ref.shape[0] - HALO :, :].astype(F32)
        halo = jnp.where(meta_ref[HAS_ONE] == 1, halo, 0.0)
        normed = unit_times_gain(halo, gain).astype(BF16)
        raw_low = mm(normed, w).astype(BF16)
        raw_halo_ref[...] = raw_low[:, KV:]
        buf_ref[0:8, :] = raw_low.astype(F32)[HALO - 8 :, :]

    normed = unit_times_gain(x_ref[...].astype(F32), gain).astype(BF16)
    raw_low = mm(normed, w).astype(BF16)
    normed_ref[...] = normed
    raw_ref[...] = raw_low
    raw = raw_low.astype(F32)
    buf_ref[8 : 8 + rows, :] = raw
    mix_rows(buf_ref, mix_ref, taps_ref[...], [meta_ref[STARTS + n] for n in range(8)], base + i * rows, rows)
    buf_ref[0:8, :] = raw[rows - 8 :, :]
    q_ref[...] = mix_ref[:, KV:].astype(BF16)
    kv = mix_ref[:, :KV]
    kv_ref[...] = kv.astype(BF16)
    kvt_ref[...] = kv.T.astype(BF16)


def project_own(meta, tokens, halo, gain, taps, w, masks):
    rows, dim = tokens.shape
    shard, width = w[0].shape[1:]
    step = 2 * TILE
    tile = lambda n: pl.BlockSpec((step, n), lambda i, *_: (i, 0))
    return pl.pallas_call(
        functools.partial(project_own_kernel, base=REACH * rows, masks=masks, shard=shard),
        out_shape=(
            jax.ShapeDtypeStruct((dim, width), BF16),
            jax.ShapeDtypeStruct((HALO, width - KV), BF16),
            jax.ShapeDtypeStruct((rows, width), BF16),
            jax.ShapeDtypeStruct((rows, dim), BF16),
            jax.ShapeDtypeStruct((rows, width - KV), BF16),
            jax.ShapeDtypeStruct((rows, KV), BF16),
            jax.ShapeDtypeStruct((KV, rows), BF16),
        ),
        grid_spec=pltpu.PrefetchScalarGridSpec(
            num_scalar_prefetch=1,
            grid=(rows // step,),
            in_specs=[tile(dim), whole(), whole(), whole(), *[whole()] * len(w)],
            out_specs=(
                whole(),
                whole(),
                tile(width),
                tile(dim),
                tile(width - KV),
                tile(KV),
                pl.BlockSpec((KV, step), lambda i, *_: (0, i)),
            ),
            scratch_shapes=[
                pltpu.VMEM((8 + step, width), F32),
                pltpu.VMEM((step, width), F32),
                pltpu.VMEM((dim, width), BF16),
            ],
        ),
        compiler_params=params(),
        cost_estimate=COST,
        name="project_own",
    )(meta, tokens, halo, gain, taps, *w)


def project_earlier_kernel(meta_ref, *refs):
    pieces = refs[:8]
    gain_ref, w_ref, taps_ref, raw_ref, normed_ref, kv_ref, kvt_ref, x_ref, buf_ref, mix_ref = refs[8:]
    i = pl.program_id(0)
    rows = x_ref.shape[0]
    quarter = rows // 2

    @pl.when(i == 0)
    def _():
        buf_ref[0:8, :] = jnp.zeros((8, KV), F32)

    for hop in range(REACH):
        for slot, d in enumerate((0, 2, 1, 3)):
            place = 4 * hop + (meta_ref[0] ^ d)

            @pl.when(i == place >> 1)
            def _(piece=pieces[4 * hop + slot], place=place):
                x_ref[pl.ds(pl.multiple_of((place & 1) * quarter, quarter), quarter), :] = piece[:quarter, :]

    exists = jnp.where(i < pl.num_programs(0) // REACH, meta_ref[HAS_TWO], meta_ref[HAS_ONE])
    x = jnp.where(exists == 1, x_ref[...].astype(F32), 0.0)
    normed = unit_times_gain(x, gain_ref[...]).astype(BF16)
    normed_ref[...] = normed
    raw_low = mm(normed, w_ref[:, :KV]).astype(BF16)
    raw_ref[...] = raw_low
    raw = raw_low.astype(F32)
    buf_ref[8 : 8 + rows, :] = raw
    mix_rows(buf_ref, mix_ref, taps_ref[:, :KV], [meta_ref[STARTS + n] for n in range(8)], i * rows, rows)
    buf_ref[0:8, :] = raw[rows - 8 :, :]
    kv = mix_ref[...]
    kv_ref[...] = kv.astype(BF16)
    kvt_ref[...] = kv.T.astype(BF16)


def project_earlier(meta, pieces, gain, w, taps):
    dim = pieces[0].shape[1]
    quarter = pieces[0].shape[0] - HALO
    step = 2 * quarter
    span = len(pieces) * quarter
    tile = lambda n: pl.BlockSpec((step, n), lambda i, *_: (i, 0))
    return pl.pallas_call(
        project_earlier_kernel,
        out_shape=(
            jax.ShapeDtypeStruct((span, KV), BF16),
            jax.ShapeDtypeStruct((span, dim), BF16),
            jax.ShapeDtypeStruct((span, KV), BF16),
            jax.ShapeDtypeStruct((KV, span), BF16),
        ),
        grid_spec=pltpu.PrefetchScalarGridSpec(
            num_scalar_prefetch=1,
            grid=(span // step,),
            in_specs=[whole()] * 11,
            out_specs=(tile(KV), tile(dim), tile(KV), pl.BlockSpec((KV, step), lambda i, *_: (0, i))),
            scratch_shapes=[
                pltpu.VMEM((step, dim), BF16),
                pltpu.VMEM((8 + step, KV), F32),
                pltpu.VMEM((step, KV), F32),
            ],
        ),
        compiler_params=params(),
        cost_estimate=COST,
        name="project_earlier",
    )(meta, *pieces, gain, w, taps)


LOW, FULL, STARTS = 1, 5, 9
HAS_ONE, HAS_TWO, NEXT_ONE, NEXT_TWO, BLK = 17, 18, 19, 20, 21


STEP = 2 * TILE


def masked_scores(scores, key_base, query_base, first, diagonal):
    keys = lax.broadcasted_iota(jnp.int32, scores.shape, 0)
    allowed = keys >= first - key_base
    if diagonal is not None:
        allowed = allowed & (keys <= lax.broadcasted_iota(jnp.int32, scores.shape, 1) + (query_base - diagonal))
    return jnp.where(allowed, scores, MASKED)


def place_heads(to_ref, lanes, across, halves):
    zero = jnp.zeros((DH, across.shape[1]), to_ref.dtype)
    for h, half in enumerate(halves):
        to_ref[h, half * DH : (half + 1) * DH, lanes] = across[h * DH : (h + 1) * DH].astype(to_ref.dtype)
        to_ref[h, (1 - half) * DH : (2 - half) * DH, lanes] = zero


KEY_HALVES, VALUE_HALVES = (0, 1, 0), (0, 1, 1)


def eights(x, how):
    return how(x.reshape(x.shape[0] // 8, 8, x.shape[1]), axis=0)


def query_tiles(rows):
    return [slice(n, n + TILE) for n in range(0, rows, TILE)]


def staged(items, first, second, depth=2):
    waiting = []
    for item in items:
        waiting.append((item, first(item)))
        if len(waiting) > depth:
            second(*waiting.pop(0))
    for pair in waiting:
        second(*pair)


def attend_tiles(steps, q_ref, kv_ref, kvt_ref, first_ref, acc_ref, q_across_ref, top_ref, sum_ref):
    for lanes in query_tiles(q_ref.shape[0]):
        place_heads(q_across_ref, lanes, (q_ref[lanes, :].astype(F32) * (DH**-0.5)).T, KEY_HALVES)
    acc_ref[...] = jnp.zeros_like(acc_ref)
    top_ref[...] = jnp.full(top_ref.shape, MASKED, F32)
    sum_ref[...] = jnp.zeros_like(sum_ref)

    def run(row, keys, window_row, begin, masked, diagonal):
        at = pl.ds(row, keys)
        items = [(h, lanes) for h in range(3) for lanes in query_tiles(q_ref.shape[0])[begin // TILE :]]
        key_rows = [kv_ref[at, KEY_LANES[h][0] : KEY_LANES[h][1]] for h in range(3)]
        values = [kvt_ref[VALUE_ROWS[h] : VALUE_ROWS[h] + DH, at] for h in range(3)]
        queries = [q_across_ref[h, :, lanes] for h, lanes in items]
        tops = [top_ref[h : h + 1, lanes] for h, lanes in items]
        firsts = {lanes.start: first_ref[:, lanes] for _, lanes in items}
        results = []

        def first(n):
            h, lanes = items[n]
            scores = mm(key_rows[h], queries[n])
            if masked:
                scores = masked_scores(scores, window_row, lanes.start, firsts[lanes.start], diagonal)
            return scores

        def second(n, scores):
            h, lanes = items[n]
            top = jnp.maximum(tops[n], jnp.max(eights(scores, jnp.max), axis=0, keepdims=True))
            weights = jnp.exp(scores - top)
            total = jnp.sum(eights(weights, jnp.sum), axis=0, keepdims=True)
            results.append((top, total, mm(values[h], weights.astype(BF16))))

        staged(range(len(items)), first, second)
        for n, (h, lanes) in enumerate(items):
            top, total, out = results[n]
            fade = jnp.exp(tops[n] - top)
            top_ref[h : h + 1, lanes] = top
            sum_ref[h : h + 1, lanes] = sum_ref[h : h + 1, lanes] * fade + total
            rows = slice(h * DH, (h + 1) * DH)
            acc_ref[rows, lanes] = acc_ref[rows, lanes] * fade + out

    steps(run)


def earlier_steps(meta_ref, before, rows):
    last = rows // TILE - 1
    end = before // STEP
    low = meta_ref[LOW] // (STEP // TILE)
    full = (meta_ref[FULL + last] + STEP // TILE - 1) // (STEP // TILE)
    middle = jnp.clip(full, low, jnp.maximum(end, low))

    def steps(run):
        def one(masked):
            def step(n, carry):
                row = pl.multiple_of(n * STEP, STEP)
                run(row, STEP, row, 0, masked, None)
                return carry

            return step

        lax.fori_loop(low, middle, one(True), 0)
        lax.fori_loop(middle, end, one(False), 0)

    return steps


def attend_own_kernel(q_ref, kv_ref, kvt_ref, first_ref, acc_ref, stat_ref, q_across_ref, *, base):
    rows = q_ref.shape[0]

    def steps(run):
        for row in range(0, rows, STEP):
            run(row, STEP, base + row, row, True, row)

    top_ref, sum_ref = stat_ref.at[0:8], stat_ref.at[8:16]
    attend_tiles(steps, q_ref, kv_ref, kvt_ref, first_ref, acc_ref, q_across_ref, top_ref, sum_ref)


def attend_earlier_kernel(
    meta_ref, q_ref, kv_ref, kvt_ref, first_ref, acc_own_ref, stat_own_ref,
    att_ref, ot_ref, lse_ref, q_across_ref, top_ref, sum_ref,
):
    rows = q_ref.shape[0]
    steps = earlier_steps(meta_ref, kv_ref.shape[0], rows)
    attend_tiles(steps, q_ref, kv_ref, kvt_ref, first_ref, ot_ref, q_across_ref, top_ref, sum_ref)
    for h in range(3):
        to = slice(h * DH, (h + 1) * DH)
        top_here, top_own = top_ref[h : h + 1, :], stat_own_ref[h : h + 1, :]
        top = jnp.maximum(top_here, top_own)
        here, own = jnp.exp(top_here - top), jnp.exp(top_own - top)
        total = here * sum_ref[h : h + 1, :] + own * stat_own_ref[8 + h : 9 + h, :]
        out = ot_ref[to, :] * (here / total) + acc_own_ref[to, :] * (own / total)
        ot_ref[to, :] = out
        lse_ref[h : h + 1, :] = top + jnp.log(total)
        for n, lanes in enumerate(query_tiles(rows)):
            att_ref[slot_of(n, meta_ref), to, :] = out[:, lanes].astype(BF16)


def slot_of(i, meta):
    d = i ^ meta[0]
    return (d >> 1) | ((d & 1) << 1)


def attend_own(q, kv, kvt, first_row):
    rows, part = q.shape
    return pl.pallas_call(
        functools.partial(attend_own_kernel, base=REACH * rows),
        out_shape=(jax.ShapeDtypeStruct((part, rows), F32), jax.ShapeDtypeStruct((16, rows), F32)),
        in_specs=[whole()] * 4,
        out_specs=(whole(), whole()),
        scratch_shapes=[pltpu.VMEM((3, PAIR, rows), BF16)],
        compiler_params=params(),
        cost_estimate=COST,
        name="attend_own",
    )(q, kv, kvt, first_row)


def attend_earlier(meta, q, kv, kvt, first_row, acc_own, stat_own):
    rows, part = q.shape
    return pl.pallas_call(
        attend_earlier_kernel,
        out_shape=(
            jax.ShapeDtypeStruct((rows // TILE, part, TILE), BF16),
            jax.ShapeDtypeStruct((part, rows), F32),
            jax.ShapeDtypeStruct((8, rows), F32),
        ),
        in_specs=[pl.BlockSpec(memory_space=pltpu.SMEM)] + [whole()] * 6,
        out_specs=(whole(), whole(), whole()),
        scratch_shapes=[
            pltpu.VMEM((3, PAIR, rows), BF16),
            pltpu.VMEM((8, rows), F32),
            pltpu.VMEM((8, rows), F32),
        ],
        compiler_params=params(),
        cost_estimate=COST,
        name="attend_earlier",
    )(meta, q, kv, kvt, first_row, acc_own, stat_own)


def back_scratch(rows):
    return [
        pltpu.VMEM((3, PAIR, rows), BF16),
        pltpu.VMEM((3, PAIR, rows), BF16),
        pltpu.VMEM((3, rows, PAIR), BF16),
        pltpu.VMEM((3, rows, PAIR), BF16),
        pltpu.VMEM((8, rows), F32),
        pltpu.VMEM((3, STEP, rows), BF16),
        pltpu.VMEM((3, STEP, rows), BF16),
    ]


def back_prepare(meta_ref, q_ref, dt_ref, ot_ref, scratch):
    q_across_ref, d_across_ref, q_alone_ref, d_alone_ref, delta_ref = scratch[:5]
    lane = lax.broadcasted_iota(jnp.int32, (TILE, PAIR), 1)
    none = jnp.zeros((TILE, PAIR), BF16)

    def alone(to_ref, rows, x, halves):
        last = jnp.concatenate([x[:, PAIR:]] * 2, axis=1)
        for h, half in enumerate(halves):
            to_ref[h, rows, :] = jnp.where((lane < DH) == (half == 0), x[:, :PAIR] if h < 2 else last, none)

    for n, rows in enumerate(query_tiles(q_ref.shape[0])):
        scaled = q_ref[rows, :].astype(F32) * (DH**-0.5)
        place_heads(q_across_ref, rows, scaled.T, KEY_HALVES)
        alone(q_alone_ref, rows, scaled.astype(BF16), KEY_HALVES)
        d_wide = dt_ref[slot_of(n, meta_ref)].astype(F32)
        place_heads(d_across_ref, rows, d_wide, VALUE_HALVES)
        alone(d_alone_ref, rows, d_wide.T.astype(BF16), VALUE_HALVES)
        terms = d_wide * ot_ref[:, rows]
        for h in range(3):
            delta_ref[h : h + 1, rows] = jnp.sum(terms[h * DH : (h + 1) * DH], axis=0, keepdims=True)


def back_step(row, keys, window_row, begin, masked, diagonal, kv_ref, kvt_ref, lse_ref, first_ref, grad_ref, lead, dq_ref, scratch):
    q_across_ref, d_across_ref, q_alone_ref, d_alone_ref, delta_ref, p_ref, ds_ref = scratch
    rows = dq_ref.shape[1]
    at = pl.ds(row, keys)
    items = [(h, lanes) for h in range(3) for lanes in query_tiles(rows)[begin // TILE :]]
    key_rows = [kv_ref[at, KEY_LANES[h][0] : KEY_LANES[h][1]] for h in range(3)]
    value_rows = [kv_ref[at, VALUE_LANES[h][0] : VALUE_LANES[h][1]] for h in range(3)]
    keys_t = [kvt_ref[KEY_ROWS[h] : KEY_ROWS[h] + DH, at] for h in range(3)]
    queries = [q_across_ref[h, :, lanes] for h, lanes in items]
    d_outs = [d_across_ref[h, :, lanes] for h, lanes in items]
    lses = [lse_ref[h : h + 1, lanes] for h, lanes in items]
    deltas = [delta_ref[h : h + 1, lanes] for h, lanes in items]
    firsts = {lanes.start: first_ref[:, lanes] for _, lanes in items}
    results = []

    def first(n):
        h, lanes = items[n]
        scores = mm(key_rows[h], queries[n])
        if masked:
            scores = masked_scores(scores, window_row, lanes.start, firsts[lanes.start], diagonal)
        return scores, mm(value_rows[h], d_outs[n])

    def second(n, both):
        h, lanes = items[n]
        scores, d_probs = both
        probs = jnp.exp(scores - lses[n])
        d_scores = (probs * (d_probs - deltas[n])).astype(BF16)
        p_ref[h, :keys, lanes] = probs.astype(BF16)
        ds_ref[h, :keys, lanes] = d_scores
        results.append(mm(keys_t[h], d_scores))

    staged(range(len(items)), first, second, 1)
    for n, (h, lanes) in enumerate(items):
        dq_ref[h * DH : (h + 1) * DH, lanes] += results[n]
    seen = slice(begin, rows)
    to = pl.ds(pl.multiple_of(lead + row, 8), keys)
    terms = (
        ((ds_ref, q_alone_ref, 0), (ds_ref, q_alone_ref, 1)),
        ((p_ref, d_alone_ref, 0), (p_ref, d_alone_ref, 1)),
        ((ds_ref, q_alone_ref, 2), (p_ref, d_alone_ref, 2)),
    )
    for n, ((left_a, right_a, a), (left_b, right_b, b)) in enumerate(terms):
        lanes = slice(n * PAIR, (n + 1) * PAIR)
        grad_ref[to, lanes] += mm(left_a[a, :keys, seen], right_a[a, seen, :]) + mm(
            left_b[b, :keys, seen], right_b[b, seen, :]
        )


def unmix_rows(grad_ref, raw_ref, fix_ref, taps, starts, rows, sums_ref):
    width = grad_ref.shape[1]

    def raw_row(r):
        group = raw_ref[pl.ds(pl.multiple_of((r // HALO) * HALO, HALO), HALO), :].astype(F32)
        row = lax.broadcasted_iota(jnp.int32, group.shape, 0)
        return jnp.sum(jnp.where(row == r % HALO, group, 0.0), axis=0, keepdims=True)

    sums_ref[...] = jnp.zeros_like(sums_ref)
    inside = [(s >= 1) & (s <= rows + 1) for s in starts]
    for n, s in enumerate(starts):

        @pl.when(inside[n])
        def _(n=n, s=s):
            one_before = grad_ref[pl.ds(7 + s, 1), :]
            fix_ref[2 * n : 2 * n + 1, :] = taps[0:1] * one_before
            fix_ref[2 * n + 1 : 2 * n + 2, :] = taps[0:1] * grad_ref[pl.ds(6 + s, 1), :] + taps[1:2] * one_before
            here = grad_ref[pl.ds(8 + s, 1), :]

            @pl.when(s >= 2)
            def _():
                sums_ref[2:3, :] -= raw_row(jnp.maximum(s - 2, 0)) * here

            @pl.when(s <= rows)
            def _():
                raw_one = raw_row(s - 1)
                sums_ref[1:2, :] -= raw_one * here
                following = starts[n + 1] if n + 1 < len(starts) else s + 2

                @pl.when(following != s + 1)
                def _():
                    sums_ref[2:3, :] -= raw_one * grad_ref[pl.ds(9 + s, 1), :]

    sizes = [HALO] * (1 if rows % TILE else 0) + [TILE] * (rows // TILE)
    lo = 0
    totals = [jnp.zeros((8, width), F32) for _ in range(3)]
    for size in sizes:
        now = grad_ref[8 + lo : 8 + lo + size, :]
        one = grad_ref[9 + lo : 9 + lo + size, :]
        two = grad_ref[10 + lo : 10 + lo + size, :]
        raw = raw_ref[lo : lo + size, :].astype(F32)
        for j, shifted in enumerate((now, one, two)):
            totals[j] = totals[j] + eights(raw * shifted, jnp.sum)
        grad_ref[8 + lo : 8 + lo + size, :] = taps[0:1] * now + taps[1:2] * one + taps[2:3] * two
        lo += size
    for j in range(3):
        sums_ref[j : j + 1, :] += jnp.sum(totals[j], axis=0, keepdims=True)
    for n in reversed(range(len(starts))):

        @pl.when(inside[n])
        def _(n=n, s=starts[n]):
            grad_ref[pl.ds(7 + s, 1), :] = fix_ref[2 * n : 2 * n + 1, :]
            grad_ref[pl.ds(6 + s, 1), :] = fix_ref[2 * n + 1 : 2 * n + 2, :]


def earlier_back_kernel(
    meta_ref, q_ref, dt_ref, ot_ref, lse_ref, first_ref, kv_ref, kvt_ref, kv_own_ref, kvt_own_ref, raw_ref,
    raw_halo_ref, taps_ref, dq_ref, two_ref, one_ref, next_ref, sums_ref, sums_q_ref,
    grad_ref, grad_q_ref, fix_ref, fix_q_ref, *scratch,
):
    before = kv_ref.shape[0]
    rows = q_ref.shape[0]
    grad_ref[...] = jnp.zeros_like(grad_ref)
    grad_q_ref[...] = jnp.zeros_like(grad_q_ref)
    dq_ref[...] = jnp.zeros_like(dq_ref)
    back_prepare(meta_ref, q_ref, dt_ref, ot_ref, scratch)
    run = lambda *step: back_step(*step, kv_ref, kvt_ref, lse_ref, first_ref, grad_ref, 8, dq_ref, scratch)
    earlier_steps(meta_ref, before, rows)(run)
    back_step(
        0, TILE, before, 0, True, 0, kv_own_ref, kvt_own_ref, lse_ref, first_ref, grad_ref, 8 + before, dq_ref, scratch
    )
    grad_q_ref[8 + HALO : 16 + HALO, :] = dq_ref[:, :PAIR].T[:8] * (DH**-0.5)
    starts = [meta_ref[STARTS + n] for n in range(8)]
    next_ref[...] = grad_ref[8 + before : 8 + before + TILE, :]
    unmix_rows(grad_ref, raw_ref, fix_ref, taps_ref[:, :KV], starts, before, sums_ref)
    starts = [s - (before - HALO) for s in starts]
    unmix_rows(grad_q_ref, raw_halo_ref, fix_q_ref, taps_ref[:, KV:], starts, HALO, sums_q_ref)
    half = before // 2
    two_ref[...] = grad_ref[8 : 8 + half, :].astype(BF16)
    one_ref[0:half, :] = grad_ref[8 + half : 8 + before, :].astype(BF16)
    queries = grad_q_ref[8 : 8 + HALO, :]
    one_ref[half : half + HALO, :] = jnp.concatenate([queries, jnp.zeros_like(queries)], axis=1).astype(BF16)


def earlier_back(meta, q, d_out_t, out_t, lse, first_row, kv, kvt, kv_own, kvt_own, raw, raw_halo, taps):
    rows, part = q.shape
    before = kv.shape[0]
    return pl.pallas_call(
        earlier_back_kernel,
        out_shape=(
            jax.ShapeDtypeStruct((part, rows), F32),
            jax.ShapeDtypeStruct((rows, KV), BF16),
            jax.ShapeDtypeStruct((rows + HALO, KV), BF16),
            jax.ShapeDtypeStruct((TILE, KV), F32),
            jax.ShapeDtypeStruct((8, KV), F32),
            jax.ShapeDtypeStruct((8, part), F32),
        ),
        grid=(1,),
        in_specs=[pl.BlockSpec(memory_space=pltpu.SMEM)]
        + [whole()] * 7
        + [
            pl.BlockSpec((TILE, KV), lambda i: (0, 0)),
            pl.BlockSpec((KV, TILE), lambda i: (0, 0)),
            whole(),
            whole(),
            whole(),
        ],
        out_specs=tuple([whole()] * 6),
        scratch_shapes=[
            pltpu.VMEM((8 + before + TILE + 8, KV), F32),
            pltpu.VMEM((8 + HALO + 8, part), F32),
            pltpu.VMEM((16, KV), F32),
            pltpu.VMEM((16, part), F32),
            *back_scratch(rows),
        ],
        compiler_params=params(34),
        cost_estimate=COST,
        name="earlier_back",
    )(meta, q, d_out_t, out_t, lse, first_row, kv, kvt, kv_own, kvt_own, raw, raw_halo, taps)


def own_back_kernel(
    meta_ref, q_ref, dt_ref, ot_ref, lse_ref, first_ref, dq_in_ref, kv_ref, kvt_ref, raw_ref, taps_ref, next_ref,
    normed_e_ref, two_ref, one_ref, normed_ref, out_keep_ref, out_near_ref, out_far_ref,
    d_raw_ref, sums_ref, mix_ref, dq_ref, grad_ref, fix_ref, *scratch,
):
    rows = kv_ref.shape[0]
    base = REACH * rows
    grad_ref[...] = jnp.zeros_like(grad_ref)
    grad_ref[8 : 8 + TILE, :KV] = next_ref[...]
    dq_ref[...] = dq_in_ref[...]
    back_prepare(meta_ref, q_ref, dt_ref, ot_ref, scratch)
    row = TILE
    while row < rows:
        keys = TILE if row % STEP else STEP
        back_step(
            row, keys, base + row, row, True, row, kv_ref, kvt_ref, lse_ref, first_ref, grad_ref, 8, dq_ref, scratch
        )
        row += keys
    for lanes in query_tiles(rows):
        grad_ref[8 + lanes.start : 8 + lanes.stop, KV:] = dq_ref[:, lanes].T * (DH**-0.5)
    starts = [meta_ref[STARTS + n] - base for n in range(8)]
    unmix_rows(grad_ref, raw_ref, fix_ref, taps_ref[...], starts, rows, sums_ref)
    d_raw_ref[...] = grad_ref[8 : 8 + rows, :].astype(BF16)
    part = out_keep_ref.shape[0]
    out_grad = out_keep_ref[...].astype(F32) + out_near_ref[0].astype(F32) + out_far_ref[...].astype(F32)
    for n in range(normed_ref.shape[1] // TILE):
        lanes = slice(n * TILE, (n + 1) * TILE)
        grad = mm(normed_ref[:, lanes], d_raw_ref[...], 0, 0)
        earlier = mm(normed_e_ref[:rows, lanes], two_ref[...], 0, 0)
        earlier = earlier + mm(normed_e_ref[rows:, lanes], one_ref[:rows, :], 0, 0)
        halo = mm(normed_e_ref[2 * rows - HALO :, lanes], one_ref[rows:, :], 0, 0)[:, :part]
        mix_ref[lanes, :KV] = (grad[:, :KV] + earlier).astype(BF16)
        rest = jnp.concatenate([grad[:, KV:] + halo, out_grad[:, lanes].T], axis=1)
        mix_ref[lanes, KV:] = rest.astype(BF16)


def own_back(
    meta, q, d_out_t, out_t, lse, first_row, dq_t, kv, kvt, raw, taps, grad_next, normed_e, two, one, normed, *grad_out
):
    rows, part = q.shape
    width = raw.shape[1]
    return pl.pallas_call(
        own_back_kernel,
        out_shape=(
            jax.ShapeDtypeStruct((rows, width), BF16),
            jax.ShapeDtypeStruct((8, width), F32),
            jax.ShapeDtypeStruct((normed.shape[1], width + part), BF16),
        ),
        in_specs=[pl.BlockSpec(memory_space=pltpu.SMEM)] + [whole()] * 18,
        out_specs=(whole(), whole(), whole()),
        scratch_shapes=[
            pltpu.VMEM((part, rows), F32),
            pltpu.VMEM((8 + rows + 8, width), F32),
            pltpu.VMEM((16, width), F32),
            *back_scratch(rows),
        ],
        compiler_params=params(34),
        cost_estimate=COST,
        name="own_back",
    )(
        meta, q, d_out_t, out_t, lse, first_row, dq_t, kv, kvt, raw, taps, grad_next,
        normed_e, two, one, normed, *grad_out,
    )


def after_attend_kernel(a0, a1, a2, a3, w0, w1, w2, w3, x_ref, gain_ref, hidden_ref, normed_ref):
    branch = mm(a0[...], w0[...], 0, 0)
    for a, w in ((a1, w1), (a2, w2), (a3, w3)):
        branch = branch + mm(a[...], w[...], 0, 0)
    hidden = x_ref[...].astype(F32) + branch
    hidden_ref[...] = hidden
    factor = lax.rsqrt(jnp.mean(hidden * hidden, axis=-1, keepdims=True) + EPS)
    normed_ref[...] = (hidden * factor * gain_ref[...]).astype(BF16)


def after_attend(attended, w_out, x, gain):
    rows, dim = x.shape
    return pl.pallas_call(
        after_attend_kernel,
        out_shape=(jax.ShapeDtypeStruct((rows, dim), F32), jax.ShapeDtypeStruct((rows, dim), BF16)),
        in_specs=[whole()] * 10,
        out_specs=(whole(), whole()),
        compiler_params=params(),
        cost_estimate=COST,
        name="after_attend",
    )(*attended, *w_out, x, gain)


def feed_kernel(meta_ref, x0, x2, x1, x3, cot_ref, *refs, masks, shard):
    count = (len(refs) - 7) // 2
    packed_refs, down_refs = refs[:count], refs[count : 2 * count]
    x_ref, act_ref, d_up_ref, keep_ref, send_ref, down_ref, up_ref = refs[2 * count :]

    def half(first, second, back_ref):
        x = jnp.concatenate([first[...], second[...]], axis=0)
        x_ref[...] = x
        up = mm(x, up_ref[...])
        pos = jnp.maximum(up, 0.0)
        act_ref[...] = (pos * pos).astype(BF16)
        d_act = mm(cot_ref[...], down_ref[...])
        d_up = (d_act * 2.0 * pos).astype(BF16)
        d_up_ref[...] = d_up
        back_ref[...] = mm(d_up, up_ref[...], 1, 1).astype(BF16)

    @pl.when(pl.program_id(0) == 0)
    def _():
        put_rows(up_ref, packed_refs, meta_ref[BLK], masks, shard)
        put_rows(down_ref, down_refs, meta_ref[BLK], masks, shard)
        half(x0, x2, keep_ref)

    @pl.when(pl.program_id(0) == 1)
    def _():
        half(x1, x3, send_ref)


def feed(meta, x, cot, packed, down, masks):
    rows, dim = cot.shape
    shard, units = down[0].shape[1:]
    step = rows // 2
    tile = lambda n: pl.BlockSpec((step, n), lambda i, *_: (i, 0))
    return pl.pallas_call(
        functools.partial(feed_kernel, masks=masks, shard=shard),
        out_shape=(
            jax.ShapeDtypeStruct((rows, dim), BF16),
            jax.ShapeDtypeStruct((rows, units), BF16),
            jax.ShapeDtypeStruct((rows, units), BF16),
            jax.ShapeDtypeStruct((step, dim), BF16),
            jax.ShapeDtypeStruct((step, dim), BF16),
            jax.ShapeDtypeStruct((dim, units), BF16),
        ),
        grid_spec=pltpu.PrefetchScalarGridSpec(
            num_scalar_prefetch=1,
            grid=(2,),
            in_specs=[whole()] * 4 + [tile(dim)] + [whole()] * (len(packed) + len(down)),
            out_specs=(tile(dim), tile(units), tile(units), whole(), whole(), whole()),
            scratch_shapes=[pltpu.VMEM((dim, units), BF16)],
        ),
        compiler_params=params(),
        cost_estimate=COST,
        name="feed",
    )(meta, *x, cot, *packed, *down)


def feed_rest_kernel(x_ref, d_up_ref, cot_ref, act_ref, down_ref, grads_ref, keep_ref, send_ref):
    grads_ref[0] = mm(x_ref[...], d_up_ref[...], 0, 0).astype(BF16)
    grads_ref[1] = mm(cot_ref[...], act_ref[...], 0, 0).astype(BF16)
    out = mm(act_ref[...], down_ref[...], 1, 1).astype(BF16)
    half = out.shape[0] // 2
    keep_ref[...] = out[:half]
    send_ref[...] = out[half:]


def feed_rest(x, d_up, cot, act, w_down_t):
    rows, dim = x.shape
    units = act.shape[1]
    block = pl.BlockSpec((rows, TILE), lambda i: (0, i))
    half = pl.BlockSpec((rows // 2, TILE), lambda i: (0, i))
    return pl.pallas_call(
        feed_rest_kernel,
        out_shape=(
            jax.ShapeDtypeStruct((2, dim, units), BF16),
            jax.ShapeDtypeStruct((rows // 2, dim), BF16),
            jax.ShapeDtypeStruct((rows // 2, dim), BF16),
        ),
        grid=(dim // TILE,),
        in_specs=[block, whole(), block, whole(), pl.BlockSpec((TILE, units), lambda i: (i, 0))],
        out_specs=(pl.BlockSpec((2, TILE, units), lambda i: (0, i, 0)), half, half),
        compiler_params=params(),
        cost_estimate=COST,
        name="feed_rest",
    )(x, d_up, cot, act, w_down_t)


def before_back_kernel(
    s_ref, r_ref, hidden_ref, gain_ref, cot_ref, w0, w1, w2, w3, a0, a1, a2, a3,
    d_hidden_ref, d0, d1, d2, d3, keep_ref, keep_far_ref, send_ref, sum_ref,
):
    d_normed = s_ref[...].astype(F32) + r_ref[...].astype(F32)
    hidden = hidden_ref[...]
    factor = lax.rsqrt(jnp.mean(hidden * hidden, axis=-1, keepdims=True) + EPS)
    unit = hidden * factor
    sum_ref[...] = jnp.sum(d_normed * unit, axis=0, keepdims=True)
    scaled = d_normed * gain_ref[...]
    inner = jnp.mean(scaled * unit, axis=-1, keepdims=True)
    d_hidden = cot_ref[...].astype(F32) + factor * (scaled - unit * inner)
    d_hidden_ref[...] = d_hidden
    d_branch = d_hidden.astype(BF16)
    for w, d in ((w0, d0), (w1, d1), (w2, d2), (w3, d3)):
        d[...] = mm(w[...], d_branch, 1, 1).astype(BF16)
    for a, to in ((a0, keep_ref), (a1, keep_far_ref), (a2, send_ref.at[0]), (a3, send_ref.at[1])):
        to[...] = mm(a[...], d_branch).astype(BF16)


def before_back(chip_sum, far_sum, hidden, gain, cot, w_out, attended):
    rows, dim = hidden.shape
    part = w_out[0].shape[0]
    return pl.pallas_call(
        before_back_kernel,
        out_shape=(
            jax.ShapeDtypeStruct((rows, dim), F32),
            *[jax.ShapeDtypeStruct((part, rows), BF16)] * 4,
            *[jax.ShapeDtypeStruct((part, dim), BF16)] * 2,
            jax.ShapeDtypeStruct((2, part, dim), BF16),
            jax.ShapeDtypeStruct((1, dim), F32),
        ),
        in_specs=[whole()] * 13,
        out_specs=tuple([whole()] * 9),
        compiler_params=params(),
        cost_estimate=COST,
        name="before_back",
    )(chip_sum, far_sum, hidden, gain, cot, *w_out, *attended)


def d_normed_kernel(meta_ref, own_ref, one_ref, halo_ref, two_ref, x_ref, w_ref, keep_ref, send_ref, sum_ref):
    i = pl.program_id(0)
    step = own_ref.shape[0]
    later = jnp.where(meta_ref[NEXT_ONE] == 1, one_ref[...].astype(F32), 0.0)
    later = later + jnp.where(meta_ref[NEXT_TWO] == 1, two_ref[...].astype(F32), 0.0)
    own = own_ref[...].astype(F32)
    queries = own[:, KV:]
    part = queries.shape[1]
    last = (i == pl.num_programs(0) - 1) & (meta_ref[NEXT_ONE] == 1)
    halo = jnp.where(last, halo_ref[...].astype(F32)[:, :part], 0.0)
    queries = queries + jnp.concatenate([jnp.zeros((step - HALO, part), F32), halo], axis=0)
    d_raw = jnp.concatenate([own[:, :KV] + later, queries], axis=1).astype(BF16)
    d_normed = mm(d_raw, w_ref[...], 1, 1)
    for n in range(step // TILE):
        slot = slot_of(i * (step // TILE) + n, meta_ref)
        rows = d_normed[n * TILE : (n + 1) * TILE].astype(BF16)
        to = pl.ds(pl.multiple_of((slot & 1) * TILE, TILE), TILE)

        @pl.when(slot < 2)
        def _(rows=rows, to=to):
            keep_ref[to, :] = rows

        @pl.when(slot >= 2)
        def _(rows=rows, to=to):
            send_ref[to, :] = rows

    x = x_ref[...].astype(F32)
    unit = x * lax.rsqrt(jnp.mean(x * x, axis=-1, keepdims=True) + EPS)

    @pl.when(i == 0)
    def _():
        sum_ref[...] = jnp.zeros_like(sum_ref)

    sum_ref[...] += jnp.sum(d_normed * unit, axis=0, keepdims=True)


def d_normed_parts(meta, own, one, two, x, w):
    rows, dim = x.shape
    width = w.shape[1]
    step = 2 * TILE
    tile = lambda n: pl.BlockSpec((step, n), lambda i, *_: (i, 0))
    return pl.pallas_call(
        d_normed_kernel,
        out_shape=(
            jax.ShapeDtypeStruct((rows // 2, dim), BF16),
            jax.ShapeDtypeStruct((rows // 2, dim), BF16),
            jax.ShapeDtypeStruct((1, dim), F32),
        ),
        grid_spec=pltpu.PrefetchScalarGridSpec(
            num_scalar_prefetch=1,
            grid=(rows // step,),
            in_specs=[
                tile(width),
                tile(KV),
                pl.BlockSpec((HALO, KV), lambda i, *_: (rows // HALO, 0)),
                tile(KV),
                tile(dim),
                whole(),
            ],
            out_specs=(whole(), whole(), pl.BlockSpec((1, dim), lambda i, *_: (0, 0))),
        ),
        compiler_params=params(),
        cost_estimate=COST,
        name="d_normed_parts",
    )(meta, own, one, one, two, x, w)


def grad_tokens_kernel(s_ref, r_ref, x_ref, gain_ref, d_hidden_ref, out_ref):
    d_normed = s_ref[...].astype(F32) + r_ref[...].astype(F32)
    x = x_ref[...].astype(F32)
    factor = lax.rsqrt(jnp.mean(x * x, axis=-1, keepdims=True) + EPS)
    unit = x * factor
    scaled = d_normed * gain_ref[...]
    inner = jnp.mean(scaled * unit, axis=-1, keepdims=True)
    out_ref[...] = (d_hidden_ref[...] + factor * (scaled - unit * inner)).astype(BF16)


def grad_tokens_own(chip_sum, far_sum, x, gain, d_hidden):
    return pl.pallas_call(
        grad_tokens_kernel,
        out_shape=jax.ShapeDtypeStruct(x.shape, BF16),
        in_specs=[whole()] * 5,
        out_specs=whole(),
        compiler_params=params(),
        name="grad_tokens_own",
    )(chip_sum, far_sum, x, gain, d_hidden)


def assemble_kernel(meta_ref, *refs):
    *pieces, out_ref = refs
    for piece, d in zip(pieces, (0, 2, 1, 3)):

        @pl.when(pl.program_id(0) == (meta_ref[0] ^ d))
        def _(piece=piece):
            out_ref[...] = piece[...].astype(out_ref.dtype)


def by_place(meta, pieces, dtype):
    rows, dim = pieces[0].shape
    return pl.pallas_call(
        assemble_kernel,
        out_shape=jax.ShapeDtypeStruct((4 * rows, dim), dtype),
        grid_spec=pltpu.PrefetchScalarGridSpec(
            num_scalar_prefetch=1,
            grid=(4,),
            in_specs=[whole()] * 4,
            out_specs=pl.BlockSpec((rows, dim), lambda i, *_: (i, 0)),
        ),
        compiler_params=params(),
        cost_estimate=COST,
        name="assemble",
    )(meta, *pieces)


def sum_halves(keep, send):
    return (keep.astype(F32) + swap(send, "head", 1).astype(F32)).astype(BF16)


def body(
    tokens,
    seg_ids,
    gain_attn,
    w_query,
    w_key,
    w_value,
    conv_kernels,
    w_out,
    gain_ffn,
    w_up,
    w_down,
    cotangent,
):
    rows, dim = tokens.shape
    part = conv_kernels.shape[2]
    quarter = rows // lax.axis_size("head")
    blk = lax.axis_index("blk")
    head = lax.axis_index("head")
    groups = bit_groups("blk")
    halves = [(bit,) for group in groups[:-1] for bit in group]
    together = lax.optimization_barrier
    own_quarter = lax.dynamic_slice_in_dim(tokens, head * quarter, quarter)
    sent = jnp.concatenate([own_quarter, tokens[rows - HALO :]])
    two = moved(sent, "blk", 2)
    shard, units = w_up.shape
    masks = gathered_masks("blk")
    w_mix = jnp.concatenate([w_query, w_key, w_value], axis=1)
    w_some = sent_round(w_mix, "blk")
    one = swap(jnp.where(bit_of("blk", 0), two, sent), "blk", 1)
    pieces = [*quarters(two), *quarters(one)]
    packed, down_some = pack(w_up, w_out, w_down)
    w_some, packed = together((joined(w_some), packed))
    w_mix = pieces_of(w_some, "blk", shard)
    packed_some = sent_round(packed, "blk")
    span = (REACH + 1) * rows
    padded_ids = jnp.pad(seg_ids, (REACH * rows, 0), constant_values=-1)
    window = lax.dynamic_slice_in_dim(padded_ids, blk * rows, span)
    starts = jnp.sum((window[None, :] <= window[0] + jnp.arange(8)[:, None]).astype(jnp.int32), axis=1)
    place = jnp.arange(REACH * rows, span, dtype=jnp.int32)
    first_row = jnp.max(jnp.where(starts[:, None] <= place, starts[:, None], 0), axis=0)
    low = first_row[::TILE] // TILE
    full = (first_row[TILE - 1 :: TILE] + TILE - 1) // TILE
    last = lax.axis_size("blk") - 1
    exists = jnp.stack([blk >= 1, blk >= 2, blk + 1 <= last, blk + 2 <= last])
    meta = jnp.concatenate([head[None], low, full, starts, exists, blk[None]]).astype(jnp.int32)
    first_row = first_row[None]
    taps = arranged(*conv_kernels)
    gain_one, gain_two = gain_attn[None], gain_ffn[None]

    hi, lo = bit_of("head", 1), bit_of("head", 0)
    cot = cotangent.reshape(2, 2, quarter, dim)
    cot = jnp.where(hi, cot[::-1], cot)
    cot = jnp.where(lo, cot[:, ::-1], cot)
    cot = jnp.swapaxes(cot, 0, 1).reshape(rows, dim)
    *w_mix, cot, pieces[4] = together((*w_mix, cot, pieces[4]))
    w_mix, raw_halo, raw, normed, q, kv, kvt = project_own(meta, tokens, pieces[4], gain_one, taps, w_mix, masks)
    q, pieces[5] = together((q, pieces[5]))
    acc_own, stat_own = attend_own(q, kv, kvt, first_row)
    acc_own, down_some, *packed_some = together((acc_own, down_some, *packed_some))
    packed = pieces_of(joined(packed_some), "blk", shard)
    down_some = sent_round(down_some, "blk")
    raw_e, normed_e, kv_e, kvt_e = project_earlier(meta, pieces, gain_one, w_mix, taps)
    raw_e, *more = together((raw_e, *packed, *down_some))
    packed, down_some = more[: len(packed)], more[len(packed) :]
    down = pieces_of(joined(down_some), "blk", shard)
    out_full = unpack_out(meta, packed, masks, shard, part)
    out_far = swap(out_full, "head", 2)
    out_pieces = [out_full, out_far, swap(out_full, "head", 1), swap(out_far, "head", 1)]
    kv_late, out_full = together((kv_e, out_full))
    att, out_t, lse = attend_earlier(meta, q, kv_late, kvt_e, first_row, acc_own, stat_own)

    near = swap(att[2:], "head", 1)
    across = swap(jnp.stack([att[1], near[1]]), "head", 2)
    attended = (att[0], across[0], near[0], across[1])
    quarter_late, *down = together((own_quarter, *down))
    hidden, normed_two = after_attend(attended, out_pieces, quarter_late, gain_two)
    ffn_in, act, d_up, *back, down_t = feed(meta, quarters(normed_two), cot, packed, down, masks)
    chip_back = sum_halves(*back)
    far_back = swap(chip_back[quarter:], "head", 2)
    feed_grads, *ffn = feed_rest(ffn_in, d_up, cot, act, down_t)
    near_parts = chosen(feed_grads.reshape(2, -1, shard, units), "blk", groups[-1])
    far_back, *near_parts = together((far_back, *near_parts))
    near_parts = received(near_parts, "blk", groups[-1])
    d_hidden, *d_outs, keep_out, keep_far, send_out, gain_two_part = before_back(
        chip_back[:quarter], far_back, hidden, gain_two, cot[:quarter], out_pieces, attended
    )
    across = swap(jnp.stack([d_outs[1], d_outs[3]]), "head", 2)
    near = swap(jnp.stack([d_outs[2], across[1]]), "head", 1)
    d_out_t = jnp.stack([d_outs[0], across[0], near[0], near[1]])
    chip_ffn = sum_halves(*ffn)
    near_out = swap(send_out, "head", 1)
    far_out = swap(total_of([keep_far, near_out[1]]).astype(BF16), "head", 2)
    d_out_t, chip_ffn = together((d_out_t, chip_ffn))
    far_ffn = swap(chip_ffn[quarter:], "head", 2)

    dq_t, d_two, d_one, grad_next, sums_before, sums_halo = earlier_back(
        meta, q, d_out_t, out_t, lse, first_row, kv_e, kvt_e, kv, kvt, raw_e, raw_halo, taps
    )
    from_two = moved(d_two, "blk", -2)
    from_one = moved(d_one, "blk", -1)
    output = (hidden + total_of([chip_ffn[:quarter], far_ffn])).astype(BF16)
    dq_t, output, far_out = together((dq_t, output, far_out))
    output_far = swap(output, "head", 2)
    d_raw, sums_own, grad_mix = own_back(
        meta, q, d_out_t, out_t, lse, first_row, dq_t, kv, kvt, raw, taps, grad_next,
        normed_e, d_two, d_one, normed, keep_out, near_out, far_out,
    )
    mix_parts = chosen(grad_mix.reshape(1, -1, shard, 4 * part), "blk", groups[-1])
    mix_parts = received(mix_parts, "blk", groups[-1])
    output_far, output, d_raw = together((output_far, output, d_raw))
    output = [output, output_far, swap(output, "head", 1), swap(output_far, "head", 1)]
    d_raw, *more = together((d_raw, *output, *near_parts, *mix_parts))
    output, near_parts, mix_parts = more[:4], more[4:6], more[6:]
    *back, gain_one_part = d_normed_parts(meta, d_raw, from_one, from_two, tokens, w_mix)
    near_parts = total_of(near_parts).astype(BF16)
    chip_back = sum_halves(*back)
    gains = jnp.concatenate([gain_two_part, gain_one_part])
    gains = gains + swap(gains, "head", 1)
    chip_back, gains, near_parts, *mix_parts = together((chip_back, gains, near_parts, *mix_parts))
    far_back = swap(chip_back[quarter:], "head", 2)
    up_parts = sum_scatter(near_parts[:1], "blk", halves)
    down_parts = sum_scatter(near_parts[1:], "blk", halves)
    mix_parts = sum_scatter(total_of(mix_parts).astype(BF16), "blk", halves)
    far_back, far_gains = together((far_back, swap(gains, "head", 2)))
    grad_tokens = grad_tokens_own(chip_back[:quarter], far_back, own_quarter, gain_one, d_hidden)
    grad_tokens, far_gains = together((grad_tokens, far_gains))
    gains = gains + far_gains
    grad_far = swap(grad_tokens, "head", 2)
    grad_far, output[0], *more = together((grad_far, output[0], *up_parts, *down_parts, *mix_parts))
    up_parts, down_parts, mix_parts = more[:2], more[2:4], more[4:]
    grad_tokens = [grad_tokens, grad_far, swap(grad_tokens, "head", 1), swap(grad_far, "head", 1)]
    grad_tokens = by_place(meta, grad_tokens, F32)

    output = by_place(meta, output, BF16)
    grad_up_shard = total_of(up_parts).reshape(shard, units)
    grad_down_shard = total_of(down_parts).reshape(shard, units).T
    mix_shard = total_of(mix_parts).reshape(shard, 4 * part)
    grad_query_shard, grad_key_shard, grad_value_shard = separated(mix_shard[:, : 3 * part])
    grad_out_shard = mix_shard[:, 3 * part :].T

    taps_part = jnp.concatenate([sums_own[:3, :KV] + sums_before[:3], sums_own[:3, KV:] + sums_halo[:3]], axis=1)
    taps_part = jnp.stack(separated(taps_part)).reshape(-1)
    small = jnp.concatenate([gains.reshape(-1), taps_part])
    small = sum_everywhere(small, "blk", groups)
    grad_gain_ffn, grad_gain_attn = small[:dim], small[dim : 2 * dim]
    grad_kernels = small[2 * dim :].reshape(3, 3, part)
    return (
        output,
        grad_tokens,
        grad_gain_attn,
        grad_query_shard,
        grad_key_shard,
        grad_value_shard,
        grad_kernels,
        grad_out_shard,
        grad_gain_ffn,
        grad_up_shard,
        grad_down_shard,
    )


def solution(mesh):
    return jax.shard_map(
        body,
        mesh=mesh,
        in_specs=(
            P("blk", None),
            P(),
            P(),
            P("blk", "head"),
            P("blk", "head"),
            P("blk", "head"),
            P(None, None, "head"),
            P("head", "blk"),
            P(),
            P("blk", "head"),
            P("head", "blk"),
            P("blk", None),
        ),
        out_specs=(
            P("blk", None),
            P("blk", None),
            P(),
            P("blk", "head"),
            P("blk", "head"),
            P("blk", "head"),
            P(None, None, "head"),
            P("head", "blk"),
            P(),
            P("blk", "head"),
            P("head", "blk"),
        ),
        check_vma=False,
    )
```
